256 devices in a mesh: gx: 32 (over y, z), gy: 8 (over x, core).
Axes of the slice: x: 4, y: 4, z: 8, core: 2. Of those that a mesh axis runs over, the one named last changes fastest.
Arguments:
- right_side: float32 [512, 256, 256], P('gx', 'gy'), may hold values from -8 to 8
- coefficient: float32 [64, 32, 32], P('gx', 'gy'), may hold values from 0.2 to 5
Outputs:
- solution_field: float32 [512, 256, 256], P('gx', 'gy')
- residual: float32 [512, 256, 256], P('gx', 'gy')
The draws below stay inside these ranges and needn't reach their ends.
All inputs are finite; a program needn't handle non-finite values.
Results may differ from the reference program's by a relative error of at most 0.0003.
Values sent between devices are 32-bit elements; how exact they have to be, the bound alone decides.
A program may use at most 128 MiB of HBM per device.

```python
import math
import jax
import jax.numpy as jnp
import numpy as np
from jax import lax

EZ = 32
ORDER = 7
COARSE_ORDER = 3
CHEB = 2
ITERS = 2
EXG = 64
EYG = 32
NX = 512
NY = 256
NZ = 256


def shard_levels(rng, shape, pieces, smallest, high):
    gain, own = 1.0, jax.random.fold_in(rng, 6)
    for dim, parts in pieces:
        draws = jnp.exp(jax.random.uniform(jax.random.fold_in(own, dim), (parts,), jnp.float32, smallest / len(pieces), high / len(pieces)))
        gain = gain * jnp.repeat(draws, shape[dim] // parts).reshape([-1 if axis == dim else 1 for axis in range(len(shape))])
    return gain


def normal_values(stream_key, dims, width, bound, split=(), held_as=jnp.bfloat16):
    loudness = shard_levels(stream_key, dims, split, -0.22, 0.18) if split else 1.0
    values = jax.random.normal(stream_key, dims, jnp.float32) * width * loudness
    return jnp.minimum(jnp.maximum(values, -bound), bound).astype(held_as)


def setup_inputs(seed: int = 0) -> dict:
    splits = jax.random.split(jax.random.key(seed), 3)
    right_side = normal_values(splits[0], (NX, NY, NZ), 1.0, 8.0, ((0, 32), (1, 8)), jnp.float32)
    coefficient = jnp.clip(jnp.exp(math.log(5.0) - 3.218876 * jax.random.uniform(splits[1], (EXG, EYG, EZ), jnp.float32) ** shard_levels(splits[1], (EXG, EYG, EZ), ((0, 32), (1, 8)), -0.2, 0.2)), 0.2, 5.0)
    return dict(right_side=right_side, coefficient=coefficient)


def legendre_pair(degree, points):
    before = points * 0.0 + 1.0
    now = points.copy()
    for power in range(2, degree + 1):
        after = ((2 * power - 1) * points * now - (power - 1) * before) / power
        before = now
        now = after
    return now, before


def gll_tables(degree):
    number = degree + 1
    points = np.cos(math.pi * np.arange(number) / degree)
    for newton in range(60):
        top, below = legendre_pair(degree, points)
        points = points - (points * top - below) / (number * top)
    points = points[::-1].copy()
    points[0] = -1.0
    points[degree] = 1.0
    values = legendre_pair(degree, points)[0]
    weights = 2.0 / (degree * (degree + 1) * values ** 2)
    derivative = np.zeros((number, number))
    for row_index in range(number):
        for column_index in range(number):
            if row_index != column_index:
                derivative[row_index, column_index] = values[row_index] / (values[column_index] * (points[row_index] - points[column_index]))
    derivative[0, 0] = -degree * (degree + 1) / 4.0
    derivative[degree, degree] = degree * (degree + 1) / 4.0
    stiffness = derivative.T @ (weights[:, None] * derivative)
    return points, weights, stiffness


def main_diagonal(matrix):
    return np.array([matrix[index, index] for index in range(matrix.shape[0])])


def upper_bound(degree):
    points, weights, stiffness = gll_tables(degree)
    rowsum = np.abs(stiffness).sum(1)
    diagonal = main_diagonal(stiffness)
    top = rowsum[:, None, None] * weights[None, :, None] * weights[None, None, :]
    top = top + weights[:, None, None] * rowsum[None, :, None] * weights[None, None, :]
    top = top + weights[:, None, None] * weights[None, :, None] * rowsum[None, None, :]
    bottom = diagonal[:, None, None] * weights[None, :, None] * weights[None, None, :]
    bottom = bottom + weights[:, None, None] * diagonal[None, :, None] * weights[None, None, :]
    bottom = bottom + weights[:, None, None] * weights[None, :, None] * diagonal[None, None, :]
    return float((top / bottom).max())


def interpolation_matrix(fine_degree, coarse_degree):
    fine_points = gll_tables(fine_degree)[0]
    coarse_points = gll_tables(coarse_degree)[0]
    matrix = np.ones((fine_degree + 1, coarse_degree + 1))
    for column_index in range(coarse_degree + 1):
        for other_index in range(coarse_degree + 1):
            if other_index != column_index:
                matrix[:, column_index] *= (fine_points - coarse_points[other_index]) / (coarse_points[column_index] - coarse_points[other_index])
    return matrix


def along_first(field, matrix):
    rows_out, rows_in = matrix.shape
    elements = field.shape[0] // rows_in
    shaped = field.reshape(elements, rows_in, field.shape[1], field.shape[2])
    result = jnp.einsum('ai,xiyz->xayz', matrix, shaped, precision=lax.Precision.HIGHEST)
    return result.reshape(elements * rows_out, field.shape[1], field.shape[2])


def along_second(field, matrix):
    rows_out, rows_in = matrix.shape
    elements = field.shape[1] // rows_in
    shaped = field.reshape(field.shape[0], elements, rows_in, field.shape[2])
    result = jnp.einsum('ai,xeiz->xeaz', matrix, shaped, precision=lax.Precision.HIGHEST)
    return result.reshape(field.shape[0], elements * rows_out, field.shape[2])


def along_third(field, matrix):
    rows_out, rows_in = matrix.shape
    elements = field.shape[2] // rows_in
    group = math.gcd(elements, max(1, 128 // rows_out))
    block = jnp.kron(jnp.eye(group, dtype=jnp.float32), matrix)
    shaped = field.reshape(field.shape[0], field.shape[1], elements // group, group * rows_in)
    result = jnp.einsum('xyqi,ai->xyqa', shaped, block, precision=lax.Precision.HIGHEST)
    return result.reshape(field.shape[0], field.shape[1], elements * rows_out)


def apply_dims(field, matrix):
    return along_third(along_second(along_first(field, matrix), matrix), matrix)


def sum_first(padded, number):
    rows = padded.shape[0] - 2
    position = jnp.arange(rows) % number
    upper = (position == number - 1).astype(jnp.float32)[:, None, None]
    lower = (position == 0).astype(jnp.float32)[:, None, None]
    return padded[1:-1] + upper * padded[2:] + lower * padded[:-2]


def sum_second(padded, number):
    columns = padded.shape[1] - 2
    position = jnp.arange(columns) % number
    upper = (position == number - 1).astype(jnp.float32)[None, :, None]
    lower = (position == 0).astype(jnp.float32)[None, :, None]
    return padded[:, 1:-1] + upper * padded[:, 2:] + lower * padded[:, :-2]


def sum_third(field, number):
    padded = jnp.pad(field, ((0, 0), (0, 0), (1, 1)))
    depth = field.shape[2]
    position = jnp.arange(depth) % number
    upper = (position == number - 1).astype(jnp.float32)[None, None, :]
    lower = (position == 0).astype(jnp.float32)[None, None, :]
    return padded[:, :, 1:-1] + upper * padded[:, :, 2:] + lower * padded[:, :, :-2]


def node_masks(count, offset, total, number):
    index = offset + jnp.arange(count, dtype=jnp.int32)
    inside = ((index != 0) & (index != total - 1)).astype(jnp.float32)
    upper = ((index % number == number - 1) & (index != total - 1)).astype(jnp.float32)
    lower = ((index % number == 0) & (index != 0)).astype(jnp.float32)
    return inside, 1.0 + upper + lower


def build_level(degree, coefficient, offsets, totals, summation):
    points, weights_np, stiffness_np = gll_tables(degree)
    number = degree + 1
    weights = jnp.asarray(weights_np, dtype=jnp.float32)
    stiffness = jnp.asarray(stiffness_np, dtype=jnp.float32)
    diagonal = jnp.asarray(main_diagonal(stiffness_np), dtype=jnp.float32)
    counts = [coefficient.shape[0] * number, coefficient.shape[1] * number, coefficient.shape[2] * number]
    tiled = [jnp.tile(weights, coefficient.shape[dim_index]) for dim_index in range(3)]
    tiled_diag = [jnp.tile(diagonal, coefficient.shape[dim_index]) for dim_index in range(3)]
    coeff_nodes = jnp.repeat(jnp.repeat(jnp.repeat(coefficient, number, 0), number, 1), number, 2)
    first = node_masks(counts[0], offsets[0], totals[0], number)
    second = node_masks(counts[1], offsets[1], totals[1], number)
    third = node_masks(counts[2], offsets[2], totals[2], number)
    mask = first[0][:, None, None] * second[0][None, :, None] * third[0][None, None, :]
    weight_inv = 1.0 / (first[1][:, None, None] * second[1][None, :, None] * third[1][None, None, :])
    wx = tiled[0][:, None, None]
    wy = tiled[1][None, :, None]
    wz = tiled[2][None, None, :]
    local_diag = coeff_nodes * (tiled_diag[0][:, None, None] * wy * wz + wx * tiled_diag[1][None, :, None] * wz + wx * wy * tiled_diag[2][None, None, :])
    dinv = mask / summation(local_diag)
    return {"stiffness": stiffness, "wx": wx, "wy": wy, "wz": wz, "coeff_nodes": coeff_nodes, "mask": mask, "weight_inv": weight_inv, "dinv": dinv, "upper": upper_bound(degree), "summation": summation}


def local_stiffness(level, field):
    stiffness = level["stiffness"]
    first = along_first(field, stiffness) * (level["wy"] * level["wz"])
    second = along_second(field, stiffness) * (level["wx"] * level["wz"])
    third = along_third(field, stiffness) * (level["wx"] * level["wy"])
    return level["coeff_nodes"] * (first + second + third)


def apply_operator(level, field):
    return level["mask"] * level["summation"](local_stiffness(level, field))


def chebyshev(level, rhs_field, start):
    upper = level["upper"]
    lower = 0.1 * upper
    center = 0.5 * (upper + lower)
    halfwidth = 0.5 * (upper - lower)
    if start is None:
        remain = rhs_field
        change = level["dinv"] * remain / center
        result = change
    else:
        remain = rhs_field - apply_operator(level, start)
        change = level["dinv"] * remain / center
        result = start + change
    previous = halfwidth / center
    for sweep in range(CHEB - 1):
        remain = remain - apply_operator(level, change)
        current = 1.0 / (2.0 * center / halfwidth - previous)
        change = current * previous * change + (2.0 * current / halfwidth) * level["dinv"] * remain
        result = result + change
        previous = current
    return result


def vcycle(fine, coarse, prolong, restrict, rhs_field):
    smoothed = chebyshev(fine, rhs_field, None)
    defect = rhs_field - apply_operator(fine, smoothed)
    coarse_rhs = coarse["mask"] * coarse["summation"](apply_dims(fine["weight_inv"] * defect, restrict))
    coarse_fix = chebyshev(coarse, coarse_rhs, None)
    smoothed = smoothed + apply_dims(coarse_fix, prolong)
    return chebyshev(fine, rhs_field, smoothed)


def make_summation(number):
    def summation(field):
        padded = jnp.pad(field, ((1, 1), (1, 1), (0, 0)))
        return sum_third(sum_second(sum_first(padded, number), number), number)
    return summation


def reference(right_side, coefficient):
    fine_number = ORDER + 1
    coarse_number = COARSE_ORDER + 1
    fine_totals = (coefficient.shape[0] * fine_number, coefficient.shape[1] * fine_number, coefficient.shape[2] * fine_number)
    coarse_totals = (coefficient.shape[0] * coarse_number, coefficient.shape[1] * coarse_number, coefficient.shape[2] * coarse_number)
    fine = build_level(ORDER, coefficient, (0, 0, 0), fine_totals, make_summation(fine_number))
    coarse = build_level(COARSE_ORDER, coefficient, (0, 0, 0), coarse_totals, make_summation(coarse_number))
    prolong_np = interpolation_matrix(ORDER, COARSE_ORDER)
    prolong = jnp.asarray(prolong_np, dtype=jnp.float32)
    restrict = jnp.asarray(prolong_np.T, dtype=jnp.float32)
    solution_field = jnp.zeros_like(right_side)
    residual = fine["mask"] * fine["summation"](right_side)
    direction = residual
    rz_old = jnp.float32(1.0)
    for step_index in range(ITERS):
        precond = vcycle(fine, coarse, prolong, restrict, residual)
        rz_now = jnp.sum(residual * precond * fine["weight_inv"])
        if step_index == 0:
            direction = precond
        else:
            direction = precond + (rz_now / rz_old) * direction
        image = apply_operator(fine, direction)
        step_size = rz_now / jnp.sum(direction * image * fine["weight_inv"])
        solution_field = solution_field + step_size * direction
        residual = residual - step_size * image
        rz_old = rz_now
    return solution_field, residual
```

```python
import functools
import math

import jax
import jax.numpy as jnp
import numpy as np
from jax import lax
from jax.experimental import pallas as pl
from jax.experimental.pallas import tpu as pltpu
from jax.sharding import PartitionSpec as P

ORDER = 7
COARSE_ORDER = 3
F32 = jnp.float32
BF16 = jnp.bfloat16
MESH = pl.DeviceIdType.MESH

EX, EY, EZ = 2, 4, 32
N, NC = ORDER + 1, COARSE_ORDER + 1
YF, ZF = EY * N, EZ * N
YC, ZC = EY * NC, EZ * NC
ROWS = N * YF
ROWS_C = NC * YC


def legendre_pair(degree, points):
    before = points * 0.0 + 1.0
    now = points.copy()
    for power in range(2, degree + 1):
        after = ((2 * power - 1) * points * now - (power - 1) * before) / power
        before = now
        now = after
    return (now, before)


def gll_tables(degree):
    number = degree + 1
    points = np.cos(math.pi * np.arange(number) / degree)
    for newton in range(60):
        top, below = legendre_pair(degree, points)
        points = points - (points * top - below) / (number * top)
    points = points[::-1].copy()
    points[0] = -1.0
    points[degree] = 1.0
    values = legendre_pair(degree, points)[0]
    weights = 2.0 / (degree * (degree + 1) * values**2)
    derivative = np.zeros((number, number))
    for row_index in range(number):
        for column_index in range(number):
            if row_index != column_index:
                derivative[row_index, column_index] = values[row_index] / (
                    values[column_index] * (points[row_index] - points[column_index])
                )
    derivative[0, 0] = -degree * (degree + 1) / 4.0
    derivative[degree, degree] = degree * (degree + 1) / 4.0
    stiffness = derivative.T @ (weights[:, None] * derivative)
    return (points, weights, stiffness)


def upper_bound(degree):
    points, weights, stiffness = gll_tables(degree)
    rowsum = np.abs(stiffness).sum(1)
    diagonal = np.diag(stiffness)
    outer = lambda a, b, c: a[:, None, None] * b[None, :, None] * c[None, None, :]
    top = outer(rowsum, weights, weights) + outer(weights, rowsum, weights) + outer(weights, weights, rowsum)
    bottom = outer(diagonal, weights, weights) + outer(weights, diagonal, weights) + outer(weights, weights, diagonal)
    return float((top / bottom).max())


def interpolation_matrix(fine_degree, coarse_degree):
    fine_points = gll_tables(fine_degree)[0]
    coarse_points = gll_tables(coarse_degree)[0]
    matrix = np.ones((fine_degree + 1, coarse_degree + 1))
    for column_index in range(coarse_degree + 1):
        for other_index in range(coarse_degree + 1):
            if other_index != column_index:
                matrix[:, column_index] *= (fine_points - coarse_points[other_index]) / (
                    coarse_points[column_index] - coarse_points[other_index]
                )
    return matrix


def cheb_numbers(degree):
    upper = upper_bound(degree)
    lower = 0.1 * upper
    center = 0.5 * (upper + lower)
    half = 0.5 * (upper - lower)
    previous = half / center
    current = 1.0 / (2.0 * center / half - previous)
    k = 2.0 * current / half
    return (1.0 / center, (1.0 + current * previous) / center + k, k)


def sum_matrix(elements, number):
    matrix = np.eye(elements * number)
    for e in range(elements - 1):
        a, b = e * number + number - 1, (e + 1) * number
        matrix[a, b] = matrix[b, a] = 1.0
    return matrix


def blocks(count, matrix):
    return np.kron(np.eye(count), matrix)


TERMS = ((0, 0), (1, 0), (0, 1), (2, 0), (0, 2), (1, 1))
HOW = dict(a=3, b=3, s=6, c=3, d=6, e=3, f=6, g=3)


def pieces_of(matrix, count):
    rest, out = np.asarray(matrix, np.float64), []
    for _ in range(count):
        out.append(rest.astype(np.float32).astype(BF16))
        rest = rest - out[-1].astype(np.float64)
    return out


def right3(matrix, steps="asef"):
    p = pieces_of(matrix, 3)
    return np.concatenate([p[j] for _, j in TERMS[: max(HOW[t] for t in steps)]], 0)


def left3(matrix, steps="asef"):
    p = pieces_of(matrix, 3)
    return np.concatenate([p[j] for _, j in TERMS[: max(HOW[t] for t in steps)]], 1)


def level_matrices(degree):
    _, w, K = gll_tables(degree)
    n = degree + 1
    wy = np.tile(w, EY)
    M0 = np.kron(K, np.diag(wy)) + np.kron(np.diag(w), blocks(EY, K))
    N0 = np.kron(np.diag(w), np.diag(wy))
    return M0, N0, np.diag(np.tile(w, EZ)), blocks(EZ, K)


def face_rows(n):
    y = EY * n
    x = EX * n
    rows = [j for j in range(y)] + [(x - 1) * y + j for j in range(y)]
    rows += [i * y for i in range(x)] + [i * y + y - 1 for i in range(x)]
    return np.array(rows)


@functools.cache
def constants():
    J = interpolation_matrix(ORDER, COARSE_ORDER)
    out = {}
    M0, N0, Wz, Kz = level_matrices(ORDER)
    Sz, Szc = sum_matrix(EZ, N), sum_matrix(EZ, NC)
    Sxy = np.kron(sum_matrix(EX, N), sum_matrix(EY, N))
    Sxyc = np.kron(sum_matrix(EX, NC), sum_matrix(EY, NC))
    Mf, Nf = blocks(EX, M0), blocks(EX, N0)
    SM, SN = Sxy @ Mf, Sxy @ Nf
    F = face_rows(N)
    FC = face_rows(NC)
    out["Bf"] = right3(np.concatenate([Wz @ Sz, Kz @ Sz], 1))
    Sy = np.kron(np.eye(EX * N), sum_matrix(EY, N))
    for e in range(EX):
        cols = slice(e * ROWS, (e + 1) * ROWS)
        full = np.concatenate([(Sy @ Mf)[cols, cols], (Sy @ Nf)[cols, cols]], 1)
        xf = F[e * YF : (e + 1) * YF]
        face = np.concatenate([xf, F[2 * YF :]])
        packed = np.concatenate([SM[face][:, cols], SN[face][:, cols]], 1)
        out[f"Gb{e}"] = left3(np.concatenate([full, packed], 0))
    out["F2F"] = left3(np.concatenate([SM[F][:, F], SN[F][:, F]], 1))
    for e in range(EX):
        rows = slice(e * ROWS, (e + 1) * ROWS)
        here = np.concatenate([np.arange(e * YF, (e + 1) * YF), np.arange(2 * YF, len(F))])
        keep = ((F[here] // ROWS) == e).astype(float)[None, :]
        full = np.concatenate([(Sy @ Mf)[rows][:, F[here]] * keep, (Sy @ Nf)[rows][:, F[here]] * keep], 1)
        out[f"F2A{e}"] = left3(full)
    Rxy = blocks(EX, np.kron(J.T, blocks(EY, J.T)))
    JZ = blocks(EZ, J)
    selc = np.concatenate([np.arange(EX * ROWS_C), FC])
    RM, RN = (Sxyc @ Rxy @ Mf)[selc], (Sxyc @ Rxy @ Nf)[selc]
    out["Br"] = right3(np.concatenate([Wz @ JZ @ Szc, Kz @ JZ @ Szc], 1), "b")
    for e in range(EX):
        cols = slice(e * ROWS, (e + 1) * ROWS)
        out[f"Gr{e}"] = left3(np.concatenate([RM[:, cols], RN[:, cols]], 1), "b")
    out["F2R"] = left3(np.concatenate([RM[:, F], RN[:, F]], 1), "b")
    inv = lambda count: np.where((np.arange(count) % N == 0) | (np.arange(count) % N == N - 1), 0.5, 1.0)
    Wxy = np.kron(np.diag(inv(EX * N)), np.diag(inv(YF)))
    RW = (Sxyc @ Rxy @ Wxy)[selc]
    out["Bw"] = right3(np.diag(inv(ZF)) @ JZ @ Szc, "b")
    out["Gw"] = left3(RW, "b")
    M0c, N0c, Wzc, Kzc = level_matrices(COARSE_ORDER)
    Mc, Nc = blocks(EX, M0c), blocks(EX, N0c)
    out["Bc"] = right3(np.concatenate([Wzc @ Szc, Kzc @ Szc], 1), "c")
    out["Gc"] = left3(np.concatenate([(Sxyc @ Mc)[selc], (Sxyc @ Nc)[selc]], 1), "c")
    Jxy = blocks(EX, np.kron(J, blocks(EY, J)))
    out["Bj"] = right3(np.concatenate([JZ.T @ Wz @ Sz, JZ.T @ Kz @ Sz, JZ.T], 1), "d")
    sel = np.concatenate([np.arange(EX * ROWS), F])
    JM, JN = (SM @ Jxy)[sel], (SN @ Jxy)[sel]
    out["Gj"] = left3(np.concatenate([JM, JN], 1), "d")
    out["Gp"] = left3(Jxy, "d")
    for name, degree, rows in (("f", ORDER, F), ("c", COARSE_ORDER, None)):
        n = degree + 1
        _, w, K = gll_tables(degree)
        kd = np.diag(K)
        S = sum_matrix(EZ, n)
        spread_w = np.zeros((128, EZ * n))
        spread_k = np.zeros((128, EZ * n))
        for ez in range(EZ):
            spread_w[ez, ez * n : (ez + 1) * n] = w
            spread_k[ez, ez * n : (ez + 1) * n] = kd
        out["Bd" + name] = right3(np.concatenate([spread_w @ S, spread_k @ S], 1), "g")
        X, Y = EX * n, EY * n
        left = np.zeros((X * Y, 2, 80))
        for x in range(X):
            for y in range(Y):
                xs = [(x // n, x % n)]
                if x % n == 0:
                    xs.append((x // n - 1, n - 1))
                if x % n == n - 1:
                    xs.append((x // n + 1, 0))
                ys = [(y // n, y % n)]
                if y % n == 0:
                    ys.append((y // n - 1, n - 1))
                if y % n == n - 1:
                    ys.append((y // n + 1, 0))
                for ex, a in xs:
                    for ey, b in ys:
                        dx, dy = ex // EX, ey // EY
                        col = ((dx + 1) * 3 + dy + 1) * 8 + (ex % EX) * EY + ey % EY
                        left[x * Y + y, 0, col] += kd[a] * w[b] + w[a] * kd[b]
                        left[x * Y + y, 1, col] += w[a] * w[b]
        left = left.reshape(X * Y, 160)
        if rows is not None:
            left = np.concatenate([left, left[rows]], 0)
        out["Gd" + name] = left3(left, "g")
    spread = np.zeros((128, ZF + ZC))
    for ez in range(EZ):
        spread[ez, ez * N : (ez + 1) * N] = 1.0
        spread[ez, ZF + ez * NC : ZF + (ez + 1) * NC] = 1.0
    out["Bs"] = np.concatenate([spread.astype(np.float32).astype(BF16)] * 3, 0)
    return out


def dot(a, b):
    return jnp.dot(a, b, preferred_element_type=F32)


def split(x, n):
    out = []
    for i in range(1 + max(i for i, _ in TERMS[:n])):
        out.append(x.astype(BF16))
        x = x - out[-1].astype(F32)
    return out


def rmul(x, b, n, cols=slice(None)):
    p = split(x, n)
    x3 = jnp.concatenate([p[i] for i, _ in TERMS[:n]], 1)
    return dot(x3, b[: x3.shape[1], cols])


def lmul(g, *parts, n, rows=slice(None)):
    split_parts = [split(x, n) for x in parts]
    x3 = jnp.concatenate([p[i] for i, _ in TERMS[:n] for p in split_parts], 0)
    return dot(g[rows, : x3.shape[0]], x3)


def kernel_body(shape, names, rhs_ref, coef_ref, *refs):
    gxn, gyn, nz = shape
    ny = gxn // nz
    n_const = len(names)
    const_hbm = dict(zip(names, refs[:n_const]))
    sol_ref, res_ref = refs[n_const : n_const + 2]
    rest = refs[n_const + 2 :]
    const = dict(zip(names, rest[:n_const]))
    (Fr, Zr, Dr, Cr, DFr, DcFr, Lr, Sr, Rr, Ar, FXr, Wr, WLr,
     Dc_r, Cc_r, g_r, e_r, cpad, tiles,
     sx, sy, rx, ry, rc, csx, csy, crx, cry, crc, dots, dred,
     const_sem, send_sem, recv_sem, csend_sem, crecv_sem, tsend_sem, trecv_sem, dsend_sem, drecv_sem) = rest[n_const:]

    inv_center, a_f, k_f = cheb_numbers(ORDER)
    inv_center_c, a_c, k_c = cheb_numbers(COARSE_ORDER)
    px, py = lax.axis_index("gx"), lax.axis_index("gy")

    def at(dx, dy):
        return (lax.rem(px + dx + gxn, gxn), lax.rem(py + dy + gyn, gyn))

    around = [(dx, dy) for dx in (-1, 0, 1) for dy in (-1, 0, 1) if (dx, dy) != (0, 0)]
    pz, pyy = lax.rem(px, nz), px // nz
    stages = [
        [(px, lax.rem(py + d, gyn)) for d in range(1, gyn)],
        [(pyy * nz + lax.rem(pz + d, nz), py) for d in range(1, nz)],
        [(lax.rem(pyy + d, ny) * nz + pz, py) for d in range(1, ny)],
    ]

    copies = [pltpu.make_async_copy(const_hbm[m], const[m], const_sem.at[i]) for i, m in enumerate(names)]
    for c in copies:
        c.start()

    rc[...] = jnp.zeros_like(rc)
    crc[...] = jnp.zeros_like(crc)
    tiles[...] = jnp.zeros_like(tiles)
    cpad[...] = jnp.zeros_like(cpad)
    cpad[0:EY, 0:EZ] = coef_ref[0]
    cpad[EY : 2 * EY, 0:EZ] = coef_ref[1]

    barrier = pltpu.get_barrier_semaphore()
    partners = [at(dx, dy) for dx, dy in around] + [p for st in stages for p in st]
    for p in partners:
        pl.semaphore_signal(barrier, inc=1, device_id=p, device_id_type=MESH)

    def local_sum(v):
        rows = lax.broadcasted_iota(jnp.int32, v.shape, 0)
        lanes = lax.broadcasted_iota(jnp.int32, v.shape, 1)
        y = lax.rem(rows, YF)
        up = (lax.rem(y, N) == N - 1) & (y != YF - 1)
        down = (lax.rem(y, N) == 0) & (y != 0)
        v = v + jnp.where(up, pltpu.roll(v, ROWS - 1, 0), 0.0) + jnp.where(down, pltpu.roll(v, 1, 0), 0.0)
        up = (lax.rem(lanes, N) == N - 1) & (lanes != ZF - 1)
        down = (lax.rem(lanes, N) == 0) & (lanes != 0)
        return v + jnp.where(up, pltpu.roll(v, ZF - 1, 1), 0.0) + jnp.where(down, pltpu.roll(v, 1, 1), 0.0)

    def middle(ref, *index):
        total = ref[(*index, 0, pl.ds(ROWS - YF, YF))] + ref[(*index, 1, pl.ds(0, YF))]
        ref[(*index, 0, pl.ds(ROWS - YF, YF))] = total
        ref[(*index, 1, pl.ds(0, YF))] = total

    for e in range(EX):
        Fr[0, e] = local_sum(rhs_ref[e])
    middle(Fr, 0)
    sx[0, 0] = Fr[0, 0, 0:YF]
    sx[0, 1] = Fr[0, 1, ROWS - YF : ROWS]
    for x in range(EX * N):
        e, r = x // N, (x % N) * YF
        sy[0, 0, x : x + 1] = Fr[0, e, r : r + 1]
        sy[0, 1, x : x + 1] = Fr[0, e, r + YF - 1 : r + YF]

    def exchange(i, sx, sy, rx, ry, rc, send_sem, recv_sem):
        last = sy.shape[2] - 1
        plan = [
            (sx.at[i, 0], rx.at[i, 1], at(-1, 0)),
            (sx.at[i, 1], rx.at[i, 0], at(1, 0)),
            (sy.at[i, 0], ry.at[i, 1], at(0, -1)),
            (sy.at[i, 1], ry.at[i, 0], at(0, 1)),
            (sy.at[i, 0, pl.ds(0, 1)], rc.at[i, 1, pl.ds(last, 1)], at(-1, -1)),
            (sy.at[i, 0, pl.ds(last, 1)], rc.at[i, 1, pl.ds(0, 1)], at(1, -1)),
            (sy.at[i, 1, pl.ds(0, 1)], rc.at[i, 0, pl.ds(last, 1)], at(-1, 1)),
            (sy.at[i, 1, pl.ds(last, 1)], rc.at[i, 0, pl.ds(0, 1)], at(1, 1)),
        ]
        return [
            pltpu.make_async_remote_copy(
                src_ref=s, dst_ref=d, send_sem=send_sem.at[i, j], recv_sem=recv_sem.at[i, j],
                device_id=dev, device_id_type=MESH,
            )
            for j, (s, d, dev) in enumerate(plan)
        ]

    def fine(i):
        return exchange(i, sx, sy, rx, ry, rc, send_sem, recv_sem)

    def coarse(i):
        return exchange(i, csx, csy, crx, cry, crc, csend_sem, crecv_sem)

    def start(copies):
        for c in copies:
            c.start()

    def arrive(copies):
        for c in copies:
            c.wait_recv()

    pl.semaphore_wait(barrier, len(partners))

    tile_copies = []
    for j, (dx, dy) in enumerate(around):
        slot = ((1 - dx) * 3 + (1 - dy)) * 8
        tile_copies.append(pltpu.make_async_remote_copy(
            src_ref=cpad, dst_ref=tiles.at[pl.ds(slot, 8)], send_sem=tsend_sem.at[j], recv_sem=trecv_sem.at[j],
            device_id=at(dx, dy), device_id_type=MESH,
        ))
    start(tile_copies)
    start(fine(0))
    tiles[32:40] = cpad[...]

    for c in copies:
        c.wait()
    own = cpad[...]
    h1 = own.astype(BF16)
    r1 = own - h1.astype(F32)
    h2 = r1.astype(BF16)
    h3 = (r1 - h2.astype(F32)).astype(BF16)
    spread = dot(jnp.concatenate([h1, h2, h3], 1), const["Bs"][...])
    for e in range(EX):
        lines = [spread[e * EY + ey : e * EY + ey + 1] for ey in range(EY)]
        cf = [jnp.broadcast_to(l[:, :ZF], (N, ZF)) for l in lines]
        one = jnp.concatenate(cf, 0)
        Cr[e] = jnp.concatenate([one] * N, 0)
        FXr[0, e * YF : (e + 1) * YF] = one
        FXr[0, 2 * YF + e * N : 2 * YF + (e + 1) * N] = cf[0]
        FXr[0, 2 * YF + (EX + e) * N : 2 * YF + (EX + e + 1) * N] = cf[EY - 1]
        cc = jnp.concatenate([jnp.broadcast_to(l[:, ZF:], (NC, ZC)) for l in lines], 0)
        Cc_r[e * ROWS_C : (e + 1) * ROWS_C] = jnp.concatenate([cc] * NC, 0)

    rows = lax.broadcasted_iota(jnp.int32, (ROWS, ZF), 0)
    lanes = lax.broadcasted_iota(jnp.int32, (ROWS, ZF), 1)
    xr, yr = rows // YF, lax.rem(rows, YF)

    def edge(i):
        return (lax.rem(i, N) == 0) | (lax.rem(i, N) == N - 1)

    wz = jnp.where(edge(lanes), 0.5, 1.0)
    Wr[...] = wz * jnp.where(edge(yr), 0.5, 1.0) * jnp.where(edge(xr), 0.5, 1.0)
    wl = wz * jnp.where(edge(yr) & (yr != 0) & (yr != YF - 1), 0.5, 1.0)
    WLr[0] = wl * jnp.where(xr == N - 1, 0.5, 1.0)
    WLr[1] = wl * jnp.where(xr == 0, 0.5, 1.0)

    arrive(tile_copies)
    ext = tiles[...]
    pd = rmul(ext, const["Bdf"], HOW["g"])
    diag = lmul(const["Gdf"], pd[:, :ZF], pd[:, ZF:], n=HOW["g"])

    def mask_of(x, y, z, n):
        inside = (x != 0) & (x != gxn * EX * n - 1) & (y != 0) & (y != gyn * EY * n - 1)
        return inside & (z != 0) & (z != EZ * n - 1)

    for e in range(EX):
        keep = mask_of(px * EX * N + e * N + xr, py * YF + yr, lanes, N)
        Dr[e] = jnp.where(keep, 1.0 / diag[e * ROWS : (e + 1) * ROWS], 0.0)
    frow = lax.broadcasted_iota(jnp.int32, (96, ZF), 0)
    flane = lax.broadcasted_iota(jnp.int32, (96, ZF), 1)
    fx = jnp.where(frow < YF, 0, jnp.where(frow < 2 * YF, EX * N - 1, lax.rem(frow, EX * N)))
    fy = jnp.where(frow < 2 * YF, lax.rem(frow, YF), jnp.where(frow < 2 * YF + EX * N, 0, YF - 1))
    keep = mask_of(px * EX * N + fx, py * YF + fy, flane, N)
    df = jnp.where(keep, 1.0 / diag[EX * ROWS :], 0.0)
    DFr[...] = df
    DcFr[...] = df * FXr[0]
    pdc = rmul(ext, const["Bdc"], HOW["g"])
    diag_c = lmul(const["Gdc"], pdc[:, :ZC], pdc[:, ZC:], n=HOW["g"])
    crow = lax.broadcasted_iota(jnp.int32, (EX * ROWS_C, ZC), 0)
    clane = lax.broadcasted_iota(jnp.int32, (EX * ROWS_C, ZC), 1)
    keep = mask_of(px * EX * NC + crow // YC, py * YC + lax.rem(crow, YC), clane, NC)
    Dc_r[...] = jnp.where(keep, 1.0 / diag_c, 0.0)

    def halo(i):
        arrive(fine(i))
        return jnp.concatenate([rx[i, 0], rx[i, 1], ry[i, 0] + rc[i, 0], ry[i, 1] + rc[i, 1]], 0)

    def add_faces(ref, index, h):
        ref[(*index, 0, pl.ds(0, YF))] += h[0:YF]
        ref[(*index, 1, pl.ds(ROWS - YF, YF))] += h[YF : 2 * YF]
        for x in range(EX * N):
            e, r = x // N, (x % N) * YF
            ref[(*index, e, pl.ds(r, 1))] += h[2 * YF + x : 2 * YF + x + 1]
            b = 2 * YF + EX * N + x
            ref[(*index, e, pl.ds(r + YF - 1, 1))] += h[b : b + 1]

    def bulk(values, n):
        y0 = y1 = None
        for e in range(EX):
            p = rmul(values(e), const["Bf"], n)
            o = lmul(const[f"Gb{e}"], p[:, :ZF], p[:, ZF:], n=n)
            Lr[e] = o[:ROWS]
            FXr[1, e * YF : (e + 1) * YF] = o[ROWS : ROWS + YF]
            y0 = o[ROWS + YF :] if e == 0 else y0 + o[ROWS + YF :]
        FXr[1, 2 * YF :] = y0

    def face_z(hs, n):
        return rmul(hs, const["Bf"], n)

    def send_faces(i, faces):
        sx[i, 0] = faces[0:YF]
        sx[i, 1] = faces[YF : 2 * YF]
        sy[i, 0] = faces[2 * YF : 2 * YF + EX * N]
        sy[i, 1] = faces[2 * YF + EX * N :]
        start(fine(i))

    def face_to_face(ph, n):
        return lmul(const["F2F"], ph[:, :ZF], ph[:, ZF:], n=n)

    def face_to_all(ph, n):
        for e in range(EX):
            part = jnp.concatenate([ph[e * YF : (e + 1) * YF], ph[2 * YF :]], 0)
            Lr[e] += lmul(const[f"F2A{e}"], part[:, :ZF], part[:, ZF:], n=n)
        middle(Lr)

    def coarse_faces(i, o):
        csx[i, 0] = o[0:YC]
        csx[i, 1] = o[YC : 2 * YC]
        csy[i, 0] = o[2 * YC : 2 * YC + EX * NC]
        csy[i, 1] = o[2 * YC + EX * NC :]
        start(coarse(i))

    def coarse_arrive(i, ref):
        arrive(coarse(i))
        ref[0:YC] += crx[i, 0]
        ref[EX * ROWS_C - YC : EX * ROWS_C] += crx[i, 1]
        h0, h1 = cry[i, 0] + crc[i, 0], cry[i, 1] + crc[i, 1]
        for x in range(EX * NC):
            ref[x * YC : x * YC + 1] += h0[x : x + 1]
            ref[x * YC + YC - 1 : x * YC + YC] += h1[x : x + 1]

    def cycle(k, carry):
        bulk(lambda e: Cr[e] * (Dr[e] * inv_center) * Fr[k, e], HOW["a"])
        h = halo(4 * k)
        ph = face_z(DcFr[...] * inv_center * h, HOW["a"])
        send_faces(4 * k + 1, FXr[1] + face_to_face(ph, HOW["a"]))
        add_faces(Fr, (k,), h)
        face_to_all(ph, HOW["a"])
        gl = None
        for e in range(EX):
            s = Dr[e] * (a_f * Fr[k, e] - k_f * Lr[e])
            Sr[e] = s
            p = rmul(Cr[e] * s, const["Br"], HOW["b"])
            f = rmul(Fr[k, e], const["Bw"], HOW["b"])
            o = -lmul(const[f"Gr{e}"], p[:, :ZC], p[:, ZC:], n=HOW["b"])
            gl = o if e == 0 else gl + o
            Ar[e, :, 0:ZC] = f
        gl = gl + lmul(const["Gw"], Ar[0, :, 0:ZC], Ar[1, :, 0:ZC], n=HOW["b"])
        h = halo(4 * k + 1)
        hs = (-k_f) * DcFr[...] * h
        pr = rmul(hs, const["Br"], HOW["b"])
        gl = gl - lmul(const["F2R"], pr[:, :ZC], pr[:, ZC:], n=HOW["b"])
        coarse_faces(2 * k, gl[EX * ROWS_C :])
        g_r[...] = gl[: EX * ROWS_C]
        bulk(lambda e: Cr[e] * Sr[e], HOW["s"])
        ph = face_z(hs, HOW["s"])
        face_to_all(ph, HOW["s"])
        FXr[1] = FXr[1] + face_to_face(ph, HOW["s"])
        add_faces(Sr, (), (-k_f) * DFr[...] * h)
        coarse_arrive(2 * k, g_r)
        p = rmul(Cc_r[...] * (Dc_r[...] * inv_center_c) * g_r[...], const["Bc"], HOW["c"])
        o = lmul(const["Gc"], p[:, :ZC], p[:, ZC:], n=HOW["c"])
        coarse_faces(2 * k + 1, o[EX * ROWS_C :])
        e_r[...] = o[: EX * ROWS_C]
        coarse_arrive(2 * k + 1, e_r)
        fix = Dc_r[...] * (a_c * g_r[...] - k_c * e_r[...])
        p = rmul(Cc_r[...] * fix, const["Bj"], HOW["d"], slice(0, 2 * ZF))
        o = lmul(const["Gj"], p[:, :ZF], p[:, ZF:], n=HOW["d"])
        send_faces(4 * k + 2, FXr[1] + o[EX * ROWS :])
        p = rmul(fix, const["Bj"], HOW["d"], slice(2 * ZF, 3 * ZF))
        up = lmul(const["Gp"], p, n=HOW["d"])
        for e in range(EX):
            rows = slice(e * ROWS, (e + 1) * ROWS)
            Sr[e] = Sr[e] + up[rows]
            Rr[e] = Fr[k, e] - Lr[e] - o[rows]
        bulk(lambda e: Cr[e] * (Dr[e] * inv_center) * Rr[e], HOW["e"])
        h = halo(4 * k + 2)
        ph = face_z((-inv_center) * DcFr[...] * h, HOW["e"])
        send_faces(4 * k + 3, FXr[1] + face_to_face(ph, HOW["e"]))
        add_faces(Rr, (), -h)
        face_to_all(ph, HOW["e"])
        for e in range(EX):
            Zr[k, e] = Sr[e] + Dr[e] * (a_f * Rr[e] - k_f * Lr[e])
        bulk(lambda e: Cr[e] * Zr[k, e], HOW["f"])
        h = halo(4 * k + 3)
        ph = face_z((-k_f) * DcFr[...] * h, HOW["f"])
        send_faces(4 * k + 4, FXr[1] + face_to_face(ph, HOW["f"]))
        add_faces(Zr, (k,), (-k_f) * DFr[...] * h)
        face_to_all(ph, HOW["f"])
        sums = [0.0] * 4
        for e in range(EX):
            z, l = Zr[k, e], Lr[e]
            Fr[k + 1, e] = l
            wz = Wr[...] * z
            wl = WLr[e] * l
            for i, t in enumerate((Fr[0, e] * wz, Fr[k, e] * wz, Zr[0, e] * wl, z * wl)):
                t = jnp.sum(t, axis=0, keepdims=True)
                sums[i] = sums[i] + t[:, : ZF // 2] + t[:, ZF // 2 :]
        dots[k, 0:4] = jnp.concatenate(sums, 0)
        return carry

    lax.fori_loop(0, 2, cycle, 0)

    dred[0, 0, 0:4] = dots[0, 0:4]
    dred[0, 0, 4:8] = dots[1, 0:4]
    dot_copies = []
    count = 0
    for s, stage in enumerate(stages):
        now = []
        for j, p in enumerate(stage):
            now.append(pltpu.make_async_remote_copy(
                src_ref=dred.at[s, 0], dst_ref=dred.at[s, j + 1], send_sem=dsend_sem.at[count], recv_sem=drecv_sem.at[count],
                device_id=p, device_id_type=MESH,
            ))
            count += 1
        start(now)
        arrive(now)
        total = dred[s, 0]
        for j in range(len(stage)):
            total = total + dred[s, j + 1]
        dred[s + 1, 0] = total
        dot_copies += now
    lanes_sum = jnp.sum(dred[3, 0], axis=1, keepdims=True)
    pick = lambda i: lanes_sum[i : i + 1, 0:1]
    rz0, c00 = pick(1), pick(3)
    r0u, wu, zv, uv = pick(4), pick(5), pick(6), pick(7)
    alpha0 = rz0 / c00
    rz1 = alpha0 * (alpha0 * wu - r0u)
    beta1 = 1.0 + rz1 / rz0
    curve = beta1 * beta1 * c00 - beta1 * alpha0 * (zv + wu) + alpha0 * alpha0 * uv
    alpha1 = rz1 / curve
    c_z = alpha0 + alpha1 * beta1
    c_u = alpha1 * alpha0
    for e in range(EX):
        sol_ref[e] = c_z * Zr[0, e] - c_u * Zr[1, e]
    h = halo(8)
    add_faces(Fr, (2,), h)
    for e in range(EX):
        res_ref[e] = jnp.where(Dr[e] > 0.0, Fr[0, e] - c_z * Fr[1, e] + c_u * Fr[2, e], 0.0)

    for c in tile_copies + dot_copies:
        c.wait_send()

    def drain(i, carry):
        for c in fine(i):
            c.wait_send()
        return carry

    lax.fori_loop(0, 9, drain, 0)

    def drain_c(i, carry):
        for c in coarse(i):
            c.wait_send()
        return carry

    lax.fori_loop(0, 4, drain_c, 0)


def solution(mesh):
    gxn, gyn = mesh.shape["gx"], mesh.shape["gy"]
    nz = 8 if gxn == 32 else 2
    ny = gxn // nz
    table = constants()
    names = tuple(table)
    n_dots = gyn - 1 + nz - 1 + ny - 1
    most = max(gyn, nz, ny)

    def per_device(right_side, coefficient):
        rhs = right_side.reshape(EX, ROWS, ZF)
        field = (EX, ROWS, ZF)
        vm = lambda *s: pltpu.VMEM(s, F32)
        dma = lambda *s: pltpu.SemaphoreType.DMA(s)
        scratch = [pltpu.VMEM(table[m].shape, BF16) for m in names]
        scratch += [
            vm(3, *field), vm(2, *field), vm(*field), vm(*field), vm(96, ZF), vm(96, ZF),
            vm(*field), vm(*field), vm(*field), vm(*field), vm(2, 96, ZF), vm(ROWS, ZF), vm(*field),
            vm(EX * ROWS_C, ZC), vm(EX * ROWS_C, ZC), vm(EX * ROWS_C, ZC), vm(EX * ROWS_C, ZC), vm(8, 128), vm(80, 128),
            vm(9, 2, YF, ZF), vm(9, 2, EX * N, ZF), vm(9, 2, YF, ZF), vm(9, 2, EX * N, ZF), vm(9, 2, EX * N, ZF),
            vm(4, 2, YC, ZC), vm(4, 2, EX * NC, ZC), vm(4, 2, YC, ZC), vm(4, 2, EX * NC, ZC), vm(4, 2, EX * NC, ZC),
            vm(2, 8, 128), vm(4, most, 8, 128),
            dma(len(names)), dma(9, 8), dma(9, 8), dma(4, 8), dma(4, 8), dma(8), dma(8), dma(n_dots), dma(n_dots),
        ]
        sol, res = pl.pallas_call(
            functools.partial(kernel_body, (gxn, gyn, nz), names),
            out_shape=[jax.ShapeDtypeStruct(field, F32)] * 2,
            in_specs=[pl.BlockSpec(memory_space=pltpu.VMEM)] * 2 + [pl.BlockSpec(memory_space=pl.ANY)] * len(names),
            out_specs=[pl.BlockSpec(memory_space=pltpu.VMEM)] * 2,
            scratch_shapes=scratch,
            compiler_params=pltpu.CompilerParams(
                collective_id=0, has_side_effects=True, vmem_limit_bytes=56 * 2**20
            ),
        )(rhs, coefficient, *[jnp.asarray(table[m]) for m in names])
        return sol.reshape(right_side.shape), res.reshape(right_side.shape)

    spec = P("gx", "gy", None)
    return jax.shard_map(
        per_device, mesh=mesh, in_specs=(spec, spec), out_specs=(spec, spec), check_vma=False
    )
```

```python
import functools
import math

import jax
import jax.numpy as jnp
import numpy as np
from jax import lax
from jax.experimental import pallas as pl
from jax.experimental.pallas import tpu as pltpu
from jax.sharding import PartitionSpec as P

ORDER = 7
COARSE_ORDER = 3
F32 = jnp.float32
BF16 = jnp.bfloat16
MESH = pl.DeviceIdType.MESH

EX, EY, EZ = 2, 4, 32
N, NC = ORDER + 1, COARSE_ORDER + 1
YF, ZF = EY * N, EZ * N
YC, ZC = EY * NC, EZ * NC
ROWS = N * YF
ROWS_C = NC * YC


def legendre_pair(degree, points):
    before = points * 0.0 + 1.0
    now = points.copy()
    for power in range(2, degree + 1):
        after = ((2 * power - 1) * points * now - (power - 1) * before) / power
        before = now
        now = after
    return (now, before)


def gll_tables(degree):
    number = degree + 1
    points = np.cos(math.pi * np.arange(number) / degree)
    for newton in range(60):
        top, below = legendre_pair(degree, points)
        points = points - (points * top - below) / (number * top)
    points = points[::-1].copy()
    points[0] = -1.0
    points[degree] = 1.0
    values = legendre_pair(degree, points)[0]
    weights = 2.0 / (degree * (degree + 1) * values**2)
    derivative = np.zeros((number, number))
    for row_index in range(number):
        for column_index in range(number):
            if row_index != column_index:
                derivative[row_index, column_index] = values[row_index] / (
                    values[column_index] * (points[row_index] - points[column_index])
                )
    derivative[0, 0] = -degree * (degree + 1) / 4.0
    derivative[degree, degree] = degree * (degree + 1) / 4.0
    stiffness = derivative.T @ (weights[:, None] * derivative)
    return (points, weights, stiffness)


def upper_bound(degree):
    points, weights, stiffness = gll_tables(degree)
    rowsum = np.abs(stiffness).sum(1)
    diagonal = np.diag(stiffness)
    outer = lambda a, b, c: a[:, None, None] * b[None, :, None] * c[None, None, :]
    top = outer(rowsum, weights, weights) + outer(weights, rowsum, weights) + outer(weights, weights, rowsum)
    bottom = outer(diagonal, weights, weights) + outer(weights, diagonal, weights) + outer(weights, weights, diagonal)
    return float((top / bottom).max())


def interpolation_matrix(fine_degree, coarse_degree):
    fine_points = gll_tables(fine_degree)[0]
    coarse_points = gll_tables(coarse_degree)[0]
    matrix = np.ones((fine_degree + 1, coarse_degree + 1))
    for column_index in range(coarse_degree + 1):
        for other_index in range(coarse_degree + 1):
            if other_index != column_index:
                matrix[:, column_index] *= (fine_points - coarse_points[other_index]) / (
                    coarse_points[column_index] - coarse_points[other_index]
                )
    return matrix


def cheb_numbers(degree):
    upper = upper_bound(degree)
    lower = 0.1 * upper
    center = 0.5 * (upper + lower)
    half = 0.5 * (upper - lower)
    previous = half / center
    current = 1.0 / (2.0 * center / half - previous)
    k = 2.0 * current / half
    return (1.0 / center, (1.0 + current * previous) / center + k, k)


def sum_matrix(elements, number):
    matrix = np.eye(elements * number)
    for e in range(elements - 1):
        a, b = e * number + number - 1, (e + 1) * number
        matrix[a, b] = matrix[b, a] = 1.0
    return matrix


def blocks(count, matrix):
    return np.kron(np.eye(count), matrix)


TERMS = ((0, 0), (1, 0), (0, 1), (2, 0), (0, 2), (1, 1))
HOW = dict(a=3, b=3, s=6, c=3, d=6, e=3, f=6, g=3, h=3)


def pieces_of(matrix, count):
    rest, out = np.asarray(matrix, np.float64), []
    for _ in range(count):
        out.append(rest.astype(np.float32).astype(BF16))
        rest = rest - out[-1].astype(np.float64)
    return out


def right3(matrix, steps="asef"):
    p = pieces_of(matrix, 3)
    return np.concatenate([p[j] for _, j in TERMS[: max(HOW[t] for t in steps)]], 0)


def left3(matrix, steps="asef"):
    p = pieces_of(matrix, 3)
    return np.concatenate([p[j] for _, j in TERMS[: max(HOW[t] for t in steps)]], 1)


def level_matrices(degree):
    _, w, K = gll_tables(degree)
    n = degree + 1
    wy = np.tile(w, EY)
    M0 = np.kron(K, np.diag(wy)) + np.kron(np.diag(w), blocks(EY, K))
    N0 = np.kron(np.diag(w), np.diag(wy))
    return M0, N0, np.diag(np.tile(w, EZ)), blocks(EZ, K)


def face_rows(n):
    y = EY * n
    x = EX * n
    rows = [j for j in range(y)] + [(x - 1) * y + j for j in range(y)]
    rows += [i * y for i in range(x)] + [i * y + y - 1 for i in range(x)]
    return np.array(rows)


def coarse_places():
    XC = EX * NC
    before, after_x, after_y = range(-NC, 0), range(XC, XC + NC), range(YC, YC + NC)
    grids = [(range(XC), range(YC)), (before, range(YC)), (after_x, range(YC)), (range(XC), before), (range(XC), after_y)]
    grids += [(a, b) for a in (before, after_x) for b in (before, after_y)]
    both = [(x, y) for xs, ys in grids for x in xs for y in ys]
    return np.array([p[0] for p in both]), np.array([p[1] for p in both])


@functools.cache
def constants():
    J = interpolation_matrix(ORDER, COARSE_ORDER)
    out = {}
    M0, N0, Wz, Kz = level_matrices(ORDER)
    Sz, Szc = sum_matrix(EZ, N), sum_matrix(EZ, NC)
    Sxy = np.kron(sum_matrix(EX, N), sum_matrix(EY, N))
    Sxyc = np.kron(sum_matrix(EX, NC), sum_matrix(EY, NC))
    Mf, Nf = blocks(EX, M0), blocks(EX, N0)
    SM, SN = Sxy @ Mf, Sxy @ Nf
    F = face_rows(N)
    out["Bf"] = right3(np.concatenate([Wz @ Sz, Kz @ Sz], 1))
    Sy = np.kron(np.eye(EX * N), sum_matrix(EY, N))
    for e in range(EX):
        cols = slice(e * ROWS, (e + 1) * ROWS)
        full = np.concatenate([(Sy @ Mf)[cols, cols], (Sy @ Nf)[cols, cols]], 1)
        xf = F[e * YF : (e + 1) * YF]
        face = np.concatenate([xf, F[2 * YF :]])
        packed = np.concatenate([SM[face][:, cols], SN[face][:, cols]], 1)
        out[f"Gb{e}"] = left3(np.concatenate([full, packed], 0))
    out["F2F"] = left3(np.concatenate([SM[F][:, F], SN[F][:, F]], 1))
    for e in range(EX):
        rows = slice(e * ROWS, (e + 1) * ROWS)
        here = np.concatenate([np.arange(e * YF, (e + 1) * YF), np.arange(2 * YF, len(F))])
        keep = ((F[here] // ROWS) == e).astype(float)[None, :]
        full = np.concatenate([(Sy @ Mf)[rows][:, F[here]] * keep, (Sy @ Nf)[rows][:, F[here]] * keep], 1)
        out[f"F2A{e}"] = left3(full)
    Rxy = blocks(EX, np.kron(J.T, blocks(EY, J.T)))
    JZ = blocks(EZ, J)
    XC = EX * NC
    first = [x * YC + y for x in range(XC) for y in range(NC)]
    last = [x * YC + YC - NC + y for x in range(XC) for y in range(NC)]
    selc = np.concatenate([np.arange(XC * YC), first, last]).astype(int)
    RM, RN = (Sxyc @ Rxy @ Mf)[selc], (Sxyc @ Rxy @ Nf)[selc]
    out["Br"] = right3(np.concatenate([Wz @ JZ @ Szc, Kz @ JZ @ Szc], 1), "b")
    for e in range(EX):
        cols = slice(e * ROWS, (e + 1) * ROWS)
        out[f"Gr{e}"] = left3(np.concatenate([RM[:, cols], RN[:, cols]], 1), "b")
    out["F2R"] = left3(np.concatenate([RM[:, F], RN[:, F]], 1), "b")
    inv = lambda count: np.where((np.arange(count) % N == 0) | (np.arange(count) % N == N - 1), 0.5, 1.0)
    Wxy = np.kron(np.diag(inv(EX * N)), np.diag(inv(YF)))
    RW = (Sxyc @ Rxy @ Wxy)[selc]
    out["Bw"] = right3(np.diag(inv(ZF)) @ JZ @ Szc, "b")
    out["Gw"] = left3(RW, "b")
    _, wc, Kc = gll_tables(COARSE_ORDER)
    Wzc, Kzc = np.diag(np.tile(wc, EZ)), blocks(EZ, Kc)
    out["Bc"] = right3(np.concatenate([Wzc @ Szc, Kzc @ Szc], 1), "c")
    cx, cy = coarse_places()
    grid = (cx + NC) * (YC + 2 * NC) + cy + NC
    wx4, wy6 = np.diag(np.tile(wc, EX + 2)), np.diag(np.tile(wc, EY + 2))
    Me = np.kron(blocks(EX + 2, Kc), wy6) + np.kron(wx4, blocks(EY + 2, Kc))
    Ne = np.kron(wx4, wy6)
    Se = np.kron(sum_matrix(EX + 2, NC), sum_matrix(EY + 2, NC))
    own = grid[: XC * YC]
    out["Gc"] = left3(np.concatenate([(Se @ Me)[own][:, grid], (Se @ Ne)[own][:, grid]], 1), "c")
    same = lambda p, ends: (p[:, None] == p[None, :]) | sum(
        ((p[:, None] == a) & (p[None, :] == b)) | ((p[:, None] == b) & (p[None, :] == a)) for a, b in ends
    ).astype(bool)
    T = (same(cx, [(-1, 0), (XC - 1, XC)]) & same(cy, [(-1, 0), (YC - 1, YC)])).astype(np.float32).astype(BF16)
    out["T"] = np.concatenate([T, T], 1)
    pick = np.zeros((len(cx), 80))
    for i, (x, y) in enumerate(zip(cx // NC, cy // NC)):
        pick[i, ((x // EX + 1) * 3 + y // EY + 1) * 8 + (x % EX) * EY + y % EY] = 1.0
    out["Pc"] = np.concatenate([pick.astype(np.float32).astype(BF16)] * 3, 1)
    Jxy = blocks(EX, np.kron(J, blocks(EY, J)))
    out["Bj"] = right3(np.concatenate([JZ.T @ Wz @ Sz, JZ.T @ Kz @ Sz, JZ.T], 1), "d")
    sel = np.concatenate([np.arange(EX * ROWS), F])
    JM, JN = (SM @ Jxy)[sel], (SN @ Jxy)[sel]
    out["Gj"] = left3(np.concatenate([JM, JN], 1), "d")
    out["Gp"] = left3(Jxy, "d")
    fine_x, fine_y = np.divmod(np.arange(EX * ROWS), YF)
    places = {"f": (np.concatenate([fine_x, F // YF]), np.concatenate([fine_y, F % YF])), "c": (cx, cy)}
    for name, degree in (("f", ORDER), ("c", COARSE_ORDER)):
        n = degree + 1
        _, w, K = gll_tables(degree)
        kd = np.diag(K)
        S = sum_matrix(EZ, n)
        spread_w = np.zeros((128, EZ * n))
        spread_k = np.zeros((128, EZ * n))
        for ez in range(EZ):
            spread_w[ez, ez * n : (ez + 1) * n] = w
            spread_k[ez, ez * n : (ez + 1) * n] = kd
        out["Bd" + name] = right3(np.concatenate([spread_w @ S, spread_k @ S], 1), "g")
        left = np.zeros((len(places[name][0]), 2, 80))
        for i, (x, y) in enumerate(zip(*places[name])):
            xs = [(x // n, x % n)]
            if x % n == 0:
                xs.append((x // n - 1, n - 1))
            if x % n == n - 1:
                xs.append((x // n + 1, 0))
            ys = [(y // n, y % n)]
            if y % n == 0:
                ys.append((y // n - 1, n - 1))
            if y % n == n - 1:
                ys.append((y // n + 1, 0))
            for ex, a in xs:
                for ey, b in ys:
                    col = ((ex // EX + 1) * 3 + ey // EY + 1) * 8 + (ex % EX) * EY + ey % EY
                    left[i, 0, col] += kd[a] * w[b] + w[a] * kd[b]
                    left[i, 1, col] += w[a] * w[b]
        left = left.reshape(len(left), 160)
        out["Gd" + name] = left3(left, "g")
    spread = np.zeros((128, ZF + ZC))
    for ez in range(EZ):
        spread[ez, ez * N : (ez + 1) * N] = 1.0
        spread[ez, ZF + ez * NC : ZF + (ez + 1) * NC] = 1.0
    out["Bs"] = np.concatenate([spread.astype(np.float32).astype(BF16)] * 3, 0)
    return out


def dot(a, b):
    return jnp.dot(a, b, preferred_element_type=F32)


def split(x, n):
    out = []
    for i in range(1 + max(i for i, _ in TERMS[:n])):
        out.append(x.astype(BF16))
        x = x - out[-1].astype(F32)
    return out


def rmul(x, b, n, cols=slice(None)):
    p = split(x, n)
    x3 = jnp.concatenate([p[i] for i, _ in TERMS[:n]], 1)
    return dot(x3, b[: x3.shape[1], cols])


def lmul(g, *parts, n, rows=slice(None)):
    split_parts = [split(x, n) for x in parts]
    x3 = jnp.concatenate([p[i] for i, _ in TERMS[:n] for p in split_parts], 0)
    return dot(g[rows, : x3.shape[0]], x3)


def kernel_body(shape, names, rhs_ref, coef_ref, *refs):
    gxn, gyn = shape
    n_const = len(names)
    const_hbm = dict(zip(names, refs[:n_const]))
    sol_ref, res_ref = refs[n_const : n_const + 2]
    rest = refs[n_const + 2 :]
    const = dict(zip(names, rest[:n_const]))
    (Fr, Zr, Dr, Cr, DFr, DcFr, Lr, Sr, Rr, Ar, FXr, FFr, PHr, Hr, Wr, WLr, WFr, WLFr,
     Dc_r, Cc_r, cpad, tiles,
     sx, sy, rx, ry, rc, cs, cr, dots, d1, d2,
     const_sem, send_sem, recv_sem, csend_sem, crecv_sem, tsend_sem, trecv_sem, dsend_sem, drecv_sem) = rest[n_const:]

    inv_center, a_f, k_f = cheb_numbers(ORDER)
    inv_center_c, a_c, k_c = cheb_numbers(COARSE_ORDER)
    px, py = lax.axis_index("gx"), lax.axis_index("gy")
    XF, XC, OWN = EX * N, EX * NC, EX * ROWS_C

    def at(dx, dy):
        return (lax.rem(px + dx + gxn, gxn), lax.rem(py + dy + gyn, gyn))

    def inside(dx, dy):
        ok = None
        for p, d, n in ((px, dx, gxn), (py, dy, gyn)):
            if d:
                here = (p > 0) if d < 0 else (p < n - 1)
                ok = here if ok is None else ok & here
        return ok

    corners = [(dx, dy) for dx in (-1, 1) for dy in (-1, 1)]
    around = corners + [(-1, 0), (1, 0), (0, -1), (0, 1)]
    stages = [
        [(px, lax.rem(py + d, gyn)) for d in range(1, gyn)],
        [(lax.rem(px + d, gxn), py) for d in range(1, gxn)],
    ]

    copies = [pltpu.make_async_copy(const_hbm[m], const[m], const_sem.at[i]) for i, m in enumerate(names)]
    for c in copies:
        c.start()

    for ref in (rx, ry, rc, cr, tiles, cpad):
        ref[...] = jnp.zeros_like(ref)
    cpad[0:EY, 0:EZ] = coef_ref[0]
    cpad[EY : 2 * EY, 0:EZ] = coef_ref[1]

    barrier = pltpu.get_barrier_semaphore()
    expected = 0
    for d in around:
        pl.when(inside(*d))(
            lambda d=d: pl.semaphore_signal(barrier, inc=1, device_id=at(*d), device_id_type=MESH)
        )
        expected = expected + inside(*d).astype(jnp.int32)
    for stage in stages:
        for p in stage:
            pl.semaphore_signal(barrier, inc=1, device_id=p, device_id_type=MESH)
        expected = expected + len(stage)

    def local_sum(v):
        rows = lax.broadcasted_iota(jnp.int32, v.shape, 0)
        lanes = lax.broadcasted_iota(jnp.int32, v.shape, 1)
        y = lax.rem(rows, YF)
        up = (lax.rem(y, N) == N - 1) & (y != YF - 1)
        down = (lax.rem(y, N) == 0) & (y != 0)
        v = v + jnp.where(up, pltpu.roll(v, ROWS - 1, 0), 0.0) + jnp.where(down, pltpu.roll(v, 1, 0), 0.0)
        up = (lax.rem(lanes, N) == N - 1) & (lanes != ZF - 1)
        down = (lax.rem(lanes, N) == 0) & (lanes != 0)
        return v + jnp.where(up, pltpu.roll(v, ZF - 1, 1), 0.0) + jnp.where(down, pltpu.roll(v, 1, 1), 0.0)

    def middle(ref, *index):
        total = ref[(*index, 0, pl.ds(ROWS - YF, YF))] + ref[(*index, 1, pl.ds(0, YF))]
        ref[(*index, 0, pl.ds(ROWS - YF, YF))] = total
        ref[(*index, 1, pl.ds(0, YF))] = total

    for e in range(EX):
        Fr[0, e] = local_sum(rhs_ref[e])
    middle(Fr, 0)
    sx[0, 0] = Fr[0, 0, 0:YF]
    sx[0, 1] = Fr[0, 1, ROWS - YF : ROWS]
    for x in range(XF):
        e, r = x // N, (x % N) * YF
        sy[0, 0, x : x + 1] = Fr[0, e, r : r + 1]
        sy[0, 1, x : x + 1] = Fr[0, e, r + YF - 1 : r + YF]

    class Exchange:
        def __init__(self, plan, send, recv):
            self.plan = [
                (pltpu.make_async_remote_copy(
                    src_ref=s, dst_ref=t, send_sem=send(j), recv_sem=recv(j), device_id=at(*d), device_id_type=MESH,
                ), inside(*d), inside(-d[0], -d[1]))
                for j, (s, t, d) in enumerate(plan)
            ]

        def start(self):
            for c, to, _ in self.plan:
                pl.when(to)(c.start)

        def arrive(self):
            for c, _, come in self.plan:
                pl.when(come)(c.wait_recv)

        def drain(self):
            for c, to, _ in self.plan:
                pl.when(to)(c.wait_send)

    def fine(i):
        one = lambda r: pl.ds(r, 1)
        plan = [
            (sy.at[i, 0, one(0)], rc.at[i, 1, one(XF - 1)], (-1, -1)),
            (sy.at[i, 1, one(0)], rc.at[i, 0, one(XF - 1)], (-1, 1)),
            (sy.at[i, 0, one(XF - 1)], rc.at[i, 1, one(0)], (1, -1)),
            (sy.at[i, 1, one(XF - 1)], rc.at[i, 0, one(0)], (1, 1)),
            (sx.at[i, 0], rx.at[i, 1], (-1, 0)),
            (sx.at[i, 1], rx.at[i, 0], (1, 0)),
            (sy.at[i, 0], ry.at[i, 1], (0, -1)),
            (sy.at[i, 1], ry.at[i, 0], (0, 1)),
        ]
        return Exchange(plan, lambda j: send_sem.at[i, j], lambda j: recv_sem.at[i, j])

    def coarse(k):
        h, q = ROWS_C, NC * NC
        y0, y1 = OWN, OWN + XC * NC
        c0 = 2 * h + 4 * q
        src = lambda a, n: cs.at[k, pl.ds(a, n)]
        dst = lambda a, n: cr.at[k, pl.ds(a, n)]
        plan = [
            (src(y0, q), dst(c0 + 3 * q, q), (-1, -1)),
            (src(y1, q), dst(c0 + 2 * q, q), (-1, 1)),
            (src(y0 + q, q), dst(c0 + q, q), (1, -1)),
            (src(y1 + q, q), dst(c0, q), (1, 1)),
            (src(0, h), dst(h, h), (-1, 0)),
            (src(h, h), dst(0, h), (1, 0)),
            (src(y0, 2 * q), dst(2 * h + 2 * q, 2 * q), (0, -1)),
            (src(y1, 2 * q), dst(2 * h, 2 * q), (0, 1)),
        ]
        return Exchange(plan, lambda j: csend_sem.at[k, j], lambda j: crecv_sem.at[k, j])

    pl.semaphore_wait(barrier, expected)

    tile_plan = []
    for dx, dy in around:
        slot = ((1 - dx) * 3 + (1 - dy)) * 8
        tile_plan.append((cpad, tiles.at[pl.ds(slot, 8)], (dx, dy)))
    tile_exchange = Exchange(tile_plan, lambda j: tsend_sem.at[j], lambda j: trecv_sem.at[j])
    tile_exchange.start()
    fine(0).start()
    tiles[32:40] = cpad[...]

    for c in copies:
        c.wait()

    def spread(x):
        h1 = x.astype(BF16)
        r1 = x - h1.astype(F32)
        h2 = r1.astype(BF16)
        return [h1, h2, (r1 - h2.astype(F32)).astype(BF16)]

    spread_own = dot(jnp.concatenate(spread(cpad[...]), 1), const["Bs"][...])
    for e in range(EX):
        lines = [spread_own[e * EY + ey : e * EY + ey + 1] for ey in range(EY)]
        cf = [jnp.broadcast_to(l[:, :ZF], (N, ZF)) for l in lines]
        one = jnp.concatenate(cf, 0)
        Cr[e] = jnp.concatenate([one] * N, 0)
        FXr[0, e * YF : (e + 1) * YF] = one
        FXr[0, 2 * YF + e * N : 2 * YF + (e + 1) * N] = cf[0]
        FXr[0, 2 * YF + (EX + e) * N : 2 * YF + (EX + e + 1) * N] = cf[EY - 1]

    rows = lax.broadcasted_iota(jnp.int32, (ROWS, ZF), 0)
    lanes = lax.broadcasted_iota(jnp.int32, (ROWS, ZF), 1)
    xr, yr = rows // YF, lax.rem(rows, YF)
    frow = lax.broadcasted_iota(jnp.int32, (96, ZF), 0)
    flane = lax.broadcasted_iota(jnp.int32, (96, ZF), 1)
    fx = jnp.where(frow < YF, 0, jnp.where(frow < 2 * YF, XF - 1, lax.rem(frow, XF)))
    fy = jnp.where(frow < 2 * YF, lax.rem(frow, YF), jnp.where(frow < 2 * YF + XF, 0, YF - 1))

    def edge(i, count=0):
        e = (lax.rem(i, N) == 0) | (lax.rem(i, N) == N - 1)
        return jnp.where(e & (i != 0) & (i != count - 1) if count else e, 0.5, 1.0)

    Wr[...] = edge(lanes) * edge(yr) * edge(xr)
    WLr[...] = edge(lanes) * edge(yr, YF)
    WFr[...] = edge(flane) * edge(fx) * edge(fy)
    WLFr[...] = edge(flane) * edge(fx, XF) * edge(fy, YF)

    tile_exchange.arrive()
    ext = tiles[...]
    pd = rmul(ext, const["Bdf"], HOW["g"])
    diag = lmul(const["Gdf"], pd[:, :ZF], pd[:, ZF:], n=HOW["g"])

    def mask_of(x, y, z, n):
        inner = (x > 0) & (x < gxn * EX * n - 1) & (y > 0) & (y < gyn * EY * n - 1)
        return inner & (z != 0) & (z != EZ * n - 1)

    for e in range(EX):
        keep = mask_of(px * XF + e * N + xr, py * YF + yr, lanes, N)
        Dr[e] = jnp.where(keep, 1.0 / diag[e * ROWS : (e + 1) * ROWS], 0.0)
    keep = mask_of(px * XF + fx, py * YF + fy, flane, N)
    df = jnp.where(keep, 1.0 / diag[EX * ROWS :], 0.0)
    DFr[...] = df
    DcFr[...] = df * FXr[0]
    pdc = rmul(ext, const["Bdc"], HOW["g"])
    diag_c = lmul(const["Gdc"], pdc[:, :ZC], pdc[:, ZC:], n=HOW["g"])
    crow = lax.broadcasted_iota(jnp.int32, (384, ZC), 0)
    clane = lax.broadcasted_iota(jnp.int32, (384, ZC), 1)

    def place(r, width, x0, y0):
        return (x0 + r // width, y0 + lax.rem(r, width))

    cx, cy = place(crow, YC, 0, 0)
    base = OWN
    for count, width, x0, y0 in (
        (ROWS_C, YC, -NC, 0), (ROWS_C, YC, XC, 0), (XC * NC, NC, 0, -NC), (XC * NC, NC, 0, YC),
        (16, NC, -NC, -NC), (16, NC, -NC, YC), (16, NC, XC, -NC), (16, NC, XC, YC),
    ):
        nx, ny = place(crow - base, width, x0, y0)
        cx, cy = jnp.where(crow >= base, nx, cx), jnp.where(crow >= base, ny, cy)
        base += count
    keep = mask_of(px * XC + cx, py * YC + cy, clane, NC)
    Dc_r[...] = jnp.where(keep, 1.0 / diag_c, 0.0)
    lines = dot(jnp.concatenate(spread(ext), 1), const["Bs"][:, ZF:])
    Cc_r[...] = dot(const["Pc"][...], jnp.concatenate(spread(lines), 0))

    def halo(i):
        fine(i).arrive()
        return jnp.concatenate([rx[i, 0], rx[i, 1], ry[i, 0] + rc[i, 0], ry[i, 1] + rc[i, 1]], 0)

    def add_faces(ref, index, h):
        ref[(*index, 0, pl.ds(0, YF))] += h[0:YF]
        ref[(*index, 1, pl.ds(ROWS - YF, YF))] += h[YF : 2 * YF]
        for x in range(XF):
            e, r = x // N, (x % N) * YF
            ref[(*index, e, pl.ds(r, 1))] += h[2 * YF + x : 2 * YF + x + 1]
            b = 2 * YF + XF + x
            ref[(*index, e, pl.ds(r + YF - 1, 1))] += h[b : b + 1]

    def bulk(values, n):
        y0 = None
        for e in range(EX):
            p = rmul(values(e), const["Bf"], n)
            o = lmul(const[f"Gb{e}"], p[:, :ZF], p[:, ZF:], n=n)
            Lr[e] = o[:ROWS]
            FXr[1, e * YF : (e + 1) * YF] = o[ROWS : ROWS + YF]
            y0 = o[ROWS + YF :] if e == 0 else y0 + o[ROWS + YF :]
        FXr[1, 2 * YF :] = y0

    def face_z(hs, n):
        return rmul(hs, const["Bf"], n)

    def send_faces(i, faces):
        sx[i, 0] = faces[0:YF]
        sx[i, 1] = faces[YF : 2 * YF]
        sy[i, 0] = faces[2 * YF : 2 * YF + XF]
        sy[i, 1] = faces[2 * YF + XF :]
        fine(i).start()

    def face_to_face(ph, n):
        return lmul(const["F2F"], ph[:, :ZF], ph[:, ZF:], n=n)

    def face_to_all(ph, n):
        for e in range(EX):
            part = jnp.concatenate([ph[e * YF : (e + 1) * YF], ph[2 * YF :]], 0)
            Lr[e] += lmul(const[f"F2A{e}"], part[:, :ZF], part[:, ZF:], n=n)
        middle(Lr)

    def finish(k):
        add_faces(Zr, (k,), (-k_f) * DFr[...] * Hr[...])
        face_to_all(PHr[...], HOW["h"])
        for e in range(EX):
            Fr[k + 1, e] = Lr[e]

    def total(x):
        x = jnp.sum(x, axis=0, keepdims=True)
        return x[:, : ZF // 2] + x[:, ZF // 2 :]

    def cycle(k, carry):
        pl.when(k > 0)(lambda: finish(k - 1))
        bulk(lambda e: Cr[e] * (Dr[e] * inv_center) * Fr[k, e], HOW["a"])
        h = halo(4 * k)
        ph = face_z(DcFr[...] * inv_center * h, HOW["a"])
        send_faces(4 * k + 1, FXr[1] + face_to_face(ph, HOW["a"]))
        add_faces(Fr, (k,), h)
        FFr[k, 0:YF] = Fr[k, 0, 0:YF]
        FFr[k, YF : 2 * YF] = Fr[k, 1, ROWS - YF : ROWS]
        for x in range(XF):
            e, r = x // N, (x % N) * YF
            FFr[k, 2 * YF + x : 2 * YF + x + 1] = Fr[k, e, r : r + 1]
            b = 2 * YF + XF + x
            FFr[k, b : b + 1] = Fr[k, e, r + YF - 1 : r + YF]
        face_to_all(ph, HOW["a"])
        gl = None
        for e in range(EX):
            s = Dr[e] * (a_f * Fr[k, e] - k_f * Lr[e])
            Sr[e] = s
            p = rmul(Cr[e] * s, const["Br"], HOW["b"])
            Ar[e, :, 0:ZC] = rmul(Fr[k, e], const["Bw"], HOW["b"])
            o = lmul(const[f"Gr{e}"], p[:, :ZC], p[:, ZC:], n=HOW["b"])
            gl = o if e == 0 else gl + o
        gl = lmul(const["Gw"], Ar[0, :, 0:ZC], Ar[1, :, 0:ZC], n=HOW["b"]) - gl
        h = halo(4 * k + 1)
        hs = (-k_f) * DcFr[...] * h
        pr = rmul(hs, const["Br"], HOW["b"])
        gl = gl - lmul(const["F2R"], pr[:, :ZC], pr[:, ZC:], n=HOW["b"])
        cs[k] = gl
        coarse(k).start()
        bulk(lambda e: Cr[e] * Sr[e], HOW["s"])
        ph = face_z(hs, HOW["s"])
        face_to_all(ph, HOW["s"])
        FXr[1] = FXr[1] + face_to_face(ph, HOW["s"])
        add_faces(Sr, (), (-k_f) * DFr[...] * h)
        coarse(k).arrive()
        g1, g2 = split(jnp.concatenate([cs[k, 0:OWN], cr[k]], 0), 3)
        g = dot(const["T"][...], jnp.concatenate([g1, g2], 0))
        p = rmul(Cc_r[...] * (Dc_r[...] * inv_center_c) * g, const["Bc"], HOW["c"])
        o = lmul(const["Gc"], p[:, :ZC], p[:, ZC:], n=HOW["c"])
        fix = Dc_r[0:OWN] * (a_c * g[0:OWN] - k_c * o)
        p = rmul(Cc_r[0:OWN] * fix, const["Bj"], HOW["d"], slice(0, 2 * ZF))
        o = lmul(const["Gj"], p[:, :ZF], p[:, ZF:], n=HOW["d"], rows=slice(EX * ROWS, EX * ROWS + 96))
        send_faces(4 * k + 2, FXr[1] + o)
        o = lmul(const["Gj"], p[:, :ZF], p[:, ZF:], n=HOW["d"], rows=slice(0, EX * ROWS))
        p = rmul(fix, const["Bj"], HOW["d"], slice(2 * ZF, 3 * ZF))
        up = lmul(const["Gp"], p, n=HOW["d"])
        for e in range(EX):
            part = slice(e * ROWS, (e + 1) * ROWS)
            Sr[e] = Sr[e] + up[part]
            Rr[e] = Fr[k, e] - Lr[e] - o[part]
        bulk(lambda e: Cr[e] * (Dr[e] * inv_center) * Rr[e], HOW["e"])
        h = halo(4 * k + 2)
        ph = face_z((-inv_center) * DcFr[...] * h, HOW["e"])
        send_faces(4 * k + 3, FXr[1] + face_to_face(ph, HOW["e"]))
        add_faces(Rr, (), -h)
        face_to_all(ph, HOW["e"])
        for e in range(EX):
            Zr[k, e] = Sr[e] + Dr[e] * (a_f * Rr[e] - k_f * Lr[e])
        bulk(lambda e: Cr[e] * Zr[k, e], HOW["f"])
        sums = [0.0] * 3
        for e in range(EX):
            z = Zr[k, e]
            wz = Wr[...] * z
            for i, t in enumerate((Fr[0, e] * wz, Fr[k, e] * wz, WLr[...] * Lr[e] * z)):
                sums[i] = sums[i] + total(t)
        h = halo(4 * k + 3)
        delta = (-k_f) * DFr[...] * h
        ph = face_z((-k_f) * DcFr[...] * h, HOW["h"])
        ff = face_to_face(ph, HOW["h"])
        send_faces(4 * k + 4, FXr[1] + ff)
        wd = WFr[...] * delta
        faces = (FFr[0] * wd, FFr[k] * wd, WLFr[...] * delta * (2.0 * FXr[1] + ff))
        for i, t in enumerate(faces):
            dots[k, i : i + 1] = sums[i] + total(t)
        PHr[...] = ph
        Hr[...] = h
        return carry

    lax.fori_loop(0, 2, cycle, 0)

    def reduce_stage(buf, stage, base):
        return [
            pltpu.make_async_remote_copy(
                src_ref=buf.at[0], dst_ref=buf.at[j + 1], send_sem=dsend_sem.at[base + j], recv_sem=drecv_sem.at[base + j],
                device_id=p, device_id_type=MESH,
            )
            for j, p in enumerate(stage)
        ]

    def summed(buf, stage, n):
        for c in stage:
            c.wait_recv()
        out = buf[0]
        for j in range(n):
            out = out + buf[j + 1]
        return out

    d1[0, 0:3] = dots[0, 0:3]
    d1[0, 3:6] = dots[1, 0:3]
    d1[0, 6:8] = jnp.zeros((2, 128), F32)
    stage1 = reduce_stage(d1, stages[0], 0)
    stage2 = reduce_stage(d2, stages[1], len(stage1))
    for c in stage1:
        c.start()
    finish(1)
    d2[0] = summed(d1, stage1, len(stage1))
    for c in stage2:
        c.start()
    h = halo(8)
    add_faces(Fr, (2,), h)
    lanes_sum = jnp.sum(summed(d2, stage2, len(stage2)), axis=1, keepdims=True)
    pick = lambda i: lanes_sum[i : i + 1, 0:1]
    rz0, c00 = pick(1), pick(2)
    r0u, wu, uv = pick(3), pick(4), pick(5)
    alpha0 = rz0 / c00
    rz1 = alpha0 * (alpha0 * wu - r0u)
    beta1 = 1.0 + rz1 / rz0
    curve = beta1 * beta1 * c00 - 2.0 * beta1 * alpha0 * wu + alpha0 * alpha0 * uv
    alpha1 = rz1 / curve
    c_z = alpha0 + alpha1 * beta1
    c_u = alpha1 * alpha0
    for e in range(EX):
        sol_ref[e] = c_z * Zr[0, e] - c_u * Zr[1, e]
        res_ref[e] = jnp.where(Dr[e] > 0.0, Fr[0, e] - c_z * Fr[1, e] + c_u * Fr[2, e], 0.0)

    tile_exchange.drain()
    for c in stage1 + stage2:
        c.wait_send()

    def drain(i, carry):
        fine(i).drain()
        return carry

    lax.fori_loop(0, 9, drain, 0)
    for k in range(2):
        coarse(k).drain()


def solution(mesh):
    gxn, gyn = mesh.shape["gx"], mesh.shape["gy"]
    table = constants()
    names = tuple(table)
    n_dots = gyn - 1 + gxn - 1

    def per_device(right_side, coefficient):
        rhs = right_side.reshape(EX, ROWS, ZF)
        field = (EX, ROWS, ZF)
        vm = lambda *s: pltpu.VMEM(s, F32)
        dma = lambda *s: pltpu.SemaphoreType.DMA(s)
        face = (96, ZF)
        scratch = [pltpu.VMEM(table[m].shape, BF16) for m in names]
        scratch += [
            vm(3, *field), vm(2, *field), vm(*field), vm(*field), vm(*face), vm(*face),
            vm(*field), vm(*field), vm(*field), vm(*field), vm(2, *face), vm(2, *face), vm(96, 2 * ZF), vm(*face),
            vm(ROWS, ZF), vm(ROWS, ZF), vm(*face), vm(*face),
            vm(384, ZC), vm(384, ZC), vm(8, 128), vm(80, 128),
            vm(9, 2, YF, ZF), vm(9, 2, EX * N, ZF), vm(9, 2, YF, ZF), vm(9, 2, EX * N, ZF), vm(9, 2, EX * N, ZF),
            vm(2, 192, ZC), vm(2, 256, ZC),
            vm(2, 8, 128), vm(gyn, 8, 128), vm(gxn, 8, 128),
            dma(len(names)), dma(9, 8), dma(9, 8), dma(2, 8), dma(2, 8), dma(8), dma(8), dma(n_dots), dma(n_dots),
        ]
        sol, res = pl.pallas_call(
            functools.partial(kernel_body, (gxn, gyn), names),
            out_shape=[jax.ShapeDtypeStruct(field, F32)] * 2,
            in_specs=[pl.BlockSpec(memory_space=pltpu.VMEM)] * 2 + [pl.BlockSpec(memory_space=pl.ANY)] * len(names),
            out_specs=[pl.BlockSpec(memory_space=pltpu.VMEM)] * 2,
            scratch_shapes=scratch,
            compiler_params=pltpu.CompilerParams(
                collective_id=0, has_side_effects=True, vmem_limit_bytes=56 * 2**20
            ),
        )(rhs, coefficient, *[jnp.asarray(table[m]) for m in names])
        return sol.reshape(right_side.shape), res.reshape(right_side.shape)

    spec = P("gx", "gy", None)
    return jax.shard_map(
        per_device, mesh=mesh, in_specs=(spec, spec), out_specs=(spec, spec), check_vma=False
    )
```

```python
import functools
import math

import jax
import jax.numpy as jnp
import numpy as np
from jax import lax
from jax.experimental import pallas as pl
from jax.experimental.pallas import tpu as pltpu
from jax.sharding import PartitionSpec as P

ORDER = 7
COARSE_ORDER = 3
F32 = jnp.float32
BF16 = jnp.bfloat16
MESH = pl.DeviceIdType.MESH

EX, EY, EZ = 2, 4, 32
N, NC = ORDER + 1, COARSE_ORDER + 1
YF, ZF = EY * N, EZ * N
YC, ZC = EY * NC, EZ * NC
ROWS = N * YF
ROWS_C = NC * YC


def legendre_pair(degree, points):
    before = points * 0.0 + 1.0
    now = points.copy()
    for power in range(2, degree + 1):
        after = ((2 * power - 1) * points * now - (power - 1) * before) / power
        before = now
        now = after
    return (now, before)


def gll_tables(degree):
    number = degree + 1
    points = np.cos(math.pi * np.arange(number) / degree)
    for newton in range(60):
        top, below = legendre_pair(degree, points)
        points = points - (points * top - below) / (number * top)
    points = points[::-1].copy()
    points[0] = -1.0
    points[degree] = 1.0
    values = legendre_pair(degree, points)[0]
    weights = 2.0 / (degree * (degree + 1) * values**2)
    derivative = np.zeros((number, number))
    for row_index in range(number):
        for column_index in range(number):
            if row_index != column_index:
                derivative[row_index, column_index] = values[row_index] / (
                    values[column_index] * (points[row_index] - points[column_index])
                )
    derivative[0, 0] = -degree * (degree + 1) / 4.0
    derivative[degree, degree] = degree * (degree + 1) / 4.0
    stiffness = derivative.T @ (weights[:, None] * derivative)
    return (points, weights, stiffness)


def upper_bound(degree):
    points, weights, stiffness = gll_tables(degree)
    rowsum = np.abs(stiffness).sum(1)
    diagonal = np.diag(stiffness)
    outer = lambda a, b, c: a[:, None, None] * b[None, :, None] * c[None, None, :]
    top = outer(rowsum, weights, weights) + outer(weights, rowsum, weights) + outer(weights, weights, rowsum)
    bottom = outer(diagonal, weights, weights) + outer(weights, diagonal, weights) + outer(weights, weights, diagonal)
    return float((top / bottom).max())


def interpolation_matrix(fine_degree, coarse_degree):
    fine_points = gll_tables(fine_degree)[0]
    coarse_points = gll_tables(coarse_degree)[0]
    matrix = np.ones((fine_degree + 1, coarse_degree + 1))
    for column_index in range(coarse_degree + 1):
        for other_index in range(coarse_degree + 1):
            if other_index != column_index:
                matrix[:, column_index] *= (fine_points - coarse_points[other_index]) / (
                    coarse_points[column_index] - coarse_points[other_index]
                )
    return matrix


def cheb_numbers(degree):
    upper = upper_bound(degree)
    lower = 0.1 * upper
    center = 0.5 * (upper + lower)
    half = 0.5 * (upper - lower)
    previous = half / center
    current = 1.0 / (2.0 * center / half - previous)
    k = 2.0 * current / half
    return (1.0 / center, (1.0 + current * previous) / center + k, k)


def sum_matrix(elements, number):
    matrix = np.eye(elements * number)
    for e in range(elements - 1):
        a, b = e * number + number - 1, (e + 1) * number
        matrix[a, b] = matrix[b, a] = 1.0
    return matrix


def blocks(count, matrix):
    return np.kron(np.eye(count), matrix)


TERMS = ((0, 0), (1, 0), (0, 1), (2, 0), (0, 2), (1, 1))
HOW = dict(a=3, b=3, s=6, c=3, d=6, e=3, f=6, g=3, h=3)


def pieces_of(matrix, count):
    rest, out = np.asarray(matrix, np.float64), []
    for _ in range(count):
        out.append(rest.astype(np.float32).astype(BF16))
        rest = rest - out[-1].astype(np.float64)
    return out


def right3(matrix, steps="asef"):
    p = pieces_of(matrix, 3)
    return np.concatenate([p[j] for _, j in TERMS[: max(HOW[t] for t in steps)]], 0)


def left3(matrix, steps="asef"):
    p = pieces_of(matrix, 3)
    return np.concatenate([p[j] for _, j in TERMS[: max(HOW[t] for t in steps)]], 1)


def level_matrices(degree):
    _, w, K = gll_tables(degree)
    n = degree + 1
    wy = np.tile(w, EY)
    M0 = np.kron(K, np.diag(wy)) + np.kron(np.diag(w), blocks(EY, K))
    N0 = np.kron(np.diag(w), np.diag(wy))
    return M0, N0, np.diag(np.tile(w, EZ)), blocks(EZ, K)


def face_rows(n):
    y = EY * n
    x = EX * n
    rows = [j for j in range(y)] + [(x - 1) * y + j for j in range(y)]
    rows += [i * y for i in range(x)] + [i * y + y - 1 for i in range(x)]
    return np.array(rows)


def coarse_places():
    XC = EX * NC
    before, after_x, after_y = range(-NC, 0), range(XC, XC + NC), range(YC, YC + NC)
    grids = [(range(XC), range(YC)), (before, range(YC)), (after_x, range(YC)), (range(XC), before), (range(XC), after_y)]
    grids += [(a, b) for a in (before, after_x) for b in (before, after_y)]
    both = [(x, y) for xs, ys in grids for x in xs for y in ys]
    return np.array([p[0] for p in both]), np.array([p[1] for p in both])


def coarse_pairs():
    x, y = coarse_places()
    row = {p: i for i, p in enumerate(zip(x.tolist(), y.tolist()))}
    XC, out = EX * NC, []
    for a, b in ((-1, 0), (XC - 1, XC)):
        for first, n in ((-NC, NC), (0, YC), (YC, NC)):
            out.append((row[a, first], row[b, first], n))
    for a, b in ((-1, 0), (YC - 1, YC)):
        out += [(row[i, a], row[i, b], 1) for i in range(-NC, XC + NC)]
    return out


@functools.cache
def constants():
    J = interpolation_matrix(ORDER, COARSE_ORDER)
    out = {}
    M0, N0, Wz, Kz = level_matrices(ORDER)
    Sz, Szc = sum_matrix(EZ, N), sum_matrix(EZ, NC)
    Sxy = np.kron(sum_matrix(EX, N), sum_matrix(EY, N))
    Sxyc = np.kron(sum_matrix(EX, NC), sum_matrix(EY, NC))
    Mf, Nf = blocks(EX, M0), blocks(EX, N0)
    SM, SN = Sxy @ Mf, Sxy @ Nf
    F = face_rows(N)
    out["Bf"] = right3(np.concatenate([Wz @ Sz, Kz @ Sz], 1))
    _, w, K = gll_tables(ORDER)
    wxy, wz = np.kron(w, np.tile(w, EY)), np.tile(w, EZ)
    out["Mh"] = left3(M0 / wxy[:, None])
    out["Kh"] = right3(Kz / wz[None, :])
    out["w3"] = (wxy[:, None] * wz[None, :]).astype(np.float32)
    y, z = np.arange(ROWS) % YF, np.arange(ZF)
    wide = lambda m, shape: np.broadcast_to(m, shape).astype(np.float32)
    out["yu"] = wide(((y % N == N - 1) & (y != YF - 1))[:, None], (ROWS, 128))
    out["yd"] = wide(((y % N == 0) & (y != 0))[:, None], (ROWS, 128))
    out["zu"] = wide(((z % N == N - 1) & (z != ZF - 1))[None, :], (8, ZF))
    out["zd"] = wide(((z % N == 0) & (z != 0))[None, :], (8, ZF))
    Sy = np.kron(np.eye(EX * N), sum_matrix(EY, N))
    out["F2F"] = left3(np.concatenate([SM[F][:, F], SN[F][:, F]], 1))
    for e in range(EX):
        rows = slice(e * ROWS, (e + 1) * ROWS)
        here = np.concatenate([np.arange(e * YF, (e + 1) * YF), np.arange(2 * YF, len(F))])
        keep = ((F[here] // ROWS) == e).astype(float)[None, :]
        full = np.concatenate([(Sy @ Mf)[rows][:, F[here]] * keep, (Sy @ Nf)[rows][:, F[here]] * keep], 1)
        out[f"F2A{e}"] = left3(full)
    Rxy = blocks(EX, np.kron(J.T, blocks(EY, J.T)))
    JZ = blocks(EZ, J)
    XC = EX * NC
    first = [x * YC + y for x in range(XC) for y in range(NC)]
    last = [x * YC + YC - NC + y for x in range(XC) for y in range(NC)]
    selc = np.concatenate([np.arange(XC * YC), first, last]).astype(int)
    RM, RN = (Sxyc @ Rxy @ Mf)[selc], (Sxyc @ Rxy @ Nf)[selc]
    out["Br"] = right3(np.concatenate([Wz @ JZ @ Szc, Kz @ JZ @ Szc], 1), "b")
    for e in range(EX):
        cols = slice(e * ROWS, (e + 1) * ROWS)
        out[f"Gr{e}"] = left3(np.concatenate([RM[:, cols], RN[:, cols]], 1), "b")
    out["F2R"] = left3(np.concatenate([RM[:, F], RN[:, F]], 1), "b")
    inv = lambda count: np.where((np.arange(count) % N == 0) | (np.arange(count) % N == N - 1), 0.5, 1.0)
    Wxy = np.kron(np.diag(inv(EX * N)), np.diag(inv(YF)))
    RW = (Sxyc @ Rxy @ Wxy)[selc]
    out["Bw"] = right3(np.diag(inv(ZF)) @ JZ @ Szc, "b")
    out["Gw"] = left3(RW, "b")
    _, wc, Kc = gll_tables(COARSE_ORDER)
    Wzc, Kzc = np.diag(np.tile(wc, EZ)), blocks(EZ, Kc)
    out["Bc"] = right3(np.concatenate([Wzc @ Szc, Kzc @ Szc], 0), "c")
    cx, cy = coarse_places()
    grid = (cx + NC) * (YC + 2 * NC) + cy + NC
    wx4, wy6 = np.diag(np.tile(wc, EX + 2)), np.diag(np.tile(wc, EY + 2))
    Me = np.kron(blocks(EX + 2, Kc), wy6) + np.kron(wx4, blocks(EY + 2, Kc))
    Ne = np.kron(wx4, wy6)
    Se = np.kron(sum_matrix(EX + 2, NC), sum_matrix(EY + 2, NC))
    own = grid[: XC * YC]
    out["Gc"] = left3(np.concatenate([(Se @ Me)[own][:, grid], (Se @ Ne)[own][:, grid]], 0), "c")
    pick = np.zeros((len(cx), 80))
    for i, (x, y) in enumerate(zip(cx // NC, cy // NC)):
        pick[i, ((x // EX + 1) * 3 + y // EY + 1) * 8 + (x % EX) * EY + y % EY] = 1.0
    out["Pc"] = np.concatenate([pick.astype(np.float32).astype(BF16)] * 3, 1)
    Jxy = blocks(EX, np.kron(J, blocks(EY, J)))
    out["Bj"] = right3(np.concatenate([JZ.T @ Wz @ Sz, JZ.T @ Kz @ Sz, JZ.T], 1), "d")
    sel = np.concatenate([np.arange(EX * ROWS), F])
    JM, JN = (SM @ Jxy)[sel], (SN @ Jxy)[sel]
    out["Gj"] = left3(np.concatenate([JM, JN], 1), "d")
    out["Gp"] = left3(Jxy, "d")
    fine_x, fine_y = np.divmod(np.arange(EX * ROWS), YF)
    places = {"f": (np.concatenate([fine_x, F // YF]), np.concatenate([fine_y, F % YF])), "c": (cx, cy)}
    for name, degree in (("f", ORDER), ("c", COARSE_ORDER)):
        n = degree + 1
        _, w, K = gll_tables(degree)
        kd = np.diag(K)
        S = sum_matrix(EZ, n)
        spread_w = np.zeros((128, EZ * n))
        spread_k = np.zeros((128, EZ * n))
        for ez in range(EZ):
            spread_w[ez, ez * n : (ez + 1) * n] = w
            spread_k[ez, ez * n : (ez + 1) * n] = kd
        out["Bd" + name] = right3(np.concatenate([spread_w @ S, spread_k @ S], 1), "g")
        left = np.zeros((len(places[name][0]), 2, 80))
        for i, (x, y) in enumerate(zip(*places[name])):
            xs = [(x // n, x % n)]
            if x % n == 0:
                xs.append((x // n - 1, n - 1))
            if x % n == n - 1:
                xs.append((x // n + 1, 0))
            ys = [(y // n, y % n)]
            if y % n == 0:
                ys.append((y // n - 1, n - 1))
            if y % n == n - 1:
                ys.append((y // n + 1, 0))
            for ex, a in xs:
                for ey, b in ys:
                    col = ((ex // EX + 1) * 3 + ey // EY + 1) * 8 + (ex % EX) * EY + ey % EY
                    left[i, 0, col] += kd[a] * w[b] + w[a] * kd[b]
                    left[i, 1, col] += w[a] * w[b]
        left = left.reshape(len(left), 160)
        out["Gd" + name] = left3(left, "g")
    spread = np.zeros((128, ZF + ZC))
    for ez in range(EZ):
        spread[ez, ez * N : (ez + 1) * N] = 1.0
        spread[ez, ZF + ez * NC : ZF + (ez + 1) * NC] = 1.0
    out["Bs"] = np.concatenate([spread.astype(np.float32).astype(BF16)] * 3, 0)
    return out


def dot(a, b):
    return jnp.dot(a, b, preferred_element_type=F32)


def split(x, n):
    out = []
    for i in range(1 + max(i for i, _ in TERMS[:n])):
        out.append(x.astype(BF16))
        x = x - out[-1].astype(F32)
    return out


def rmul(x, b, n, cols=slice(None)):
    p = split(x, n)
    x3 = jnp.concatenate([p[i] for i, _ in TERMS[:n]], 1)
    return dot(x3, b[: x3.shape[1], cols])


def lmul(g, *parts, n, rows=slice(None)):
    split_parts = [split(x, n) for x in parts]
    x3 = jnp.concatenate([p[i] for i, _ in TERMS[:n] for p in split_parts], 0)
    return dot(g[rows, : x3.shape[0]], x3)


def kernel_body(shape, names, rhs_ref, coef_ref, *refs):
    gxn, gyn = shape
    n_const = len(names)
    const_hbm = dict(zip(names, refs[:n_const]))
    sol_ref, res_ref = refs[n_const : n_const + 2]
    rest = refs[n_const + 2 :]
    const = dict(zip(names, rest[:n_const]))
    (Fr, Zr, Dr, Cr, W3r, gr, DFr, DcFr, Lr, Sr, Rr, Ar, FXr, FFr, PHr, Hr, Wr, WLr, WFr, WLFr,
     Dc_r, Cc_r, cpad, tiles,
     sx, sy, rx, ry, rc, cs, cr, dots, d1, d2,
     const_sem, send_sem, recv_sem, csend_sem, crecv_sem, tsend_sem, trecv_sem, dsend_sem, drecv_sem) = rest[n_const:]

    inv_center, a_f, k_f = cheb_numbers(ORDER)
    inv_center_c, a_c, k_c = cheb_numbers(COARSE_ORDER)
    px, py = lax.axis_index("gx"), lax.axis_index("gy")
    XF, XC, OWN = EX * N, EX * NC, EX * ROWS_C

    def at(dx, dy):
        return (lax.rem(px + dx + gxn, gxn), lax.rem(py + dy + gyn, gyn))

    def inside(dx, dy):
        ok = None
        for p, d, n in ((px, dx, gxn), (py, dy, gyn)):
            if d:
                here = (p > 0) if d < 0 else (p < n - 1)
                ok = here if ok is None else ok & here
        return ok

    corners = [(dx, dy) for dx in (-1, 1) for dy in (-1, 1)]
    around = corners + [(-1, 0), (1, 0), (0, -1), (0, 1)]
    stages = [
        [(px, lax.rem(py + d, gyn)) for d in range(1, gyn)],
        [(lax.rem(px + d, gxn), py) for d in range(1, gxn)],
    ]

    copies = [pltpu.make_async_copy(const_hbm[m], const[m], const_sem.at[i]) for i, m in enumerate(names)]
    for c in copies:
        c.start()

    for ref in (rx, ry, rc, cr, tiles, cpad):
        ref[...] = jnp.zeros_like(ref)
    cpad[0:EY, 0:EZ] = coef_ref[0]
    cpad[EY : 2 * EY, 0:EZ] = coef_ref[1]

    barrier = pltpu.get_barrier_semaphore()
    expected = 0
    for d in around:
        pl.when(inside(*d))(
            lambda d=d: pl.semaphore_signal(barrier, inc=1, device_id=at(*d), device_id_type=MESH)
        )
        expected = expected + inside(*d).astype(jnp.int32)
    for stage in stages:
        for p in stage:
            pl.semaphore_signal(barrier, inc=1, device_id=p, device_id_type=MESH)
        expected = expected + len(stage)

    def local_sum(v):
        rows = lax.broadcasted_iota(jnp.int32, v.shape, 0)
        lanes = lax.broadcasted_iota(jnp.int32, v.shape, 1)
        y = lax.rem(rows, YF)
        up = (lax.rem(y, N) == N - 1) & (y != YF - 1)
        down = (lax.rem(y, N) == 0) & (y != 0)
        v = v + jnp.where(up, pltpu.roll(v, ROWS - 1, 0), 0.0) + jnp.where(down, pltpu.roll(v, 1, 0), 0.0)
        up = (lax.rem(lanes, N) == N - 1) & (lanes != ZF - 1)
        down = (lax.rem(lanes, N) == 0) & (lanes != 0)
        return v + jnp.where(up, pltpu.roll(v, ZF - 1, 1), 0.0) + jnp.where(down, pltpu.roll(v, 1, 1), 0.0)

    def middle(ref, *index):
        total = ref[(*index, 0, pl.ds(ROWS - YF, YF))] + ref[(*index, 1, pl.ds(0, YF))]
        ref[(*index, 0, pl.ds(ROWS - YF, YF))] = total
        ref[(*index, 1, pl.ds(0, YF))] = total

    for e in range(EX):
        Fr[0, e] = local_sum(rhs_ref[e])
    middle(Fr, 0)
    sx[0, 0] = Fr[0, 0, 0:YF]
    sx[0, 1] = Fr[0, 1, ROWS - YF : ROWS]
    for x in range(XF):
        e, r = x // N, (x % N) * YF
        sy[0, 0, x : x + 1] = Fr[0, e, r : r + 1]
        sy[0, 1, x : x + 1] = Fr[0, e, r + YF - 1 : r + YF]

    class Exchange:
        def __init__(self, plan, send, recv):
            self.plan = [
                (pltpu.make_async_remote_copy(
                    src_ref=s, dst_ref=t, send_sem=send(j), recv_sem=recv(j), device_id=at(*d), device_id_type=MESH,
                ), inside(*d), inside(-d[0], -d[1]))
                for j, (s, t, d) in enumerate(plan)
            ]

        def start(self):
            for c, to, _ in self.plan:
                pl.when(to)(c.start)

        def arrive(self):
            for c, _, come in self.plan:
                pl.when(come)(c.wait_recv)

        def drain(self):
            for c, to, _ in self.plan:
                pl.when(to)(c.wait_send)

    def fine(i):
        one = lambda r: pl.ds(r, 1)
        plan = [
            (sy.at[i, 0, one(0)], rc.at[i, 1, one(XF - 1)], (-1, -1)),
            (sy.at[i, 1, one(0)], rc.at[i, 0, one(XF - 1)], (-1, 1)),
            (sy.at[i, 0, one(XF - 1)], rc.at[i, 1, one(0)], (1, -1)),
            (sy.at[i, 1, one(XF - 1)], rc.at[i, 0, one(0)], (1, 1)),
            (sx.at[i, 0], rx.at[i, 1], (-1, 0)),
            (sx.at[i, 1], rx.at[i, 0], (1, 0)),
            (sy.at[i, 0], ry.at[i, 1], (0, -1)),
            (sy.at[i, 1], ry.at[i, 0], (0, 1)),
        ]
        return Exchange(plan, lambda j: send_sem.at[i, j], lambda j: recv_sem.at[i, j])

    def coarse(k):
        h, q = ROWS_C, NC * NC
        y0, y1 = OWN, OWN + XC * NC
        c0 = 2 * h + 4 * q
        src = lambda a, n: cs.at[k, pl.ds(a, n)]
        dst = lambda a, n: cr.at[k, pl.ds(a, n)]
        plan = [
            (src(y0, q), dst(c0 + 3 * q, q), (-1, -1)),
            (src(y1, q), dst(c0 + 2 * q, q), (-1, 1)),
            (src(y0 + q, q), dst(c0 + q, q), (1, -1)),
            (src(y1 + q, q), dst(c0, q), (1, 1)),
            (src(0, h), dst(h, h), (-1, 0)),
            (src(h, h), dst(0, h), (1, 0)),
            (src(y0, 2 * q), dst(2 * h + 2 * q, 2 * q), (0, -1)),
            (src(y1, 2 * q), dst(2 * h, 2 * q), (0, 1)),
        ]
        return Exchange(plan, lambda j: csend_sem.at[k, j], lambda j: crecv_sem.at[k, j])

    pl.semaphore_wait(barrier, expected)

    tile_plan = []
    for dx, dy in around:
        slot = ((1 - dx) * 3 + (1 - dy)) * 8
        tile_plan.append((cpad, tiles.at[pl.ds(slot, 8)], (dx, dy)))
    tile_exchange = Exchange(tile_plan, lambda j: tsend_sem.at[j], lambda j: trecv_sem.at[j])
    tile_exchange.start()
    fine(0).start()
    tiles[32:40] = cpad[...]

    for c in copies:
        c.wait()

    def spread(x):
        h1 = x.astype(BF16)
        r1 = x - h1.astype(F32)
        h2 = r1.astype(BF16)
        return [h1, h2, (r1 - h2.astype(F32)).astype(BF16)]

    spread_own = dot(jnp.concatenate(spread(cpad[...]), 1), const["Bs"][...])
    for e in range(EX):
        lines = [spread_own[e * EY + ey : e * EY + ey + 1] for ey in range(EY)]
        cf = [jnp.broadcast_to(l[:, :ZF], (N, ZF)) for l in lines]
        one = jnp.concatenate(cf, 0)
        Cr[e] = jnp.concatenate([one] * N, 0)
        W3r[e] = Cr[e] * const["w3"][...]
        FXr[0, e * YF : (e + 1) * YF] = one
        FXr[0, 2 * YF + e * N : 2 * YF + (e + 1) * N] = cf[0]
        FXr[0, 2 * YF + (EX + e) * N : 2 * YF + (EX + e + 1) * N] = cf[EY - 1]

    rows = lax.broadcasted_iota(jnp.int32, (ROWS, ZF), 0)
    lanes = lax.broadcasted_iota(jnp.int32, (ROWS, ZF), 1)
    xr, yr = rows // YF, lax.rem(rows, YF)
    frow = lax.broadcasted_iota(jnp.int32, (96, ZF), 0)
    flane = lax.broadcasted_iota(jnp.int32, (96, ZF), 1)
    fx = jnp.where(frow < YF, 0, jnp.where(frow < 2 * YF, XF - 1, lax.rem(frow, XF)))
    fy = jnp.where(frow < 2 * YF, lax.rem(frow, YF), jnp.where(frow < 2 * YF + XF, 0, YF - 1))

    def edge(i, count=0):
        e = (lax.rem(i, N) == 0) | (lax.rem(i, N) == N - 1)
        return jnp.where(e & (i != 0) & (i != count - 1) if count else e, 0.5, 1.0)

    Wr[...] = edge(lanes) * edge(yr) * edge(xr)
    WLr[...] = edge(lanes) * edge(yr, YF)
    WFr[...] = edge(flane) * edge(fx) * edge(fy)
    WLFr[...] = edge(flane) * edge(fx, XF) * edge(fy, YF)

    tile_exchange.arrive()
    ext = tiles[...]
    pd = rmul(ext, const["Bdf"], HOW["g"])
    diag = lmul(const["Gdf"], pd[:, :ZF], pd[:, ZF:], n=HOW["g"])

    def mask_of(x, y, z, n):
        inner = (x > 0) & (x < gxn * EX * n - 1) & (y > 0) & (y < gyn * EY * n - 1)
        return inner & (z != 0) & (z != EZ * n - 1)

    for e in range(EX):
        keep = mask_of(px * XF + e * N + xr, py * YF + yr, lanes, N)
        Dr[e] = jnp.where(keep, 1.0 / diag[e * ROWS : (e + 1) * ROWS], 0.0)
    keep = mask_of(px * XF + fx, py * YF + fy, flane, N)
    df = jnp.where(keep, 1.0 / diag[EX * ROWS :], 0.0)
    DFr[...] = df
    DcFr[...] = df * FXr[0]
    pdc = rmul(ext, const["Bdc"], HOW["g"])
    diag_c = lmul(const["Gdc"], pdc[:, :ZC], pdc[:, ZC:], n=HOW["g"])
    crow = lax.broadcasted_iota(jnp.int32, (384, ZC), 0)
    clane = lax.broadcasted_iota(jnp.int32, (384, ZC), 1)

    def place(r, width, x0, y0):
        return (x0 + r // width, y0 + lax.rem(r, width))

    cx, cy = place(crow, YC, 0, 0)
    base = OWN
    for count, width, x0, y0 in (
        (ROWS_C, YC, -NC, 0), (ROWS_C, YC, XC, 0), (XC * NC, NC, 0, -NC), (XC * NC, NC, 0, YC),
        (16, NC, -NC, -NC), (16, NC, -NC, YC), (16, NC, XC, -NC), (16, NC, XC, YC),
    ):
        nx, ny = place(crow - base, width, x0, y0)
        cx, cy = jnp.where(crow >= base, nx, cx), jnp.where(crow >= base, ny, cy)
        base += count
    keep = mask_of(px * XC + cx, py * YC + cy, clane, NC)
    Dc_r[...] = jnp.where(keep, 1.0 / diag_c, 0.0)
    lines = dot(jnp.concatenate(spread(ext), 1), const["Bs"][:, ZF:])
    Cc_r[...] = dot(const["Pc"][...], jnp.concatenate(spread(lines), 0))

    def halo(i):
        fine(i).arrive()
        return jnp.concatenate([rx[i, 0], rx[i, 1], ry[i, 0] + rc[i, 0], ry[i, 1] + rc[i, 1]], 0)

    def add_faces(ref, index, h):
        ref[(*index, 0, pl.ds(0, YF))] += h[0:YF]
        ref[(*index, 1, pl.ds(ROWS - YF, YF))] += h[YF : 2 * YF]
        for x in range(XF):
            e, r = x // N, (x % N) * YF
            ref[(*index, e, pl.ds(r, 1))] += h[2 * YF + x : 2 * YF + x + 1]
            b = 2 * YF + XF + x
            ref[(*index, e, pl.ds(r + YF - 1, 1))] += h[b : b + 1]

    def sums_inside(v):
        wide = lambda name: jnp.concatenate([const[name][...]] * 2, 1)
        v = v + wide("yu") * pltpu.roll(v, ROWS - 1, 0) + wide("yd") * pltpu.roll(v, 1, 0)
        return v + const["zu"][0:1] * pltpu.roll(v, ZF - 1, 1) + const["zd"][0:1] * pltpu.roll(v, 1, 1)

    def bulk(values, n):
        for e in range(EX):
            p = split(values(e), n)
            p = [p[i] for i, _ in TERMS[:n]]
            t = dot(const["Mh"][:, : n * ROWS], jnp.concatenate(p, 0))
            t = t + dot(jnp.concatenate(p, 1), const["Kh"][: n * ZF])
            Lr[e] = sums_inside(W3r[e] * t)
        FXr[1, 0:YF] = Lr[0, 0:YF]
        FXr[1, YF : 2 * YF] = Lr[1, ROWS - YF : ROWS]
        for side, y in ((2 * YF, 0), (2 * YF + XF, YF - 1)):
            for x in range(XF):
                e, r = x // N, (x % N) * YF + y
                FXr[1, side + x : side + x + 1] = Lr[e, r : r + 1]
            both = Lr[0, ROWS - YF + y : ROWS - YF + y + 1] + Lr[1, y : y + 1]
            FXr[1, side + N - 1 : side + N] = both
            FXr[1, side + N : side + N + 1] = both

    def face_z(hs, n):
        return rmul(hs, const["Bf"], n)

    def send_faces(i, faces):
        sx[i, 0] = faces[0:YF]
        sx[i, 1] = faces[YF : 2 * YF]
        sy[i, 0] = faces[2 * YF : 2 * YF + XF]
        sy[i, 1] = faces[2 * YF + XF :]
        fine(i).start()

    def face_to_face(ph, n):
        return lmul(const["F2F"], ph[:, :ZF], ph[:, ZF:], n=n)

    def face_to_all(ph, n):
        for e in range(EX):
            part = jnp.concatenate([ph[e * YF : (e + 1) * YF], ph[2 * YF :]], 0)
            Lr[e] += lmul(const[f"F2A{e}"], part[:, :ZF], part[:, ZF:], n=n)
        middle(Lr)

    def finish(k):
        add_faces(Zr, (k,), (-k_f) * DFr[...] * Hr[...])
        face_to_all(PHr[...], HOW["h"])
        for e in range(EX):
            Fr[k + 1, e] = Lr[e]

    def total(x):
        x = jnp.sum(x, axis=0, keepdims=True)
        return x[:, : ZF // 2] + x[:, ZF // 2 :]

    def cycle(k, carry):
        pl.when(k > 0)(lambda: finish(k - 1))
        bulk(lambda e: (Dr[e] * inv_center) * Fr[k, e], HOW["a"])
        h = halo(4 * k)
        ph = face_z(DcFr[...] * inv_center * h, HOW["a"])
        send_faces(4 * k + 1, FXr[1] + face_to_face(ph, HOW["a"]))
        add_faces(Fr, (k,), h)
        FFr[k, 0:YF] = Fr[k, 0, 0:YF]
        FFr[k, YF : 2 * YF] = Fr[k, 1, ROWS - YF : ROWS]
        for x in range(XF):
            e, r = x // N, (x % N) * YF
            FFr[k, 2 * YF + x : 2 * YF + x + 1] = Fr[k, e, r : r + 1]
            b = 2 * YF + XF + x
            FFr[k, b : b + 1] = Fr[k, e, r + YF - 1 : r + YF]
        face_to_all(ph, HOW["a"])
        gl = None
        for e in range(EX):
            s = Dr[e] * (a_f * Fr[k, e] - k_f * Lr[e])
            Sr[e] = s
            p = rmul(Cr[e] * s, const["Br"], HOW["b"])
            Ar[e, :, 0:ZC] = rmul(Fr[k, e], const["Bw"], HOW["b"])
            o = lmul(const[f"Gr{e}"], p[:, :ZC], p[:, ZC:], n=HOW["b"])
            gl = o if e == 0 else gl + o
        gl = lmul(const["Gw"], Ar[0, :, 0:ZC], Ar[1, :, 0:ZC], n=HOW["b"]) - gl
        h = halo(4 * k + 1)
        hs = (-k_f) * DcFr[...] * h
        pr = rmul(hs, const["Br"], HOW["b"])
        gl = gl - lmul(const["F2R"], pr[:, :ZC], pr[:, ZC:], n=HOW["b"])
        cs[k] = gl
        coarse(k).start()
        gr[0:OWN] = gl[0:OWN]
        bulk(lambda e: Sr[e], HOW["s"])
        ph = face_z(hs, HOW["s"])
        face_to_all(ph, HOW["s"])
        FXr[1] = FXr[1] + face_to_face(ph, HOW["s"])
        add_faces(Sr, (), (-k_f) * DFr[...] * h)
        coarse(k).arrive()
        gr[OWN:] = cr[k]
        for a, b, n in coarse_pairs():
            t = gr[a : a + n] + gr[b : b + n]
            gr[a : a + n] = t
            gr[b : b + n] = t
        p = lmul(const["Gc"], Cc_r[...] * (Dc_r[...] * inv_center_c) * gr[...], n=HOW["c"])
        o = rmul(jnp.concatenate([p[:OWN], p[OWN:]], 1), const["Bc"], HOW["c"])
        g = gr[0:OWN]
        fix = Dc_r[0:OWN] * (a_c * g - k_c * o)
        p = rmul(Cc_r[0:OWN] * fix, const["Bj"], HOW["d"], slice(0, 2 * ZF))
        o = lmul(const["Gj"], p[:, :ZF], p[:, ZF:], n=HOW["d"], rows=slice(EX * ROWS, EX * ROWS + 96))
        send_faces(4 * k + 2, FXr[1] + o)
        o = lmul(const["Gj"], p[:, :ZF], p[:, ZF:], n=HOW["d"], rows=slice(0, EX * ROWS))
        p = rmul(fix, const["Bj"], HOW["d"], slice(2 * ZF, 3 * ZF))
        up = lmul(const["Gp"], p, n=HOW["d"])
        for e in range(EX):
            part = slice(e * ROWS, (e + 1) * ROWS)
            Sr[e] = Sr[e] + up[part]
            Rr[e] = Fr[k, e] - Lr[e] - o[part]
        bulk(lambda e: (Dr[e] * inv_center) * Rr[e], HOW["e"])
        h = halo(4 * k + 2)
        ph = face_z((-inv_center) * DcFr[...] * h, HOW["e"])
        send_faces(4 * k + 3, FXr[1] + face_to_face(ph, HOW["e"]))
        add_faces(Rr, (), -h)
        face_to_all(ph, HOW["e"])
        for e in range(EX):
            Zr[k, e] = Sr[e] + Dr[e] * (a_f * Rr[e] - k_f * Lr[e])
        bulk(lambda e: Zr[k, e], HOW["f"])
        sums = [0.0] * 3
        for e in range(EX):
            z = Zr[k, e]
            wz = Wr[...] * z
            for i, t in enumerate((Fr[0, e] * wz, Fr[k, e] * wz, WLr[...] * Lr[e] * z)):
                sums[i] = sums[i] + total(t)
        h = halo(4 * k + 3)
        delta = (-k_f) * DFr[...] * h
        ph = face_z((-k_f) * DcFr[...] * h, HOW["h"])
        ff = face_to_face(ph, HOW["h"])
        send_faces(4 * k + 4, FXr[1] + ff)
        wd = WFr[...] * delta
        faces = (FFr[0] * wd, FFr[k] * wd, WLFr[...] * delta * (2.0 * FXr[1] + ff))
        for i, t in enumerate(faces):
            dots[k, i : i + 1] = sums[i] + total(t)
        PHr[...] = ph
        Hr[...] = h
        return carry

    lax.fori_loop(0, 2, cycle, 0)

    def reduce_stage(buf, stage, base):
        return [
            pltpu.make_async_remote_copy(
                src_ref=buf.at[0], dst_ref=buf.at[j + 1], send_sem=dsend_sem.at[base + j], recv_sem=drecv_sem.at[base + j],
                device_id=p, device_id_type=MESH,
            )
            for j, p in enumerate(stage)
        ]

    def summed(buf, stage, n):
        for c in stage:
            c.wait_recv()
        out = buf[0]
        for j in range(n):
            out = out + buf[j + 1]
        return out

    d1[0, 0:3] = dots[0, 0:3]
    d1[0, 3:6] = dots[1, 0:3]
    d1[0, 6:8] = jnp.zeros((2, 128), F32)
    stage1 = reduce_stage(d1, stages[0], 0)
    stage2 = reduce_stage(d2, stages[1], len(stage1))
    for c in stage1:
        c.start()
    finish(1)
    d2[0] = summed(d1, stage1, len(stage1))
    for c in stage2:
        c.start()
    h = halo(8)
    add_faces(Fr, (2,), h)
    lanes_sum = jnp.sum(summed(d2, stage2, len(stage2)), axis=1, keepdims=True)
    pick = lambda i: lanes_sum[i : i + 1, 0:1]
    rz0, c00 = pick(1), pick(2)
    r0u, wu, uv = pick(3), pick(4), pick(5)
    alpha0 = rz0 / c00
    rz1 = alpha0 * (alpha0 * wu - r0u)
    beta1 = 1.0 + rz1 / rz0
    curve = beta1 * beta1 * c00 - 2.0 * beta1 * alpha0 * wu + alpha0 * alpha0 * uv
    alpha1 = rz1 / curve
    c_z = alpha0 + alpha1 * beta1
    c_u = alpha1 * alpha0
    for e in range(EX):
        sol_ref[e] = c_z * Zr[0, e] - c_u * Zr[1, e]
        res_ref[e] = jnp.where(Dr[e] > 0.0, Fr[0, e] - c_z * Fr[1, e] + c_u * Fr[2, e], 0.0)

    tile_exchange.drain()
    for c in stage1 + stage2:
        c.wait_send()

    def drain(i, carry):
        fine(i).drain()
        return carry

    lax.fori_loop(0, 9, drain, 0)
    for k in range(2):
        coarse(k).drain()


def solution(mesh):
    gxn, gyn = mesh.shape["gx"], mesh.shape["gy"]
    table = constants()
    names = tuple(table)
    n_dots = gyn - 1 + gxn - 1

    def per_device(right_side, coefficient):
        rhs = right_side.reshape(EX, ROWS, ZF)
        field = (EX, ROWS, ZF)
        vm = lambda *s: pltpu.VMEM(s, F32)
        dma = lambda *s: pltpu.SemaphoreType.DMA(s)
        face = (96, ZF)
        scratch = [pltpu.VMEM(table[m].shape, table[m].dtype) for m in names]
        scratch += [
            vm(3, *field), vm(2, *field), vm(*field), vm(*field), vm(*field), vm(384, ZC), vm(*face), vm(*face),
            vm(*field), vm(*field), vm(*field), vm(*field), vm(2, *face), vm(2, *face), vm(96, 2 * ZF), vm(*face),
            vm(ROWS, ZF), vm(ROWS, ZF), vm(*face), vm(*face),
            vm(384, ZC), vm(384, ZC), vm(8, 128), vm(80, 128),
            vm(9, 2, YF, ZF), vm(9, 2, EX * N, ZF), vm(9, 2, YF, ZF), vm(9, 2, EX * N, ZF), vm(9, 2, EX * N, ZF),
            vm(2, 192, ZC), vm(2, 256, ZC),
            vm(2, 8, 128), vm(gyn, 8, 128), vm(gxn, 8, 128),
            dma(len(names)), dma(9, 8), dma(9, 8), dma(2, 8), dma(2, 8), dma(8), dma(8), dma(n_dots), dma(n_dots),
        ]
        sol, res = pl.pallas_call(
            functools.partial(kernel_body, (gxn, gyn), names),
            out_shape=[pltpu.VMEM(field, F32)] * 2,
            in_specs=[pl.BlockSpec(memory_space=pltpu.VMEM)] * 2 + [pl.BlockSpec(memory_space=pl.ANY)] * len(names),
            out_specs=[pl.BlockSpec(memory_space=pltpu.VMEM)] * 2,
            scratch_shapes=scratch,
            compiler_params=pltpu.CompilerParams(
                collective_id=0, has_side_effects=True, vmem_limit_bytes=56 * 2**20
            ),
        )(rhs, coefficient, *[jnp.asarray(table[m]) for m in names])
        return sol.reshape(right_side.shape), res.reshape(right_side.shape)

    spec = P("gx", "gy", None)
    return jax.shard_map(
        per_device, mesh=mesh, in_specs=(spec, spec), out_specs=(spec, spec), check_vma=False
    )
```

```python
import functools
import math

import jax
import jax.numpy as jnp
import numpy as np
from jax import lax
from jax.experimental import pallas as pl
from jax.experimental.pallas import tpu as pltpu
from jax.sharding import PartitionSpec as P

ORDER = 7
COARSE_ORDER = 3
F32 = jnp.float32
BF16 = jnp.bfloat16
MESH = pl.DeviceIdType.MESH

EX, EY, EZ = 2, 4, 32
N, NC = ORDER + 1, COARSE_ORDER + 1
YF, ZF = EY * N, EZ * N
YC, ZC = EY * NC, EZ * NC
ROWS = N * YF
ROWS_C = NC * YC


def legendre_pair(degree, points):
    before = points * 0.0 + 1.0
    now = points.copy()
    for power in range(2, degree + 1):
        after = ((2 * power - 1) * points * now - (power - 1) * before) / power
        before = now
        now = after
    return (now, before)


def gll_tables(degree):
    number = degree + 1
    points = np.cos(math.pi * np.arange(number) / degree)
    for newton in range(60):
        top, below = legendre_pair(degree, points)
        points = points - (points * top - below) / (number * top)
    points = points[::-1].copy()
    points[0] = -1.0
    points[degree] = 1.0
    values = legendre_pair(degree, points)[0]
    weights = 2.0 / (degree * (degree + 1) * values**2)
    derivative = np.zeros((number, number))
    for row_index in range(number):
        for column_index in range(number):
            if row_index != column_index:
                derivative[row_index, column_index] = values[row_index] / (
                    values[column_index] * (points[row_index] - points[column_index])
                )
    derivative[0, 0] = -degree * (degree + 1) / 4.0
    derivative[degree, degree] = degree * (degree + 1) / 4.0
    stiffness = derivative.T @ (weights[:, None] * derivative)
    return (points, weights, stiffness)


def upper_bound(degree):
    points, weights, stiffness = gll_tables(degree)
    rowsum = np.abs(stiffness).sum(1)
    diagonal = np.diag(stiffness)
    outer = lambda a, b, c: a[:, None, None] * b[None, :, None] * c[None, None, :]
    top = outer(rowsum, weights, weights) + outer(weights, rowsum, weights) + outer(weights, weights, rowsum)
    bottom = outer(diagonal, weights, weights) + outer(weights, diagonal, weights) + outer(weights, weights, diagonal)
    return float((top / bottom).max())


def interpolation_matrix(fine_degree, coarse_degree):
    fine_points = gll_tables(fine_degree)[0]
    coarse_points = gll_tables(coarse_degree)[0]
    matrix = np.ones((fine_degree + 1, coarse_degree + 1))
    for column_index in range(coarse_degree + 1):
        for other_index in range(coarse_degree + 1):
            if other_index != column_index:
                matrix[:, column_index] *= (fine_points - coarse_points[other_index]) / (
                    coarse_points[column_index] - coarse_points[other_index]
                )
    return matrix


def cheb_numbers(degree):
    upper = upper_bound(degree)
    lower = 0.1 * upper
    center = 0.5 * (upper + lower)
    half = 0.5 * (upper - lower)
    previous = half / center
    current = 1.0 / (2.0 * center / half - previous)
    k = 2.0 * current / half
    return (1.0 / center, (1.0 + current * previous) / center + k, k)


def sum_matrix(elements, number):
    matrix = np.eye(elements * number)
    for e in range(elements - 1):
        a, b = e * number + number - 1, (e + 1) * number
        matrix[a, b] = matrix[b, a] = 1.0
    return matrix


def blocks(count, matrix):
    return np.kron(np.eye(count), matrix)


TERMS = ((0, 0), (1, 0), (0, 1), (2, 0), (0, 2), (1, 1))
HOW = dict(a=3, b=3, s=6, c=3, d=6, e=3, f=6, g=3, h=3)


def pieces_of(matrix, count):
    rest, out = np.asarray(matrix, np.float64), []
    for _ in range(count):
        out.append(rest.astype(np.float32).astype(BF16))
        rest = rest - out[-1].astype(np.float64)
    return out


def right3(matrix, steps="asef"):
    p = pieces_of(matrix, 3)
    return np.concatenate([p[j] for _, j in TERMS[: max(HOW[t] for t in steps)]], 0)


def left3(matrix, steps="asef"):
    p = pieces_of(matrix, 3)
    return np.concatenate([p[j] for _, j in TERMS[: max(HOW[t] for t in steps)]], 1)


def level_matrices(degree):
    _, w, K = gll_tables(degree)
    n = degree + 1
    wy = np.tile(w, EY)
    M0 = np.kron(K, np.diag(wy)) + np.kron(np.diag(w), blocks(EY, K))
    N0 = np.kron(np.diag(w), np.diag(wy))
    return M0, N0, np.diag(np.tile(w, EZ)), blocks(EZ, K)


def face_rows(n):
    y = EY * n
    x = EX * n
    rows = [j for j in range(y)] + [(x - 1) * y + j for j in range(y)]
    rows += [i * y for i in range(x)] + [i * y + y - 1 for i in range(x)]
    return np.array(rows)


def coarse_places():
    XC = EX * NC
    before, after_x, after_y = range(-NC, 0), range(XC, XC + NC), range(YC, YC + NC)
    grids = [(range(XC), range(YC)), (before, range(YC)), (after_x, range(YC)), (range(XC), before), (range(XC), after_y)]
    grids += [(a, b) for a in (before, after_x) for b in (before, after_y)]
    both = [(x, y) for xs, ys in grids for x in xs for y in ys]
    return np.array([p[0] for p in both]), np.array([p[1] for p in both])


def coarse_pairs():
    x, y = coarse_places()
    row = {p: i for i, p in enumerate(zip(x.tolist(), y.tolist()))}
    XC, out = EX * NC, []
    for a, b in ((-1, 0), (XC - 1, XC)):
        for first, n in ((-NC, NC), (0, YC), (YC, NC)):
            out.append((row[a, first], row[b, first], n))
    for a, b in ((-1, 0), (YC - 1, YC)):
        out += [(row[i, a], row[i, b], 1) for i in range(-NC, XC + NC)]
    return out


@functools.cache
def constants():
    J = interpolation_matrix(ORDER, COARSE_ORDER)
    out = {}
    M0, N0, Wz, Kz = level_matrices(ORDER)
    Sz, Szc = sum_matrix(EZ, N), sum_matrix(EZ, NC)
    Sxy = np.kron(sum_matrix(EX, N), sum_matrix(EY, N))
    Sxyc = np.kron(sum_matrix(EX, NC), sum_matrix(EY, NC))
    Mf, Nf = blocks(EX, M0), blocks(EX, N0)
    SM, SN = Sxy @ Mf, Sxy @ Nf
    F = face_rows(N)
    out["Bf"] = right3(np.concatenate([Wz @ Sz, Kz @ Sz], 1))
    _, w, K = gll_tables(ORDER)
    wxy, wz = np.kron(w, np.tile(w, EY)), np.tile(w, EZ)
    out["Mh"] = left3(M0 / wxy[:, None])
    out["Kh"] = right3(Kz / wz[None, :])
    out["w3"] = (wxy[:, None] * wz[None, :]).astype(np.float32)
    y, z = np.arange(ROWS) % YF, np.arange(ZF)
    wide = lambda m, shape: np.broadcast_to(m, shape).astype(np.float32)
    out["yu"] = wide(((y % N == N - 1) & (y != YF - 1))[:, None], (ROWS, 128))
    out["yd"] = wide(((y % N == 0) & (y != 0))[:, None], (ROWS, 128))
    out["zu"] = wide(((z % N == N - 1) & (z != ZF - 1))[None, :], (8, ZF))
    out["zd"] = wide(((z % N == 0) & (z != 0))[None, :], (8, ZF))
    Sy = np.kron(np.eye(EX * N), sum_matrix(EY, N))
    out["F2F"] = left3(np.concatenate([SM[F][:, F], SN[F][:, F]], 1))
    for e in range(EX):
        rows = slice(e * ROWS, (e + 1) * ROWS)
        here = np.concatenate([np.arange(e * YF, (e + 1) * YF), np.arange(2 * YF, len(F))])
        keep = ((F[here] // ROWS) == e).astype(float)[None, :]
        full = np.concatenate([(Sy @ Mf)[rows][:, F[here]] * keep, (Sy @ Nf)[rows][:, F[here]] * keep], 1)
        out[f"F2A{e}"] = left3(full)
    Rxy = blocks(EX, np.kron(J.T, blocks(EY, J.T)))
    JZ = blocks(EZ, J)
    XC = EX * NC
    first = [x * YC + y for x in range(XC) for y in range(NC)]
    last = [x * YC + YC - NC + y for x in range(XC) for y in range(NC)]
    selc = np.concatenate([np.arange(XC * YC), first, last]).astype(int)
    RM, RN = (Sxyc @ Rxy @ Mf)[selc], (Sxyc @ Rxy @ Nf)[selc]
    out["Br"] = right3(np.concatenate([Wz @ JZ @ Szc, Kz @ JZ @ Szc], 1), "b")
    for e in range(EX):
        cols = slice(e * ROWS, (e + 1) * ROWS)
        out[f"Gr{e}"] = left3(np.concatenate([RM[:, cols], RN[:, cols]], 1), "b")
    out["F2R"] = left3(np.concatenate([RM[:, F], RN[:, F]], 1), "b")
    inv = lambda count: np.where((np.arange(count) % N == 0) | (np.arange(count) % N == N - 1), 0.5, 1.0)
    Wxy = np.kron(np.diag(inv(EX * N)), np.diag(inv(YF)))
    RW = (Sxyc @ Rxy @ Wxy)[selc]
    out["Bw"] = right3(np.diag(inv(ZF)) @ JZ @ Szc, "b")
    out["Gw"] = left3(RW, "b")
    _, wc, Kc = gll_tables(COARSE_ORDER)
    Wzc, Kzc = np.diag(np.tile(wc, EZ)), blocks(EZ, Kc)
    out["Bc"] = right3(np.concatenate([Wzc @ Szc, Kzc @ Szc], 0), "c")
    cx, cy = coarse_places()
    grid = (cx + NC) * (YC + 2 * NC) + cy + NC
    wx4, wy6 = np.diag(np.tile(wc, EX + 2)), np.diag(np.tile(wc, EY + 2))
    Me = np.kron(blocks(EX + 2, Kc), wy6) + np.kron(wx4, blocks(EY + 2, Kc))
    Ne = np.kron(wx4, wy6)
    Se = np.kron(sum_matrix(EX + 2, NC), sum_matrix(EY + 2, NC))
    own = grid[: XC * YC]
    out["Gc"] = left3(np.concatenate([(Se @ Me)[own][:, grid], (Se @ Ne)[own][:, grid]], 0), "c")
    pick = np.zeros((len(cx), 80))
    for i, (x, y) in enumerate(zip(cx // NC, cy // NC)):
        pick[i, ((x // EX + 1) * 3 + y // EY + 1) * 8 + (x % EX) * EY + y % EY] = 1.0
    out["Pc"] = np.concatenate([pick.astype(np.float32).astype(BF16)] * 3, 1)
    Jxy = blocks(EX, np.kron(J, blocks(EY, J)))
    out["Bj"] = right3(np.concatenate([JZ.T @ Wz @ Sz, JZ.T @ Kz @ Sz, JZ.T], 1), "d")
    sel = np.concatenate([np.arange(EX * ROWS), F])
    JM, JN = (SM @ Jxy)[sel], (SN @ Jxy)[sel]
    out["Gj"] = left3(np.concatenate([JM, JN], 1), "d")
    out["Gp"] = left3(Jxy, "d")
    fine_x, fine_y = np.divmod(np.arange(EX * ROWS), YF)
    places = {"f": (np.concatenate([fine_x, F // YF]), np.concatenate([fine_y, F % YF])), "c": (cx, cy)}
    for name, degree in (("f", ORDER), ("c", COARSE_ORDER)):
        n = degree + 1
        _, w, K = gll_tables(degree)
        kd = np.diag(K)
        S = sum_matrix(EZ, n)
        spread_w = np.zeros((128, EZ * n))
        spread_k = np.zeros((128, EZ * n))
        for ez in range(EZ):
            spread_w[ez, ez * n : (ez + 1) * n] = w
            spread_k[ez, ez * n : (ez + 1) * n] = kd
        out["Bd" + name] = right3(np.concatenate([spread_w @ S, spread_k @ S], 1), "g")
        left = np.zeros((len(places[name][0]), 2, 80))
        for i, (x, y) in enumerate(zip(*places[name])):
            xs = [(x // n, x % n)]
            if x % n == 0:
                xs.append((x // n - 1, n - 1))
            if x % n == n - 1:
                xs.append((x // n + 1, 0))
            ys = [(y // n, y % n)]
            if y % n == 0:
                ys.append((y // n - 1, n - 1))
            if y % n == n - 1:
                ys.append((y // n + 1, 0))
            for ex, a in xs:
                for ey, b in ys:
                    col = ((ex // EX + 1) * 3 + ey // EY + 1) * 8 + (ex % EX) * EY + ey % EY
                    left[i, 0, col] += kd[a] * w[b] + w[a] * kd[b]
                    left[i, 1, col] += w[a] * w[b]
        left = left.reshape(len(left), 160)
        if name == "f":
            here = left.reshape(len(left), 2, 80)[: EX * ROWS, :, 32:40].reshape(EX * ROWS, 16)
            out["Gdo"] = left3(here, "g")
            left = left[EX * ROWS :]
        out["Gd" + name] = left3(left, "g")
    spread = np.zeros((128, ZF + ZC))
    for ez in range(EZ):
        spread[ez, ez * N : (ez + 1) * N] = 1.0
        spread[ez, ZF + ez * NC : ZF + (ez + 1) * NC] = 1.0
    out["Bs"] = np.concatenate([spread.astype(np.float32).astype(BF16)] * 3, 0)
    return out


def dot(a, b):
    return jnp.dot(a, b, preferred_element_type=F32)


def split(x, n):
    out = []
    for i in range(1 + max(i for i, _ in TERMS[:n])):
        out.append(x.astype(BF16))
        x = x - out[-1].astype(F32)
    return out


def rmul(x, b, n, cols=slice(None)):
    p = split(x, n)
    x3 = jnp.concatenate([p[i] for i, _ in TERMS[:n]], 1)
    return dot(x3, b[: x3.shape[1], cols])


def lmul(g, *parts, n, rows=slice(None)):
    split_parts = [split(x, n) for x in parts]
    x3 = jnp.concatenate([p[i] for i, _ in TERMS[:n] for p in split_parts], 0)
    return dot(g[rows, : x3.shape[0]], x3)


def kernel_body(shape, names, rhs_ref, coef_ref, *refs):
    gxn, gyn = shape
    n_const = len(names)
    const_hbm = dict(zip(names, refs[:n_const]))
    sol_ref, res_ref = refs[n_const : n_const + 2]
    rest = refs[n_const + 2 :]
    const = dict(zip(names, rest[:n_const]))
    (Fr, Zr, Dr, Cr, W3r, gr, DFr, DcFr, Lr, Sr, Rr, Ar, FXr, FFr, PHr, Hr, Wr, WLr, WFr, WLFr,
     Dc_r, Cc_r, cpad, coef, tiles,
     sx, sy, rx, ry, rc, cs, cr, dots, d1, d2,
     const_sem, send_sem, recv_sem, csend_sem, crecv_sem, tsend_sem, trecv_sem, dsend_sem, drecv_sem) = rest[n_const:]

    inv_center, a_f, k_f = cheb_numbers(ORDER)
    inv_center_c, a_c, k_c = cheb_numbers(COARSE_ORDER)
    px, py = lax.axis_index("gx"), lax.axis_index("gy")
    XF, XC, OWN = EX * N, EX * NC, EX * ROWS_C

    def at(dx, dy):
        return (lax.rem(px + dx + gxn, gxn), lax.rem(py + dy + gyn, gyn))

    def inside(dx, dy):
        ok = None
        for p, d, n in ((px, dx, gxn), (py, dy, gyn)):
            if d:
                here = (p > 0) if d < 0 else (p < n - 1)
                ok = here if ok is None else ok & here
        return ok

    corners = [(dx, dy) for dx in (-1, 1) for dy in (-1, 1)]
    around = corners + [(-1, 0), (1, 0), (0, -1), (0, 1)]
    stages = [
        [(px, lax.rem(py + d, gyn)) for d in range(1, gyn)],
        [(lax.rem(px + d, gxn), py) for d in range(1, gxn)],
    ]

    copies = [pltpu.make_async_copy(const_hbm[m], const[m], const_sem.at[i]) for i, m in enumerate(names)]
    load_rhs = pltpu.make_async_copy(rhs_ref, Ar, const_sem.at[n_const])
    load_coef = pltpu.make_async_copy(coef_ref, coef, const_sem.at[n_const + 1])
    load_rhs.start()
    load_coef.start()
    for c in copies:
        c.start()

    for ref in (rx, ry, rc, cr, tiles, cpad):
        ref[...] = jnp.zeros_like(ref)

    barrier = pltpu.get_barrier_semaphore()
    expected = 0
    for d in around:
        pl.when(inside(*d))(
            lambda d=d: pl.semaphore_signal(barrier, inc=1, device_id=at(*d), device_id_type=MESH)
        )
        expected = expected + inside(*d).astype(jnp.int32)
    for stage in stages:
        for p in stage:
            pl.semaphore_signal(barrier, inc=1, device_id=p, device_id_type=MESH)
        expected = expected + len(stage)

    def local_sum(v):
        rows = lax.broadcasted_iota(jnp.int32, v.shape, 0)
        lanes = lax.broadcasted_iota(jnp.int32, v.shape, 1)
        y = lax.rem(rows, YF)
        up = (lax.rem(y, N) == N - 1) & (y != YF - 1)
        down = (lax.rem(y, N) == 0) & (y != 0)
        v = v + jnp.where(up, pltpu.roll(v, ROWS - 1, 0), 0.0) + jnp.where(down, pltpu.roll(v, 1, 0), 0.0)
        up = (lax.rem(lanes, N) == N - 1) & (lanes != ZF - 1)
        down = (lax.rem(lanes, N) == 0) & (lanes != 0)
        return v + jnp.where(up, pltpu.roll(v, ZF - 1, 1), 0.0) + jnp.where(down, pltpu.roll(v, 1, 1), 0.0)

    def middle(ref, *index):
        total = ref[(*index, 0, pl.ds(ROWS - YF, YF))] + ref[(*index, 1, pl.ds(0, YF))]
        ref[(*index, 0, pl.ds(ROWS - YF, YF))] = total
        ref[(*index, 1, pl.ds(0, YF))] = total

    load_coef.wait()
    cpad[0:EY, 0:EZ] = coef[0]
    cpad[EY : 2 * EY, 0:EZ] = coef[1]
    load_rhs.wait()
    for e in range(EX):
        Fr[0, e] = local_sum(Ar[e])
    middle(Fr, 0)
    sx[0, 0] = Fr[0, 0, 0:YF]
    sx[0, 1] = Fr[0, 1, ROWS - YF : ROWS]
    for x in range(XF):
        e, r = x // N, (x % N) * YF
        sy[0, 0, x : x + 1] = Fr[0, e, r : r + 1]
        sy[0, 1, x : x + 1] = Fr[0, e, r + YF - 1 : r + YF]

    class Exchange:
        def __init__(self, plan, send, recv):
            self.plan = [
                (pltpu.make_async_remote_copy(
                    src_ref=s, dst_ref=t, send_sem=send(j), recv_sem=recv(j), device_id=at(*d), device_id_type=MESH,
                ), inside(*d), inside(-d[0], -d[1]))
                for j, (s, t, d) in enumerate(plan)
            ]

        def start(self):
            for c, to, _ in self.plan:
                pl.when(to)(c.start)

        def arrive(self):
            for c, _, come in self.plan:
                pl.when(come)(c.wait_recv)

        def drain(self):
            for c, to, _ in self.plan:
                pl.when(to)(c.wait_send)

    def fine(i):
        one = lambda r: pl.ds(r, 1)
        plan = [
            (sy.at[i, 0, one(0)], rc.at[i, 1, one(XF - 1)], (-1, -1)),
            (sy.at[i, 1, one(0)], rc.at[i, 0, one(XF - 1)], (-1, 1)),
            (sy.at[i, 0, one(XF - 1)], rc.at[i, 1, one(0)], (1, -1)),
            (sy.at[i, 1, one(XF - 1)], rc.at[i, 0, one(0)], (1, 1)),
            (sx.at[i, 0], rx.at[i, 1], (-1, 0)),
            (sx.at[i, 1], rx.at[i, 0], (1, 0)),
            (sy.at[i, 0], ry.at[i, 1], (0, -1)),
            (sy.at[i, 1], ry.at[i, 0], (0, 1)),
        ]
        return Exchange(plan, lambda j: send_sem.at[i, j], lambda j: recv_sem.at[i, j])

    def coarse(k):
        h, q = ROWS_C, NC * NC
        y0, y1 = OWN, OWN + XC * NC
        c0 = 2 * h + 4 * q
        src = lambda a, n: cs.at[k, pl.ds(a, n)]
        dst = lambda a, n: cr.at[k, pl.ds(a, n)]
        plan = [
            (src(y0, q), dst(c0 + 3 * q, q), (-1, -1)),
            (src(y1, q), dst(c0 + 2 * q, q), (-1, 1)),
            (src(y0 + q, q), dst(c0 + q, q), (1, -1)),
            (src(y1 + q, q), dst(c0, q), (1, 1)),
            (src(0, h), dst(h, h), (-1, 0)),
            (src(h, h), dst(0, h), (1, 0)),
            (src(y0, 2 * q), dst(2 * h + 2 * q, 2 * q), (0, -1)),
            (src(y1, 2 * q), dst(2 * h, 2 * q), (0, 1)),
        ]
        return Exchange(plan, lambda j: csend_sem.at[k, j], lambda j: crecv_sem.at[k, j])

    pl.semaphore_wait(barrier, expected)

    tile_plan = []
    for dx, dy in around:
        slot = ((1 - dx) * 3 + (1 - dy)) * 8
        tile_plan.append((cpad, tiles.at[pl.ds(slot, 8)], (dx, dy)))
    tile_exchange = Exchange(tile_plan, lambda j: tsend_sem.at[j], lambda j: trecv_sem.at[j])
    tile_exchange.start()
    fine(0).start()
    tiles[32:40] = cpad[...]

    for c in copies:
        c.wait()

    def spread(x):
        h1 = x.astype(BF16)
        r1 = x - h1.astype(F32)
        h2 = r1.astype(BF16)
        return [h1, h2, (r1 - h2.astype(F32)).astype(BF16)]

    spread_own = dot(jnp.concatenate(spread(cpad[...]), 1), const["Bs"][...])
    for e in range(EX):
        lines = [spread_own[e * EY + ey : e * EY + ey + 1] for ey in range(EY)]
        cf = [jnp.broadcast_to(l[:, :ZF], (N, ZF)) for l in lines]
        one = jnp.concatenate(cf, 0)
        Cr[e] = jnp.concatenate([one] * N, 0)
        W3r[e] = Cr[e] * const["w3"][...]
        FXr[0, e * YF : (e + 1) * YF] = one
        FXr[0, 2 * YF + e * N : 2 * YF + (e + 1) * N] = cf[0]
        FXr[0, 2 * YF + (EX + e) * N : 2 * YF + (EX + e + 1) * N] = cf[EY - 1]

    rows = lax.broadcasted_iota(jnp.int32, (ROWS, ZF), 0)
    lanes = lax.broadcasted_iota(jnp.int32, (ROWS, ZF), 1)
    xr, yr = rows // YF, lax.rem(rows, YF)
    frow = lax.broadcasted_iota(jnp.int32, (96, ZF), 0)
    flane = lax.broadcasted_iota(jnp.int32, (96, ZF), 1)
    fx = jnp.where(frow < YF, 0, jnp.where(frow < 2 * YF, XF - 1, lax.rem(frow, XF)))
    fy = jnp.where(frow < 2 * YF, lax.rem(frow, YF), jnp.where(frow < 2 * YF + XF, 0, YF - 1))

    def edge(i, count=0):
        e = (lax.rem(i, N) == 0) | (lax.rem(i, N) == N - 1)
        return jnp.where(e & (i != 0) & (i != count - 1) if count else e, 0.5, 1.0)

    Wr[...] = edge(lanes) * edge(yr) * edge(xr)
    WLr[...] = edge(lanes) * edge(yr, YF)
    WFr[...] = edge(flane) * edge(fx) * edge(fy)
    WLFr[...] = edge(flane) * edge(fx, XF) * edge(fy, YF)

    def mask_of(x, y, z, n):
        inner = (x > 0) & (x < gxn * EX * n - 1) & (y > 0) & (y < gyn * EY * n - 1)
        return inner & (z != 0) & (z != EZ * n - 1)

    pd = rmul(cpad[...], const["Bdf"], HOW["g"])
    diag = lmul(const["Gdo"], jnp.concatenate([pd[:, :ZF], pd[:, ZF:]], 0), n=HOW["g"])
    for e in range(EX):
        keep = mask_of(px * XF + e * N + xr, py * YF + yr, lanes, N)
        Dr[e] = jnp.where(keep, 1.0 / diag[e * ROWS : (e + 1) * ROWS], 0.0)
    fkeep = mask_of(px * XF + fx, py * YF + fy, flane, N)
    tile_exchange.arrive()
    pd = rmul(tiles[...], const["Bdf"], HOW["g"])
    diag = lmul(const["Gdf"], pd[:, :ZF], pd[:, ZF:], n=HOW["g"])
    df = jnp.where(fkeep, 1.0 / diag, 0.0)
    DFr[...] = df
    DcFr[...] = df * FXr[0]
    Dr[0, 0:YF] = df[0:YF]
    Dr[1, ROWS - YF : ROWS] = df[YF : 2 * YF]
    for x in range(XF):
        e, r = x // N, (x % N) * YF
        Dr[e, r : r + 1] = df[2 * YF + x : 2 * YF + x + 1]
        b = 2 * YF + XF + x
        Dr[e, r + YF - 1 : r + YF] = df[b : b + 1]

    def coarse_setup():
        ext = tiles[...]
        pdc = rmul(ext, const["Bdc"], HOW["g"])
        diag_c = lmul(const["Gdc"], pdc[:, :ZC], pdc[:, ZC:], n=HOW["g"])
        crow = lax.broadcasted_iota(jnp.int32, (384, ZC), 0)
        clane = lax.broadcasted_iota(jnp.int32, (384, ZC), 1)

        def place(r, width, x0, y0):
            return (x0 + r // width, y0 + lax.rem(r, width))

        cx, cy = place(crow, YC, 0, 0)
        base = OWN
        for count, width, x0, y0 in (
            (ROWS_C, YC, -NC, 0), (ROWS_C, YC, XC, 0), (XC * NC, NC, 0, -NC), (XC * NC, NC, 0, YC),
            (16, NC, -NC, -NC), (16, NC, -NC, YC), (16, NC, XC, -NC), (16, NC, XC, YC),
        ):
            nx, ny = place(crow - base, width, x0, y0)
            cx, cy = jnp.where(crow >= base, nx, cx), jnp.where(crow >= base, ny, cy)
            base += count
        keep = mask_of(px * XC + cx, py * YC + cy, clane, NC)
        Dc_r[...] = jnp.where(keep, 1.0 / diag_c, 0.0)
        lines = dot(jnp.concatenate(spread(ext), 1), const["Bs"][:, ZF:])
        Cc_r[...] = dot(const["Pc"][...], jnp.concatenate(spread(lines), 0))

    def halo(i):
        fine(i).arrive()
        return jnp.concatenate([rx[i, 0], rx[i, 1], ry[i, 0] + rc[i, 0], ry[i, 1] + rc[i, 1]], 0)

    def add_faces(ref, index, h):
        ref[(*index, 0, pl.ds(0, YF))] += h[0:YF]
        ref[(*index, 1, pl.ds(ROWS - YF, YF))] += h[YF : 2 * YF]
        for x in range(XF):
            e, r = x // N, (x % N) * YF
            ref[(*index, e, pl.ds(r, 1))] += h[2 * YF + x : 2 * YF + x + 1]
            b = 2 * YF + XF + x
            ref[(*index, e, pl.ds(r + YF - 1, 1))] += h[b : b + 1]

    def sums_inside(v):
        wide = lambda name: jnp.concatenate([const[name][...]] * 2, 1)
        v = v + wide("yu") * pltpu.roll(v, ROWS - 1, 0) + wide("yd") * pltpu.roll(v, 1, 0)
        return v + const["zu"][0:1] * pltpu.roll(v, ZF - 1, 1) + const["zd"][0:1] * pltpu.roll(v, 1, 1)

    def bulk(values, n):
        for e in range(EX):
            p = split(values(e), n)
            p = [p[i] for i, _ in TERMS[:n]]
            t = dot(const["Mh"][:, : n * ROWS], jnp.concatenate(p, 0))
            t = t + dot(jnp.concatenate(p, 1), const["Kh"][: n * ZF])
            Lr[e] = sums_inside(W3r[e] * t)
        FXr[1, 0:YF] = Lr[0, 0:YF]
        FXr[1, YF : 2 * YF] = Lr[1, ROWS - YF : ROWS]
        for side, y in ((2 * YF, 0), (2 * YF + XF, YF - 1)):
            for x in range(XF):
                e, r = x // N, (x % N) * YF + y
                FXr[1, side + x : side + x + 1] = Lr[e, r : r + 1]
            both = Lr[0, ROWS - YF + y : ROWS - YF + y + 1] + Lr[1, y : y + 1]
            FXr[1, side + N - 1 : side + N] = both
            FXr[1, side + N : side + N + 1] = both

    def face_z(hs, n):
        return rmul(hs, const["Bf"], n)

    def send_faces(i, faces):
        sx[i, 0] = faces[0:YF]
        sx[i, 1] = faces[YF : 2 * YF]
        sy[i, 0] = faces[2 * YF : 2 * YF + XF]
        sy[i, 1] = faces[2 * YF + XF :]
        fine(i).start()

    def face_to_face(ph, n):
        return lmul(const["F2F"], ph[:, :ZF], ph[:, ZF:], n=n)

    def face_to_all(ph, n):
        for e in range(EX):
            part = jnp.concatenate([ph[e * YF : (e + 1) * YF], ph[2 * YF :]], 0)
            Lr[e] += lmul(const[f"F2A{e}"], part[:, :ZF], part[:, ZF:], n=n)
        middle(Lr)

    def finish(k):
        add_faces(Zr, (k,), (-k_f) * DFr[...] * Hr[...])
        face_to_all(PHr[...], HOW["h"])
        for e in range(EX):
            Fr[k + 1, e] = Lr[e]

    def total(x):
        x = jnp.sum(x, axis=0, keepdims=True)
        return x[:, : ZF // 2] + x[:, ZF // 2 :]

    def cycle(k, carry):
        pl.when(k > 0)(lambda: finish(k - 1))
        bulk(lambda e: (Dr[e] * inv_center) * Fr[k, e], HOW["a"])
        @pl.when(k > 0)
        def _():
            h = halo(4 * k)
            ph = face_z(DcFr[...] * inv_center * h, HOW["a"])
            FXr[1] = FXr[1] + face_to_face(ph, HOW["a"])
            PHr[...] = ph
            Hr[...] = h

        send_faces(4 * k + 1, FXr[1])

        @pl.when(k > 0)
        def _():
            add_faces(Fr, (k,), Hr[...])
            face_to_all(PHr[...], HOW["a"])

        @pl.when(k == 0)
        def _():
            middle(Lr)
            coarse_setup()

        FFr[k, 0:YF] = Fr[k, 0, 0:YF]
        FFr[k, YF : 2 * YF] = Fr[k, 1, ROWS - YF : ROWS]
        for x in range(XF):
            e, r = x // N, (x % N) * YF
            FFr[k, 2 * YF + x : 2 * YF + x + 1] = Fr[k, e, r : r + 1]
            b = 2 * YF + XF + x
            FFr[k, b : b + 1] = Fr[k, e, r + YF - 1 : r + YF]
        gl = None
        for e in range(EX):
            s = Dr[e] * (a_f * Fr[k, e] - k_f * Lr[e])
            Sr[e] = s
            p = rmul(Cr[e] * s, const["Br"], HOW["b"])
            Ar[e, :, 0:ZC] = rmul(Fr[k, e], const["Bw"], HOW["b"])
            o = lmul(const[f"Gr{e}"], p[:, :ZC], p[:, ZC:], n=HOW["b"])
            gl = o if e == 0 else gl + o
        gl = lmul(const["Gw"], Ar[0, :, 0:ZC], Ar[1, :, 0:ZC], n=HOW["b"]) - gl
        h = halo(4 * k + 1)
        hs = (-k_f) * DcFr[...] * h
        pr = rmul(hs, const["Br"], HOW["b"])
        gl = gl - lmul(const["F2R"], pr[:, :ZC], pr[:, ZC:], n=HOW["b"])
        cs[k] = gl
        coarse(k).start()
        gr[0:OWN] = gl[0:OWN]
        bulk(lambda e: Sr[e], HOW["s"])
        ph = face_z(hs, HOW["s"])
        face_to_all(ph, HOW["s"])
        FXr[1] = FXr[1] + face_to_face(ph, HOW["s"])
        add_faces(Sr, (), (-k_f) * DFr[...] * h)
        coarse(k).arrive()
        gr[OWN:] = cr[k]
        for a, b, n in coarse_pairs():
            t = gr[a : a + n] + gr[b : b + n]
            gr[a : a + n] = t
            gr[b : b + n] = t
        p = lmul(const["Gc"], Cc_r[...] * (Dc_r[...] * inv_center_c) * gr[...], n=HOW["c"])
        o = rmul(jnp.concatenate([p[:OWN], p[OWN:]], 1), const["Bc"], HOW["c"])
        g = gr[0:OWN]
        fix = Dc_r[0:OWN] * (a_c * g - k_c * o)
        p = rmul(Cc_r[0:OWN] * fix, const["Bj"], HOW["d"], slice(0, 2 * ZF))
        o = lmul(const["Gj"], p[:, :ZF], p[:, ZF:], n=HOW["d"], rows=slice(EX * ROWS, EX * ROWS + 96))
        send_faces(4 * k + 2, FXr[1] + o)
        o = lmul(const["Gj"], p[:, :ZF], p[:, ZF:], n=HOW["d"], rows=slice(0, EX * ROWS))
        p = rmul(fix, const["Bj"], HOW["d"], slice(2 * ZF, 3 * ZF))
        up = lmul(const["Gp"], p, n=HOW["d"])
        for e in range(EX):
            part = slice(e * ROWS, (e + 1) * ROWS)
            Sr[e] = Sr[e] + up[part]
            Rr[e] = Fr[k, e] - Lr[e] - o[part]
        bulk(lambda e: (Dr[e] * inv_center) * Rr[e], HOW["e"])
        h = halo(4 * k + 2)
        ph = face_z((-inv_center) * DcFr[...] * h, HOW["e"])
        send_faces(4 * k + 3, FXr[1] + face_to_face(ph, HOW["e"]))
        add_faces(Rr, (), -h)
        face_to_all(ph, HOW["e"])
        for e in range(EX):
            Zr[k, e] = Sr[e] + Dr[e] * (a_f * Rr[e] - k_f * Lr[e])
        bulk(lambda e: Zr[k, e], HOW["f"])
        sums = [0.0] * 3
        for e in range(EX):
            z = Zr[k, e]
            wz = Wr[...] * z
            for i, t in enumerate((Fr[0, e] * wz, Fr[k, e] * wz, WLr[...] * Lr[e] * z)):
                sums[i] = sums[i] + total(t)
        h = halo(4 * k + 3)
        delta = (-k_f) * DFr[...] * h
        ph = face_z((-k_f) * DcFr[...] * h, HOW["h"])
        ff = face_to_face(ph, HOW["h"])
        send_faces(4 * k + 4, FXr[1] + ff)
        wd = WFr[...] * delta
        faces = (FFr[0] * wd, FFr[k] * wd, WLFr[...] * delta * (2.0 * FXr[1] + ff))
        for i, t in enumerate(faces):
            dots[k, i : i + 1] = sums[i] + total(t)
        PHr[...] = ph
        Hr[...] = h
        return carry

    add_faces(Fr, (0,), halo(0))
    lax.fori_loop(0, 2, cycle, 0)

    def reduce_stage(buf, stage, base):
        return [
            pltpu.make_async_remote_copy(
                src_ref=buf.at[0], dst_ref=buf.at[j + 1], send_sem=dsend_sem.at[base + j], recv_sem=drecv_sem.at[base + j],
                device_id=p, device_id_type=MESH,
            )
            for j, p in enumerate(stage)
        ]

    def summed(buf, stage, n):
        for c in stage:
            c.wait_recv()
        out = buf[0]
        for j in range(n):
            out = out + buf[j + 1]
        return out

    d1[0, 0:3] = dots[0, 0:3]
    d1[0, 3:6] = dots[1, 0:3]
    d1[0, 6:8] = jnp.zeros((2, 128), F32)
    stage1 = reduce_stage(d1, stages[0], 0)
    stage2 = reduce_stage(d2, stages[1], len(stage1))
    for c in stage1:
        c.start()
    finish(1)
    d2[0] = summed(d1, stage1, len(stage1))
    for c in stage2:
        c.start()
    h = halo(8)
    add_faces(Fr, (2,), h)
    lanes_sum = jnp.sum(summed(d2, stage2, len(stage2)), axis=1, keepdims=True)
    pick = lambda i: lanes_sum[i : i + 1, 0:1]
    rz0, c00 = pick(1), pick(2)
    r0u, wu, uv = pick(3), pick(4), pick(5)
    alpha0 = rz0 / c00
    rz1 = alpha0 * (alpha0 * wu - r0u)
    beta1 = 1.0 + rz1 / rz0
    curve = beta1 * beta1 * c00 - 2.0 * beta1 * alpha0 * wu + alpha0 * alpha0 * uv
    alpha1 = rz1 / curve
    c_z = alpha0 + alpha1 * beta1
    c_u = alpha1 * alpha0
    for e in range(EX):
        sol_ref[e] = c_z * Zr[0, e] - c_u * Zr[1, e]
        res_ref[e] = jnp.where(Dr[e] > 0.0, Fr[0, e] - c_z * Fr[1, e] + c_u * Fr[2, e], 0.0)

    tile_exchange.drain()
    for c in stage1 + stage2:
        c.wait_send()

    def drain(i, carry):
        fine(i).drain()
        return carry

    lax.fori_loop(0, 9, drain, 0)
    for k in range(2):
        coarse(k).drain()


def solution(mesh):
    gxn, gyn = mesh.shape["gx"], mesh.shape["gy"]
    table = constants()
    names = tuple(table)
    n_dots = gyn - 1 + gxn - 1

    def per_device(right_side, coefficient):
        rhs = right_side.reshape(EX, ROWS, ZF)
        field = (EX, ROWS, ZF)
        vm = lambda *s: pltpu.VMEM(s, F32)
        dma = lambda *s: pltpu.SemaphoreType.DMA(s)
        face = (96, ZF)
        scratch = [pltpu.VMEM(table[m].shape, table[m].dtype) for m in names]
        scratch += [
            vm(3, *field), vm(2, *field), vm(*field), vm(*field), vm(*field), vm(384, ZC), vm(*face), vm(*face),
            vm(*field), vm(*field), vm(*field), vm(*field), vm(2, *face), vm(2, *face), vm(96, 2 * ZF), vm(*face),
            vm(ROWS, ZF), vm(ROWS, ZF), vm(*face), vm(*face),
            vm(384, ZC), vm(384, ZC), vm(8, 128), vm(EX, EY, EZ), vm(80, 128),
            vm(9, 2, YF, ZF), vm(9, 2, EX * N, ZF), vm(9, 2, YF, ZF), vm(9, 2, EX * N, ZF), vm(9, 2, EX * N, ZF),
            vm(2, 192, ZC), vm(2, 256, ZC),
            vm(2, 8, 128), vm(gyn, 8, 128), vm(gxn, 8, 128),
            dma(len(names) + 2), dma(9, 8), dma(9, 8), dma(2, 8), dma(2, 8), dma(8), dma(8), dma(n_dots), dma(n_dots),
        ]
        sol, res = pl.pallas_call(
            functools.partial(kernel_body, (gxn, gyn), names),
            out_shape=[pltpu.VMEM(field, F32)] * 2,
            in_specs=[pl.BlockSpec(memory_space=pl.ANY)] * (2 + len(names)),
            out_specs=[pl.BlockSpec(memory_space=pltpu.VMEM)] * 2,
            scratch_shapes=scratch,
            compiler_params=pltpu.CompilerParams(
                collective_id=0, has_side_effects=True, vmem_limit_bytes=56 * 2**20
            ),
        )(rhs, coefficient, *[jnp.asarray(table[m]) for m in names])
        return sol.reshape(right_side.shape), res.reshape(right_side.shape)

    spec = P("gx", "gy", None)
    return jax.shard_map(
        per_device, mesh=mesh, in_specs=(spec, spec), out_specs=(spec, spec), check_vma=False
    )
```

```python
import functools
import math

import jax
import jax.numpy as jnp
import numpy as np
from jax import lax
from jax.experimental import pallas as pl
from jax.experimental.pallas import tpu as pltpu
from jax.sharding import PartitionSpec as P

ORDER = 7
COARSE_ORDER = 3
F32 = jnp.float32
BF16 = jnp.bfloat16
MESH = pl.DeviceIdType.MESH

EX, EY, EZ = 2, 4, 32
N, NC = ORDER + 1, COARSE_ORDER + 1
YF, ZF = EY * N, EZ * N
YC, ZC = EY * NC, EZ * NC
ROWS = N * YF
ROWS_C = NC * YC


def legendre_pair(degree, points):
    before = points * 0.0 + 1.0
    now = points.copy()
    for power in range(2, degree + 1):
        after = ((2 * power - 1) * points * now - (power - 1) * before) / power
        before = now
        now = after
    return (now, before)


def gll_tables(degree):
    number = degree + 1
    points = np.cos(math.pi * np.arange(number) / degree)
    for newton in range(60):
        top, below = legendre_pair(degree, points)
        points = points - (points * top - below) / (number * top)
    points = points[::-1].copy()
    points[0] = -1.0
    points[degree] = 1.0
    values = legendre_pair(degree, points)[0]
    weights = 2.0 / (degree * (degree + 1) * values**2)
    derivative = np.zeros((number, number))
    for row_index in range(number):
        for column_index in range(number):
            if row_index != column_index:
                derivative[row_index, column_index] = values[row_index] / (
                    values[column_index] * (points[row_index] - points[column_index])
                )
    derivative[0, 0] = -degree * (degree + 1) / 4.0
    derivative[degree, degree] = degree * (degree + 1) / 4.0
    stiffness = derivative.T @ (weights[:, None] * derivative)
    return (points, weights, stiffness)


def upper_bound(degree):
    points, weights, stiffness = gll_tables(degree)
    rowsum = np.abs(stiffness).sum(1)
    diagonal = np.diag(stiffness)
    outer = lambda a, b, c: a[:, None, None] * b[None, :, None] * c[None, None, :]
    top = outer(rowsum, weights, weights) + outer(weights, rowsum, weights) + outer(weights, weights, rowsum)
    bottom = outer(diagonal, weights, weights) + outer(weights, diagonal, weights) + outer(weights, weights, diagonal)
    return float((top / bottom).max())


def interpolation_matrix(fine_degree, coarse_degree):
    fine_points = gll_tables(fine_degree)[0]
    coarse_points = gll_tables(coarse_degree)[0]
    matrix = np.ones((fine_degree + 1, coarse_degree + 1))
    for column_index in range(coarse_degree + 1):
        for other_index in range(coarse_degree + 1):
            if other_index != column_index:
                matrix[:, column_index] *= (fine_points - coarse_points[other_index]) / (
                    coarse_points[column_index] - coarse_points[other_index]
                )
    return matrix


def cheb_numbers(degree):
    upper = upper_bound(degree)
    lower = 0.1 * upper
    center = 0.5 * (upper + lower)
    half = 0.5 * (upper - lower)
    previous = half / center
    current = 1.0 / (2.0 * center / half - previous)
    k = 2.0 * current / half
    return (1.0 / center, (1.0 + current * previous) / center + k, k)


def sum_matrix(elements, number):
    matrix = np.eye(elements * number)
    for e in range(elements - 1):
        a, b = e * number + number - 1, (e + 1) * number
        matrix[a, b] = matrix[b, a] = 1.0
    return matrix


def blocks(count, matrix):
    return np.kron(np.eye(count), matrix)


TERMS = ((0, 0), (1, 0), (0, 1), (2, 0), (0, 2), (1, 1))
HOW = dict(a=3, b=3, s=6, c=3, d=6, e=3, f=6, g=3, h=3)


def pieces_of(matrix, count):
    rest, out = np.asarray(matrix, np.float64), []
    for _ in range(count):
        out.append(rest.astype(np.float32).astype(BF16))
        rest = rest - out[-1].astype(np.float64)
    return out


def right3(matrix, steps="asef"):
    p = pieces_of(matrix, 3)
    return np.concatenate([p[j] for _, j in TERMS[: max(HOW[t] for t in steps)]], 0)


def left3(matrix, steps="asef"):
    p = pieces_of(matrix, 3)
    return np.concatenate([p[j] for _, j in TERMS[: max(HOW[t] for t in steps)]], 1)


def level_matrices(degree):
    _, w, K = gll_tables(degree)
    n = degree + 1
    wy = np.tile(w, EY)
    M0 = np.kron(K, np.diag(wy)) + np.kron(np.diag(w), blocks(EY, K))
    N0 = np.kron(np.diag(w), np.diag(wy))
    return M0, N0, np.diag(np.tile(w, EZ)), blocks(EZ, K)


def face_rows(n):
    y = EY * n
    x = EX * n
    rows = [j for j in range(y)] + [(x - 1) * y + j for j in range(y)]
    rows += [i * y for i in range(x)] + [i * y + y - 1 for i in range(x)]
    return np.array(rows)


def coarse_places():
    XC = EX * NC
    before, after_x, after_y = range(-NC, 0), range(XC, XC + NC), range(YC, YC + NC)
    grids = [(range(XC), range(YC)), (before, range(YC)), (after_x, range(YC)), (range(XC), before), (range(XC), after_y)]
    grids += [(a, b) for a in (before, after_x) for b in (before, after_y)]
    both = [(x, y) for xs, ys in grids for x in xs for y in ys]
    return np.array([p[0] for p in both]), np.array([p[1] for p in both])


def coarse_pairs():
    x, y = coarse_places()
    row = {p: i for i, p in enumerate(zip(x.tolist(), y.tolist()))}
    XC, out = EX * NC, []
    for a, b in ((-1, 0), (XC - 1, XC)):
        for first, n in ((-NC, NC), (0, YC), (YC, NC)):
            out.append((row[a, first], row[b, first], n))
    for a, b in ((-1, 0), (YC - 1, YC)):
        out += [(row[i, a], row[i, b], 1) for i in range(-NC, XC + NC)]
    return out


@functools.cache
def constants():
    J = interpolation_matrix(ORDER, COARSE_ORDER)
    out = {}
    M0, N0, Wz, Kz = level_matrices(ORDER)
    Sz, Szc = sum_matrix(EZ, N), sum_matrix(EZ, NC)
    Sxy = np.kron(sum_matrix(EX, N), sum_matrix(EY, N))
    Sxyc = np.kron(sum_matrix(EX, NC), sum_matrix(EY, NC))
    Mf, Nf = blocks(EX, M0), blocks(EX, N0)
    SM, SN = Sxy @ Mf, Sxy @ Nf
    F = face_rows(N)
    out["Bf"] = right3(np.concatenate([Wz @ Sz, Kz @ Sz], 1))
    _, w, K = gll_tables(ORDER)
    wxy, wz = np.kron(w, np.tile(w, EY)), np.tile(w, EZ)
    out["Mh"] = left3(M0 / wxy[:, None])
    out["Kh"] = right3(Kz / wz[None, :])
    out["w3"] = (wxy[:, None] * wz[None, :]).astype(np.float32)
    y, z = np.arange(ROWS) % YF, np.arange(ZF)
    wide = lambda m, shape: np.broadcast_to(m, shape).astype(np.float32)
    out["yu"] = wide(((y % N == N - 1) & (y != YF - 1))[:, None], (ROWS, 128))
    out["yd"] = wide(((y % N == 0) & (y != 0))[:, None], (ROWS, 128))
    out["zu"] = wide(((z % N == N - 1) & (z != ZF - 1))[None, :], (8, ZF))
    out["zd"] = wide(((z % N == 0) & (z != 0))[None, :], (8, ZF))
    Sy = np.kron(np.eye(EX * N), sum_matrix(EY, N))
    out["Mff"] = left3(blocks(EX, M0 / wxy[:, None])[F][:, F])
    out["Kz1"] = right3((Kz / wz[None, :])[:128, :128])
    out["w3f"] = (np.tile(wxy, EX)[F][:, None] * wz[None, :]).astype(np.float32)
    along = np.concatenate([np.arange(YF), np.arange(YF), np.arange(EX * N), np.arange(EX * N)])
    ends = np.concatenate([np.full(2 * YF, YF), np.full(2 * EX * N, EX * N)])
    out["fu"] = wide(((along % N == N - 1) & (along != ends - 1))[:, None], (96, 128))
    out["fd"] = wide(((along % N == 0) & (along != 0))[:, None], (96, 128))
    for e in range(EX):
        rows = slice(e * ROWS, (e + 1) * ROWS)
        here = np.concatenate([np.arange(e * YF, (e + 1) * YF), np.arange(2 * YF, len(F))])
        keep = ((F[here] // ROWS) == e).astype(float)[None, :]
        full = np.concatenate([(Sy @ Mf)[rows][:, F[here]] * keep, (Sy @ Nf)[rows][:, F[here]] * keep], 1)
        out[f"F2A{e}"] = left3(full)
    Rxy = blocks(EX, np.kron(J.T, blocks(EY, J.T)))
    JZ = blocks(EZ, J)
    XC = EX * NC
    first = [x * YC + y for x in range(XC) for y in range(NC)]
    last = [x * YC + YC - NC + y for x in range(XC) for y in range(NC)]
    selc = np.concatenate([np.arange(XC * YC), first, last]).astype(int)
    RM, RN = (Sxyc @ Rxy @ Mf)[selc], (Sxyc @ Rxy @ Nf)[selc]
    out["Br"] = right3(np.concatenate([Wz @ JZ @ Szc, Kz @ JZ @ Szc], 1), "b")
    for e in range(EX):
        cols = slice(e * ROWS, (e + 1) * ROWS)
        out[f"Gr{e}"] = left3(np.concatenate([RM[:, cols], RN[:, cols]], 1), "b")
    out["F2R"] = left3(np.concatenate([RM[:, F], RN[:, F]], 1), "b")
    inv = lambda count: np.where((np.arange(count) % N == 0) | (np.arange(count) % N == N - 1), 0.5, 1.0)
    Wxy = np.kron(np.diag(inv(EX * N)), np.diag(inv(YF)))
    RW = (Sxyc @ Rxy @ Wxy)[selc]
    out["Bw"] = right3(np.diag(inv(ZF)) @ JZ @ Szc, "b")
    out["Gw"] = left3(RW, "b")
    _, wc, Kc = gll_tables(COARSE_ORDER)
    Wzc, Kzc = np.diag(np.tile(wc, EZ)), blocks(EZ, Kc)
    out["Bc"] = right3(np.concatenate([Wzc @ Szc, Kzc @ Szc], 0), "c")
    cx, cy = coarse_places()
    grid = (cx + NC) * (YC + 2 * NC) + cy + NC
    wx4, wy6 = np.diag(np.tile(wc, EX + 2)), np.diag(np.tile(wc, EY + 2))
    Me = np.kron(blocks(EX + 2, Kc), wy6) + np.kron(wx4, blocks(EY + 2, Kc))
    Ne = np.kron(wx4, wy6)
    Se = np.kron(sum_matrix(EX + 2, NC), sum_matrix(EY + 2, NC))
    own = grid[: XC * YC]
    out["Gc"] = left3(np.concatenate([(Se @ Me)[own][:, grid], (Se @ Ne)[own][:, grid]], 0), "c")
    pick = np.zeros((len(cx), 80))
    for i, (x, y) in enumerate(zip(cx // NC, cy // NC)):
        pick[i, ((x // EX + 1) * 3 + y // EY + 1) * 8 + (x % EX) * EY + y % EY] = 1.0
    out["Pc"] = np.concatenate([pick.astype(np.float32).astype(BF16)] * 3, 1)
    Jxy = blocks(EX, np.kron(J, blocks(EY, J)))
    out["Bj"] = right3(np.concatenate([JZ.T @ Wz @ Sz, JZ.T @ Kz @ Sz, JZ.T], 1), "d")
    out["Bjv"] = right3(np.concatenate([JZ.T @ Wz @ Sz, JZ.T @ Kz @ Sz], 0), "d")
    JM, JN = SM @ Jxy, SN @ Jxy
    out["Gj"] = left3(np.concatenate([JM, JN], 1), "d")
    out["Gjf"] = left3(np.concatenate([JM[F], JN[F]], 0), "d")
    out["Gp"] = left3(Jxy, "d")
    fine_x, fine_y = np.divmod(np.arange(EX * ROWS), YF)
    places = {"f": (np.concatenate([fine_x, F // YF]), np.concatenate([fine_y, F % YF])), "c": (cx, cy)}
    for name, degree in (("f", ORDER), ("c", COARSE_ORDER)):
        n = degree + 1
        _, w, K = gll_tables(degree)
        kd = np.diag(K)
        S = sum_matrix(EZ, n)
        spread_w = np.zeros((128, EZ * n))
        spread_k = np.zeros((128, EZ * n))
        for ez in range(EZ):
            spread_w[ez, ez * n : (ez + 1) * n] = w
            spread_k[ez, ez * n : (ez + 1) * n] = kd
        out["Bd" + name] = right3(np.concatenate([spread_w @ S, spread_k @ S], 1), "g")
        left = np.zeros((len(places[name][0]), 2, 80))
        for i, (x, y) in enumerate(zip(*places[name])):
            xs = [(x // n, x % n)]
            if x % n == 0:
                xs.append((x // n - 1, n - 1))
            if x % n == n - 1:
                xs.append((x // n + 1, 0))
            ys = [(y // n, y % n)]
            if y % n == 0:
                ys.append((y // n - 1, n - 1))
            if y % n == n - 1:
                ys.append((y // n + 1, 0))
            for ex, a in xs:
                for ey, b in ys:
                    col = ((ex // EX + 1) * 3 + ey // EY + 1) * 8 + (ex % EX) * EY + ey % EY
                    left[i, 0, col] += kd[a] * w[b] + w[a] * kd[b]
                    left[i, 1, col] += w[a] * w[b]
        left = left.reshape(len(left), 160)
        if name == "f":
            here = left.reshape(len(left), 2, 80)[: EX * ROWS, :, 32:40].reshape(EX * ROWS, 16)
            out["Gdo"] = left3(here, "g")
            left = left[EX * ROWS :]
        out["Gd" + name] = left3(left, "g")
    spread = np.zeros((128, ZF + ZC))
    for ez in range(EZ):
        spread[ez, ez * N : (ez + 1) * N] = 1.0
        spread[ez, ZF + ez * NC : ZF + (ez + 1) * NC] = 1.0
    out["Bs"] = np.concatenate([spread.astype(np.float32).astype(BF16)] * 3, 0)
    return out


def dot(a, b):
    return jnp.dot(a, b, preferred_element_type=F32)


def split(x, n):
    out = []
    for i in range(1 + max(i for i, _ in TERMS[:n])):
        out.append(x.astype(BF16))
        x = x - out[-1].astype(F32)
    return out


def rmul(x, b, n, cols=slice(None)):
    p = split(x, n)
    x3 = jnp.concatenate([p[i] for i, _ in TERMS[:n]], 1)
    return dot(x3, b[: x3.shape[1], cols])


def lmul(g, *parts, n, rows=slice(None)):
    split_parts = [split(x, n) for x in parts]
    x3 = jnp.concatenate([p[i] for i, _ in TERMS[:n] for p in split_parts], 0)
    return dot(g[rows, : x3.shape[0]], x3)


def kernel_body(shape, names, rhs_ref, coef_ref, *refs):
    gxn, gyn = shape
    n_const = len(names)
    const_hbm = dict(zip(names, refs[:n_const]))
    sol_ref, res_ref = refs[n_const : n_const + 2]
    rest = refs[n_const + 2 :]
    const = dict(zip(names, rest[:n_const]))
    (Fr, Zr, Dr, Cr, W3r, W3Fr, Er, gr, DFr, DcFr, Lr, Sr, Rr, Ar, FXr, FFr, Hr, Wr, WLr, WFr, WLFr,
     Dc_r, Cc_r, cpad, coef, tiles,
     sx, sy, rx, ry, rc, cs, cr, dots, d1, d2,
     const_sem, send_sem, recv_sem, csend_sem, crecv_sem, tsend_sem, trecv_sem, dsend_sem, drecv_sem) = rest[n_const:]

    inv_center, a_f, k_f = cheb_numbers(ORDER)
    inv_center_c, a_c, k_c = cheb_numbers(COARSE_ORDER)
    px, py = lax.axis_index("gx"), lax.axis_index("gy")
    XF, XC, OWN = EX * N, EX * NC, EX * ROWS_C

    def at(dx, dy):
        return (lax.rem(px + dx + gxn, gxn), lax.rem(py + dy + gyn, gyn))

    def inside(dx, dy):
        ok = None
        for p, d, n in ((px, dx, gxn), (py, dy, gyn)):
            if d:
                here = (p > 0) if d < 0 else (p < n - 1)
                ok = here if ok is None else ok & here
        return ok

    corners = [(dx, dy) for dx in (-1, 1) for dy in (-1, 1)]
    around = corners + [(-1, 0), (1, 0), (0, -1), (0, 1)]
    def ring(coarse_n, fine_n, hops):
        every = [(a, b) for a in range(coarse_n) for b in range(fine_n) if (a, b) != (0, 0)]
        near = lambda d, n: min(d, n - d)
        return sorted(every, key=lambda o: -(near(o[0], coarse_n) + hops * near(o[1], fine_n)))

    def shifted(p, fine_n, coarse_n, o):
        return lax.rem(p // fine_n + o[0], coarse_n) * fine_n + lax.rem(lax.rem(p, fine_n) + o[1], fine_n)

    nz = 8 if gxn % 8 == 0 else 2
    nx, ny = gyn // 2, gxn // nz
    stages = [
        [(px, shifted(py, 2, nx, o)) for o in ring(nx, 2, 0.5)],
        [(shifted(px, nz, ny, o), py) for o in ring(ny, nz, 1)],
    ]

    copies = [pltpu.make_async_copy(const_hbm[m], const[m], const_sem.at[i]) for i, m in enumerate(names)]
    load_rhs = pltpu.make_async_copy(rhs_ref, Ar, const_sem.at[n_const])
    load_coef = pltpu.make_async_copy(coef_ref, coef, const_sem.at[n_const + 1])
    load_rhs.start()
    load_coef.start()
    for c in copies:
        c.start()

    for ref in (rx, ry, rc, cr, tiles, cpad):
        ref[...] = jnp.zeros_like(ref)

    barrier = pltpu.get_barrier_semaphore()
    expected = 0
    for d in around:
        pl.when(inside(*d))(
            lambda d=d: pl.semaphore_signal(barrier, inc=1, device_id=at(*d), device_id_type=MESH)
        )
        expected = expected + inside(*d).astype(jnp.int32)
    for stage in stages:
        for p in stage:
            pl.semaphore_signal(barrier, inc=1, device_id=p, device_id_type=MESH)
        expected = expected + len(stage)

    def local_sum(v):
        rows = lax.broadcasted_iota(jnp.int32, v.shape, 0)
        lanes = lax.broadcasted_iota(jnp.int32, v.shape, 1)
        y = lax.rem(rows, YF)
        up = (lax.rem(y, N) == N - 1) & (y != YF - 1)
        down = (lax.rem(y, N) == 0) & (y != 0)
        v = v + jnp.where(up, pltpu.roll(v, ROWS - 1, 0), 0.0) + jnp.where(down, pltpu.roll(v, 1, 0), 0.0)
        up = (lax.rem(lanes, N) == N - 1) & (lanes != ZF - 1)
        down = (lax.rem(lanes, N) == 0) & (lanes != 0)
        return v + jnp.where(up, pltpu.roll(v, ZF - 1, 1), 0.0) + jnp.where(down, pltpu.roll(v, 1, 1), 0.0)

    def middle(ref, *index):
        total = ref[(*index, 0, pl.ds(ROWS - YF, YF))] + ref[(*index, 1, pl.ds(0, YF))]
        ref[(*index, 0, pl.ds(ROWS - YF, YF))] = total
        ref[(*index, 1, pl.ds(0, YF))] = total

    load_coef.wait()
    cpad[0:EY, 0:EZ] = coef[0]
    cpad[EY : 2 * EY, 0:EZ] = coef[1]
    load_rhs.wait()
    for e in range(EX):
        Fr[0, e] = local_sum(Ar[e])
    middle(Fr, 0)
    sx[0, 0] = Fr[0, 0, 0:YF]
    sx[0, 1] = Fr[0, 1, ROWS - YF : ROWS]
    for x in range(XF):
        e, r = x // N, (x % N) * YF
        sy[0, 0, x : x + 1] = Fr[0, e, r : r + 1]
        sy[0, 1, x : x + 1] = Fr[0, e, r + YF - 1 : r + YF]

    class Exchange:
        def __init__(self, plan, send, recv):
            self.plan = [
                (pltpu.make_async_remote_copy(
                    src_ref=s, dst_ref=t, send_sem=send(j), recv_sem=recv(j), device_id=at(*d), device_id_type=MESH,
                ), inside(*d), inside(-d[0], -d[1]))
                for j, (s, t, d) in enumerate(plan)
            ]

        def start(self):
            for c, to, _ in self.plan:
                pl.when(to)(c.start)

        def arrive(self):
            for c, _, come in self.plan:
                pl.when(come)(c.wait_recv)

        def drain(self):
            for c, to, _ in self.plan:
                pl.when(to)(c.wait_send)

    def fine(i):
        one = lambda r: pl.ds(r, 1)
        plan = [
            (sy.at[i, 0, one(0)], rc.at[i, 1, one(XF - 1)], (-1, -1)),
            (sy.at[i, 1, one(0)], rc.at[i, 0, one(XF - 1)], (-1, 1)),
            (sy.at[i, 0, one(XF - 1)], rc.at[i, 1, one(0)], (1, -1)),
            (sy.at[i, 1, one(XF - 1)], rc.at[i, 0, one(0)], (1, 1)),
            (sx.at[i, 0], rx.at[i, 1], (-1, 0)),
            (sx.at[i, 1], rx.at[i, 0], (1, 0)),
            (sy.at[i, 0], ry.at[i, 1], (0, -1)),
            (sy.at[i, 1], ry.at[i, 0], (0, 1)),
        ]
        return Exchange(plan, lambda j: send_sem.at[i, j], lambda j: recv_sem.at[i, j])

    def coarse(k):
        h, q = ROWS_C, NC * NC
        y0, y1 = OWN, OWN + XC * NC
        c0 = 2 * h + 4 * q
        src = lambda a, n: cs.at[k, pl.ds(a, n)]
        dst = lambda a, n: cr.at[k, pl.ds(a, n)]
        plan = [
            (src(y0, q), dst(c0 + 3 * q, q), (-1, -1)),
            (src(y1, q), dst(c0 + 2 * q, q), (-1, 1)),
            (src(y0 + q, q), dst(c0 + q, q), (1, -1)),
            (src(y1 + q, q), dst(c0, q), (1, 1)),
            (src(0, h), dst(h, h), (-1, 0)),
            (src(h, h), dst(0, h), (1, 0)),
            (src(y0, 2 * q), dst(2 * h + 2 * q, 2 * q), (0, -1)),
            (src(y1, 2 * q), dst(2 * h, 2 * q), (0, 1)),
        ]
        return Exchange(plan, lambda j: csend_sem.at[k, j], lambda j: crecv_sem.at[k, j])

    pl.semaphore_wait(barrier, expected)

    tile_plan = []
    for dx, dy in around:
        slot = ((1 - dx) * 3 + (1 - dy)) * 8
        tile_plan.append((cpad, tiles.at[pl.ds(slot, 8)], (dx, dy)))
    tile_exchange = Exchange(tile_plan, lambda j: tsend_sem.at[j], lambda j: trecv_sem.at[j])
    tile_exchange.start()
    fine(0).start()
    tiles[32:40] = cpad[...]

    for c in copies:
        c.wait()

    def spread(x):
        h1 = x.astype(BF16)
        r1 = x - h1.astype(F32)
        h2 = r1.astype(BF16)
        return [h1, h2, (r1 - h2.astype(F32)).astype(BF16)]

    spread_own = dot(jnp.concatenate(spread(cpad[...]), 1), const["Bs"][...])
    for e in range(EX):
        lines = [spread_own[e * EY + ey : e * EY + ey + 1] for ey in range(EY)]
        cf = [jnp.broadcast_to(l[:, :ZF], (N, ZF)) for l in lines]
        one = jnp.concatenate(cf, 0)
        Cr[e] = jnp.concatenate([one] * N, 0)
        W3r[e] = Cr[e] * const["w3"][...]
        FXr[0, e * YF : (e + 1) * YF] = one
        FXr[0, 2 * YF + e * N : 2 * YF + (e + 1) * N] = cf[0]
        FXr[0, 2 * YF + (EX + e) * N : 2 * YF + (EX + e + 1) * N] = cf[EY - 1]

    W3Fr[...] = FXr[0] * const["w3f"][...]

    rows = lax.broadcasted_iota(jnp.int32, (ROWS, ZF), 0)
    lanes = lax.broadcasted_iota(jnp.int32, (ROWS, ZF), 1)
    xr, yr = rows // YF, lax.rem(rows, YF)
    frow = lax.broadcasted_iota(jnp.int32, (96, ZF), 0)
    flane = lax.broadcasted_iota(jnp.int32, (96, ZF), 1)
    fx = jnp.where(frow < YF, 0, jnp.where(frow < 2 * YF, XF - 1, lax.rem(frow, XF)))
    fy = jnp.where(frow < 2 * YF, lax.rem(frow, YF), jnp.where(frow < 2 * YF + XF, 0, YF - 1))

    def edge(i, count=0):
        e = (lax.rem(i, N) == 0) | (lax.rem(i, N) == N - 1)
        return jnp.where(e & (i != 0) & (i != count - 1) if count else e, 0.5, 1.0)

    Wr[...] = edge(lanes) * edge(yr) * edge(xr)
    WLr[...] = edge(lanes) * edge(yr, YF)
    WFr[...] = edge(flane) * edge(fx) * edge(fy)
    WLFr[...] = edge(flane) * edge(fx, XF) * edge(fy, YF)

    def mask_of(x, y, z, n):
        inner = (x > 0) & (x < gxn * EX * n - 1) & (y > 0) & (y < gyn * EY * n - 1)
        return inner & (z != 0) & (z != EZ * n - 1)

    pd = rmul(cpad[...], const["Bdf"], HOW["g"])
    diag = lmul(const["Gdo"], jnp.concatenate([pd[:, :ZF], pd[:, ZF:]], 0), n=HOW["g"])
    for e in range(EX):
        keep = mask_of(px * XF + e * N + xr, py * YF + yr, lanes, N)
        Dr[e] = jnp.where(keep, 1.0 / diag[e * ROWS : (e + 1) * ROWS], 0.0)
    fkeep = mask_of(px * XF + fx, py * YF + fy, flane, N)
    tile_exchange.arrive()
    pd = rmul(tiles[...], const["Bdf"], HOW["g"])
    diag = lmul(const["Gdf"], pd[:, :ZF], pd[:, ZF:], n=HOW["g"])
    df = jnp.where(fkeep, 1.0 / diag, 0.0)
    DFr[...] = df
    DcFr[...] = df * FXr[0]
    Dr[0, 0:YF] = df[0:YF]
    Dr[1, ROWS - YF : ROWS] = df[YF : 2 * YF]
    for x in range(XF):
        e, r = x // N, (x % N) * YF
        Dr[e, r : r + 1] = df[2 * YF + x : 2 * YF + x + 1]
        b = 2 * YF + XF + x
        Dr[e, r + YF - 1 : r + YF] = df[b : b + 1]

    def coarse_setup():
        ext = tiles[...]
        pdc = rmul(ext, const["Bdc"], HOW["g"])
        diag_c = lmul(const["Gdc"], pdc[:, :ZC], pdc[:, ZC:], n=HOW["g"])
        crow = lax.broadcasted_iota(jnp.int32, (384, ZC), 0)
        clane = lax.broadcasted_iota(jnp.int32, (384, ZC), 1)

        def place(r, width, x0, y0):
            return (x0 + r // width, y0 + lax.rem(r, width))

        cx, cy = place(crow, YC, 0, 0)
        base = OWN
        for count, width, x0, y0 in (
            (ROWS_C, YC, -NC, 0), (ROWS_C, YC, XC, 0), (XC * NC, NC, 0, -NC), (XC * NC, NC, 0, YC),
            (16, NC, -NC, -NC), (16, NC, -NC, YC), (16, NC, XC, -NC), (16, NC, XC, YC),
        ):
            nx, ny = place(crow - base, width, x0, y0)
            cx, cy = jnp.where(crow >= base, nx, cx), jnp.where(crow >= base, ny, cy)
            base += count
        keep = mask_of(px * XC + cx, py * YC + cy, clane, NC)
        Dc_r[...] = jnp.where(keep, 1.0 / diag_c, 0.0)
        lines = dot(jnp.concatenate(spread(ext), 1), const["Bs"][:, ZF:])
        Cc_r[...] = dot(const["Pc"][...], jnp.concatenate(spread(lines), 0))

    def halo(i):
        fine(i).arrive()
        return jnp.concatenate([rx[i, 0], rx[i, 1], ry[i, 0] + rc[i, 0], ry[i, 1] + rc[i, 1]], 0)

    def add_faces(ref, index, h):
        ref[(*index, 0, pl.ds(0, YF))] += h[0:YF]
        ref[(*index, 1, pl.ds(ROWS - YF, YF))] += h[YF : 2 * YF]
        for x in range(XF):
            e, r = x // N, (x % N) * YF
            ref[(*index, e, pl.ds(r, 1))] += h[2 * YF + x : 2 * YF + x + 1]
            b = 2 * YF + XF + x
            ref[(*index, e, pl.ds(r + YF - 1, 1))] += h[b : b + 1]

    def sums_inside(v):
        wide = lambda name: jnp.concatenate([const[name][...]] * 2, 1)
        v = v + wide("yu") * pltpu.roll(v, ROWS - 1, 0) + wide("yd") * pltpu.roll(v, 1, 0)
        return v + const["zu"][0:1] * pltpu.roll(v, ZF - 1, 1) + const["zd"][0:1] * pltpu.roll(v, 1, 1)

    def bulk(values, n):
        for e in range(EX):
            p = split(values(e), n)
            p = [p[i] for i, _ in TERMS[:n]]
            t = dot(const["Mh"][:, : n * ROWS], jnp.concatenate(p, 0))
            t = t + dot(jnp.concatenate(p, 1), const["Kh"][: n * ZF])
            Lr[e] = sums_inside(W3r[e] * t)
        FXr[1, 0:YF] = Lr[0, 0:YF]
        FXr[1, YF : 2 * YF] = Lr[1, ROWS - YF : ROWS]
        for side, y in ((2 * YF, 0), (2 * YF + XF, YF - 1)):
            for x in range(XF):
                e, r = x // N, (x % N) * YF + y
                FXr[1, side + x : side + x + 1] = Lr[e, r : r + 1]
            both = Lr[0, ROWS - YF + y : ROWS - YF + y + 1] + Lr[1, y : y + 1]
            FXr[1, side + N - 1 : side + N] = both
            FXr[1, side + N : side + N + 1] = both

    def face_z(hs, n):
        return rmul(hs, const["Bf"], n)

    def send_faces(i, faces):
        sx[i, 0] = faces[0:YF]
        sx[i, 1] = faces[YF : 2 * YF]
        sy[i, 0] = faces[2 * YF : 2 * YF + XF]
        sy[i, 1] = faces[2 * YF + XF :]
        fine(i).start()

    def face_to_face(delta, n):
        p = split(delta, n)
        p = [p[i] for i, _ in TERMS[:n]]
        t = dot(const["Mff"][:, : n * 96], jnp.concatenate(p, 0))
        halves = [jnp.concatenate([q[:, :128], q[:, 128:]], 0) for q in p]
        r = dot(jnp.concatenate(halves, 1), const["Kz1"][: n * 128])
        Er[...] = jnp.concatenate([r[:96], r[96:]], 1)
        for a, b in ((0, 2 * YF), (YF - 1, 2 * YF + XF), (YF, 2 * YF + XF - 1), (2 * YF - 1, 2 * YF + 2 * XF - 1)):
            both = Er[a : a + 1] + Er[b : b + 1]
            Er[a : a + 1] = both
            Er[b : b + 1] = both
        v = W3Fr[...] * (t + Er[...])
        wide = lambda name: jnp.concatenate([const[name][...]] * 2, 1)
        v = v + wide("fu") * pltpu.roll(v, 95, 0) + wide("fd") * pltpu.roll(v, 1, 0)
        return v + const["zu"][0:1] * pltpu.roll(v, ZF - 1, 1) + const["zd"][0:1] * pltpu.roll(v, 1, 1)

    def face_to_all(ph, n):
        for e in range(EX):
            part = jnp.concatenate([ph[e * YF : (e + 1) * YF], ph[2 * YF :]], 0)
            Lr[e] += lmul(const[f"F2A{e}"], part[:, :ZF], part[:, ZF:], n=n)
        middle(Lr)

    def finish(k):
        add_faces(Zr, (k,), (-k_f) * DFr[...] * Hr[...])
        face_to_all(face_z((-k_f) * DcFr[...] * Hr[...], HOW["h"]), HOW["h"])
        for e in range(EX):
            Fr[k + 1, e] = Lr[e]

    def total(x):
        x = jnp.sum(x, axis=0, keepdims=True)
        return x[:, : ZF // 2] + x[:, ZF // 2 :]

    def cycle(k, carry):
        pl.when(k > 0)(lambda: finish(k - 1))
        bulk(lambda e: (Dr[e] * inv_center) * Fr[k, e], HOW["a"])
        @pl.when(k > 0)
        def _():
            h = halo(4 * k)
            FXr[1] = FXr[1] + face_to_face(DFr[...] * inv_center * h, HOW["a"])
            Hr[...] = h

        send_faces(4 * k + 1, FXr[1])

        @pl.when(k > 0)
        def _():
            add_faces(Fr, (k,), Hr[...])
            face_to_all(face_z(DcFr[...] * inv_center * Hr[...], HOW["a"]), HOW["a"])

        @pl.when(k == 0)
        def _():
            middle(Lr)
            coarse_setup()

        FFr[k, 0:YF] = Fr[k, 0, 0:YF]
        FFr[k, YF : 2 * YF] = Fr[k, 1, ROWS - YF : ROWS]
        for x in range(XF):
            e, r = x // N, (x % N) * YF
            FFr[k, 2 * YF + x : 2 * YF + x + 1] = Fr[k, e, r : r + 1]
            b = 2 * YF + XF + x
            FFr[k, b : b + 1] = Fr[k, e, r + YF - 1 : r + YF]
        gl = None
        for e in range(EX):
            s = Dr[e] * (a_f * Fr[k, e] - k_f * Lr[e])
            Sr[e] = s
            p = rmul(Cr[e] * s, const["Br"], HOW["b"])
            Ar[e, :, 0:ZC] = rmul(Fr[k, e], const["Bw"], HOW["b"])
            o = lmul(const[f"Gr{e}"], p[:, :ZC], p[:, ZC:], n=HOW["b"])
            gl = o if e == 0 else gl + o
        gl = lmul(const["Gw"], Ar[0, :, 0:ZC], Ar[1, :, 0:ZC], n=HOW["b"]) - gl
        h = halo(4 * k + 1)
        hs = (-k_f) * DcFr[...] * h
        pr = rmul(hs, const["Br"], HOW["b"])
        gl = gl - lmul(const["F2R"], pr[:, :ZC], pr[:, ZC:], n=HOW["b"])
        cs[k] = gl
        coarse(k).start()
        gr[0:OWN] = gl[0:OWN]
        bulk(lambda e: Sr[e], HOW["s"])
        ph = face_z(hs, HOW["s"])
        face_to_all(ph, HOW["s"])
        FXr[1] = FXr[1] + face_to_face((-k_f) * DFr[...] * h, HOW["s"])
        add_faces(Sr, (), (-k_f) * DFr[...] * h)
        coarse(k).arrive()
        gr[OWN:] = cr[k]
        for a, b, n in coarse_pairs():
            t = gr[a : a + n] + gr[b : b + n]
            gr[a : a + n] = t
            gr[b : b + n] = t
        p = lmul(const["Gc"], Cc_r[...] * (Dc_r[...] * inv_center_c) * gr[...], n=HOW["c"])
        o = rmul(jnp.concatenate([p[:OWN], p[OWN:]], 1), const["Bc"], HOW["c"])
        g = gr[0:OWN]
        fix = Dc_r[0:OWN] * (a_c * g - k_c * o)
        fix_c = Cc_r[0:OWN] * fix
        p = lmul(const["Gjf"], fix_c, n=HOW["d"])
        o = rmul(jnp.concatenate([p[:96], p[96:]], 1), const["Bjv"], HOW["d"])
        send_faces(4 * k + 2, FXr[1] + o)
        p = rmul(fix_c, const["Bj"], HOW["d"], slice(0, 2 * ZF))
        o = lmul(const["Gj"], p[:, :ZF], p[:, ZF:], n=HOW["d"])
        p = rmul(fix, const["Bj"], HOW["d"], slice(2 * ZF, 3 * ZF))
        up = lmul(const["Gp"], p, n=HOW["d"])
        for e in range(EX):
            part = slice(e * ROWS, (e + 1) * ROWS)
            Sr[e] = Sr[e] + up[part]
            Rr[e] = Fr[k, e] - Lr[e] - o[part]
        bulk(lambda e: (Dr[e] * inv_center) * Rr[e], HOW["e"])
        h = halo(4 * k + 2)
        send_faces(4 * k + 3, FXr[1] + face_to_face((-inv_center) * DFr[...] * h, HOW["e"]))
        add_faces(Rr, (), -h)
        face_to_all(face_z((-inv_center) * DcFr[...] * h, HOW["e"]), HOW["e"])
        for e in range(EX):
            Zr[k, e] = Sr[e] + Dr[e] * (a_f * Rr[e] - k_f * Lr[e])
        bulk(lambda e: Zr[k, e], HOW["f"])
        sums = [0.0] * 3
        for e in range(EX):
            z = Zr[k, e]
            wz = Wr[...] * z
            for i, t in enumerate((Fr[0, e] * wz, Fr[k, e] * wz, WLr[...] * Lr[e] * z)):
                sums[i] = sums[i] + total(t)
        h = halo(4 * k + 3)
        delta = (-k_f) * DFr[...] * h
        ff = face_to_face(delta, HOW["h"])
        send_faces(4 * k + 4, FXr[1] + ff)
        wd = WFr[...] * delta
        faces = (FFr[0] * wd, FFr[k] * wd, WLFr[...] * delta * (2.0 * FXr[1] + ff))
        for i, t in enumerate(faces):
            dots[k, i : i + 1] = sums[i] + total(t)
        Hr[...] = h
        return carry

    add_faces(Fr, (0,), halo(0))
    lax.fori_loop(0, 2, cycle, 0)

    def reduce_stage(buf, stage, base):
        return [
            pltpu.make_async_remote_copy(
                src_ref=buf.at[0], dst_ref=buf.at[j + 1], send_sem=dsend_sem.at[base + j], recv_sem=drecv_sem.at[base + j],
                device_id=p, device_id_type=MESH,
            )
            for j, p in enumerate(stage)
        ]

    def summed(buf, stage, n):
        for c in stage:
            c.wait_recv()
        out = buf[0]
        for j in range(n):
            out = out + buf[j + 1]
        return out

    d1[0, 0:3] = dots[0, 0:3]
    d1[0, 3:6] = dots[1, 0:3]
    d1[0, 6:8] = jnp.zeros((2, 128), F32)
    stage1 = reduce_stage(d1, stages[0], 0)
    stage2 = reduce_stage(d2, stages[1], len(stage1))
    for c in stage1:
        c.start()
    finish(1)
    d2[0] = summed(d1, stage1, len(stage1))
    for c in stage2:
        c.start()
    h = halo(8)
    add_faces(Fr, (2,), h)
    lanes_sum = jnp.sum(summed(d2, stage2, len(stage2)), axis=1, keepdims=True)
    pick = lambda i: lanes_sum[i : i + 1, 0:1]
    rz0, c00 = pick(1), pick(2)
    r0u, wu, uv = pick(3), pick(4), pick(5)
    alpha0 = rz0 / c00
    rz1 = alpha0 * (alpha0 * wu - r0u)
    beta1 = 1.0 + rz1 / rz0
    curve = beta1 * beta1 * c00 - 2.0 * beta1 * alpha0 * wu + alpha0 * alpha0 * uv
    alpha1 = rz1 / curve
    c_z = alpha0 + alpha1 * beta1
    c_u = alpha1 * alpha0
    for e in range(EX):
        sol_ref[e] = c_z * Zr[0, e] - c_u * Zr[1, e]
        res_ref[e] = jnp.where(Dr[e] > 0.0, Fr[0, e] - c_z * Fr[1, e] + c_u * Fr[2, e], 0.0)

    tile_exchange.drain()
    for c in stage1 + stage2:
        c.wait_send()

    def drain(i, carry):
        fine(i).drain()
        return carry

    lax.fori_loop(0, 9, drain, 0)
    for k in range(2):
        coarse(k).drain()


def store(sol_ref, res_ref, sol_out, res_out, sem):
    pairs = [(a.at[e], b.at[e]) for e in range(EX) for a, b in ((sol_ref, sol_out), (res_ref, res_out))]
    copies = [pltpu.make_async_copy(a, b, sem.at[i]) for i, (a, b) in enumerate(pairs)]
    for c in copies:
        c.start()
    for c in copies:
        c.wait()


def solution(mesh):
    gxn, gyn = mesh.shape["gx"], mesh.shape["gy"]
    table = constants()
    names = tuple(table)
    n_dots = gyn - 1 + gxn - 1

    def per_device(right_side, coefficient):
        rhs = right_side.reshape(EX, ROWS, ZF)
        field = (EX, ROWS, ZF)
        vm = lambda *s: pltpu.VMEM(s, F32)
        dma = lambda *s: pltpu.SemaphoreType.DMA(s)
        face = (96, ZF)
        scratch = [pltpu.VMEM(table[m].shape, table[m].dtype) for m in names]
        scratch += [
            vm(3, *field), vm(2, *field), vm(*field), vm(*field), vm(*field), vm(*face), vm(*face), vm(384, ZC), vm(*face), vm(*face),
            vm(*field), vm(*field), vm(*field), vm(*field), vm(2, *face), vm(2, *face), vm(*face),
            vm(ROWS, ZF), vm(ROWS, ZF), vm(*face), vm(*face),
            vm(384, ZC), vm(384, ZC), vm(8, 128), vm(EX, EY, EZ), vm(80, 128),
            vm(9, 2, YF, ZF), vm(9, 2, EX * N, ZF), vm(9, 2, YF, ZF), vm(9, 2, EX * N, ZF), vm(9, 2, EX * N, ZF),
            vm(2, 192, ZC), vm(2, 256, ZC),
            vm(2, 8, 128), vm(gyn, 8, 128), vm(gxn, 8, 128),
            dma(len(names) + 2), dma(9, 8), dma(9, 8), dma(2, 8), dma(2, 8), dma(8), dma(8), dma(n_dots), dma(n_dots),
        ]
        sol, res = pl.pallas_call(
            functools.partial(kernel_body, (gxn, gyn), names),
            out_shape=[pltpu.VMEM(field, F32)] * 2,
            in_specs=[pl.BlockSpec(memory_space=pl.ANY)] * (2 + len(names)),
            out_specs=[pl.BlockSpec(memory_space=pltpu.VMEM)] * 2,
            scratch_shapes=scratch,
            compiler_params=pltpu.CompilerParams(
                collective_id=0, has_side_effects=True, vmem_limit_bytes=56 * 2**20
            ),
        )(rhs, coefficient, *[jnp.asarray(table[m]) for m in names])
        sol, res = pl.pallas_call(
            store,
            out_shape=[jax.ShapeDtypeStruct(field, F32)] * 2,
            in_specs=[pl.BlockSpec(memory_space=pltpu.VMEM)] * 2,
            out_specs=[pl.BlockSpec(memory_space=pl.ANY)] * 2,
            scratch_shapes=[pltpu.SemaphoreType.DMA((4,))],
        )(sol, res)
        return sol.reshape(right_side.shape), res.reshape(right_side.shape)

    spec = P("gx", "gy", None)
    return jax.shard_map(
        per_device, mesh=mesh, in_specs=(spec, spec), out_specs=(spec, spec), check_vma=False
    )
```

```python
import functools
import math

import jax
import jax.numpy as jnp
import numpy as np
from jax import lax
from jax.experimental import pallas as pl
from jax.experimental.pallas import tpu as pltpu
from jax.sharding import PartitionSpec as P

ORDER = 7
COARSE_ORDER = 3
F32 = jnp.float32
BF16 = jnp.bfloat16
MESH = pl.DeviceIdType.MESH

EX, EY, EZ = 2, 4, 32
N, NC = ORDER + 1, COARSE_ORDER + 1
YF, ZF = EY * N, EZ * N
YC, ZC = EY * NC, EZ * NC
ROWS = N * YF
ROWS_C = NC * YC


def legendre_pair(degree, points):
    before = points * 0.0 + 1.0
    now = points.copy()
    for power in range(2, degree + 1):
        after = ((2 * power - 1) * points * now - (power - 1) * before) / power
        before = now
        now = after
    return (now, before)


def gll_tables(degree):
    number = degree + 1
    points = np.cos(math.pi * np.arange(number) / degree)
    for newton in range(60):
        top, below = legendre_pair(degree, points)
        points = points - (points * top - below) / (number * top)
    points = points[::-1].copy()
    points[0] = -1.0
    points[degree] = 1.0
    values = legendre_pair(degree, points)[0]
    weights = 2.0 / (degree * (degree + 1) * values**2)
    derivative = np.zeros((number, number))
    for row_index in range(number):
        for column_index in range(number):
            if row_index != column_index:
                derivative[row_index, column_index] = values[row_index] / (
                    values[column_index] * (points[row_index] - points[column_index])
                )
    derivative[0, 0] = -degree * (degree + 1) / 4.0
    derivative[degree, degree] = degree * (degree + 1) / 4.0
    stiffness = derivative.T @ (weights[:, None] * derivative)
    return (points, weights, stiffness)


def upper_bound(degree):
    points, weights, stiffness = gll_tables(degree)
    rowsum = np.abs(stiffness).sum(1)
    diagonal = np.diag(stiffness)
    outer = lambda a, b, c: a[:, None, None] * b[None, :, None] * c[None, None, :]
    top = outer(rowsum, weights, weights) + outer(weights, rowsum, weights) + outer(weights, weights, rowsum)
    bottom = outer(diagonal, weights, weights) + outer(weights, diagonal, weights) + outer(weights, weights, diagonal)
    return float((top / bottom).max())


def interpolation_matrix(fine_degree, coarse_degree):
    fine_points = gll_tables(fine_degree)[0]
    coarse_points = gll_tables(coarse_degree)[0]
    matrix = np.ones((fine_degree + 1, coarse_degree + 1))
    for column_index in range(coarse_degree + 1):
        for other_index in range(coarse_degree + 1):
            if other_index != column_index:
                matrix[:, column_index] *= (fine_points - coarse_points[other_index]) / (
                    coarse_points[column_index] - coarse_points[other_index]
                )
    return matrix


def cheb_numbers(degree):
    upper = upper_bound(degree)
    lower = 0.1 * upper
    center = 0.5 * (upper + lower)
    half = 0.5 * (upper - lower)
    previous = half / center
    current = 1.0 / (2.0 * center / half - previous)
    k = 2.0 * current / half
    return (1.0 / center, (1.0 + current * previous) / center + k, k)


def sum_matrix(elements, number):
    matrix = np.eye(elements * number)
    for e in range(elements - 1):
        a, b = e * number + number - 1, (e + 1) * number
        matrix[a, b] = matrix[b, a] = 1.0
    return matrix


def blocks(count, matrix):
    return np.kron(np.eye(count), matrix)


TERMS = ((0, 0), (1, 0), (0, 1), (2, 0), (0, 2), (1, 1))
HOW = dict(a=3, b=3, s=6, c=3, d=6, e=3, f=6, g=3, h=3)


def pieces_of(matrix, count):
    rest, out = np.asarray(matrix, np.float64), []
    for _ in range(count):
        out.append(rest.astype(np.float32).astype(BF16))
        rest = rest - out[-1].astype(np.float64)
    return out


def right3(matrix, steps="asef"):
    p = pieces_of(matrix, 3)
    return np.concatenate([p[j] for _, j in TERMS[: max(HOW[t] for t in steps)]], 0)


def left3(matrix, steps="asef"):
    p = pieces_of(matrix, 3)
    return np.concatenate([p[j] for _, j in TERMS[: max(HOW[t] for t in steps)]], 1)


def level_matrices(degree):
    _, w, K = gll_tables(degree)
    n = degree + 1
    wy = np.tile(w, EY)
    M0 = np.kron(K, np.diag(wy)) + np.kron(np.diag(w), blocks(EY, K))
    N0 = np.kron(np.diag(w), np.diag(wy))
    return M0, N0, np.diag(np.tile(w, EZ)), blocks(EZ, K)


def face_rows(n):
    y = EY * n
    x = EX * n
    rows = [j for j in range(y)] + [(x - 1) * y + j for j in range(y)]
    rows += [i * y for i in range(x)] + [i * y + y - 1 for i in range(x)]
    return np.array(rows)


def coarse_places():
    XC = EX * NC
    before, after_x, after_y = range(-NC, 0), range(XC, XC + NC), range(YC, YC + NC)
    grids = [(range(XC), range(YC)), (before, range(YC)), (after_x, range(YC)), (range(XC), before), (range(XC), after_y)]
    grids += [(a, b) for a in (before, after_x) for b in (before, after_y)]
    both = [(x, y) for xs, ys in grids for x in xs for y in ys]
    return np.array([p[0] for p in both]), np.array([p[1] for p in both])


def coarse_pairs():
    x, y = coarse_places()
    row = {p: i for i, p in enumerate(zip(x.tolist(), y.tolist()))}
    XC, out = EX * NC, []
    for a, b in ((-1, 0), (XC - 1, XC)):
        for first, n in ((-NC, NC), (0, YC), (YC, NC)):
            out.append((row[a, first], row[b, first], n))
    for a, b in ((-1, 0), (YC - 1, YC)):
        out += [(row[i, a], row[i, b], 1) for i in range(-NC, XC + NC)]
    return out


@functools.cache
def constants():
    J = interpolation_matrix(ORDER, COARSE_ORDER)
    out = {}
    M0, N0, Wz, Kz = level_matrices(ORDER)
    Sz, Szc = sum_matrix(EZ, N), sum_matrix(EZ, NC)
    Sxy = np.kron(sum_matrix(EX, N), sum_matrix(EY, N))
    Sxyc = np.kron(sum_matrix(EX, NC), sum_matrix(EY, NC))
    Mf, Nf = blocks(EX, M0), blocks(EX, N0)
    SM, SN = Sxy @ Mf, Sxy @ Nf
    F = face_rows(N)
    out["Bf"] = right3(np.concatenate([Wz @ Sz, Kz @ Sz], 1))
    _, w, K = gll_tables(ORDER)
    wxy, wz = np.kron(w, np.tile(w, EY)), np.tile(w, EZ)
    out["Mh"] = left3(M0 / wxy[:, None])
    out["Kh"] = right3(Kz / wz[None, :])
    out["w3"] = (wxy[:, None] * wz[None, :]).astype(np.float32)
    y, z = np.arange(ROWS) % YF, np.arange(ZF)
    wide = lambda m, shape: np.broadcast_to(m, shape).astype(np.float32)
    out["yu"] = wide(((y % N == N - 1) & (y != YF - 1))[:, None], (ROWS, 128))
    out["yd"] = wide(((y % N == 0) & (y != 0))[:, None], (ROWS, 128))
    out["zu"] = wide(((z % N == N - 1) & (z != ZF - 1))[None, :], (8, ZF))
    out["zd"] = wide(((z % N == 0) & (z != 0))[None, :], (8, ZF))
    Sy = np.kron(np.eye(EX * N), sum_matrix(EY, N))
    out["Mff"] = left3(blocks(EX, M0 / wxy[:, None])[F][:, F])
    out["Kz1"] = right3((Kz / wz[None, :])[:128, :128])
    out["w3f"] = (np.tile(wxy, EX)[F][:, None] * wz[None, :]).astype(np.float32)
    along = np.concatenate([np.arange(YF), np.arange(YF), np.arange(EX * N), np.arange(EX * N)])
    ends = np.concatenate([np.full(2 * YF, YF), np.full(2 * EX * N, EX * N)])
    out["fu"] = wide(((along % N == N - 1) & (along != ends - 1))[:, None], (96, 128))
    out["fd"] = wide(((along % N == 0) & (along != 0))[:, None], (96, 128))
    for e in range(EX):
        rows = slice(e * ROWS, (e + 1) * ROWS)
        here = np.concatenate([np.arange(e * YF, (e + 1) * YF), np.arange(2 * YF, len(F))])
        keep = ((F[here] // ROWS) == e).astype(float)[None, :]
        full = np.concatenate([(Sy @ Mf)[rows][:, F[here]] * keep, (Sy @ Nf)[rows][:, F[here]] * keep], 1)
        out[f"F2A{e}"] = left3(full)
    Rxy = blocks(EX, np.kron(J.T, blocks(EY, J.T)))
    JZ = blocks(EZ, J)
    XC = EX * NC
    first = [x * YC + y for x in range(XC) for y in range(NC)]
    last = [x * YC + YC - NC + y for x in range(XC) for y in range(NC)]
    selc = np.concatenate([np.arange(XC * YC), first, last]).astype(int)
    RM, RN = (Sxyc @ Rxy @ Mf)[selc], (Sxyc @ Rxy @ Nf)[selc]
    out["Br"] = right3(np.concatenate([Wz @ JZ @ Szc, Kz @ JZ @ Szc], 1), "b")
    for e in range(EX):
        cols = slice(e * ROWS, (e + 1) * ROWS)
        out[f"Gr{e}"] = left3(np.concatenate([RM[:, cols], RN[:, cols]], 1), "b")
    out["F2R"] = left3(np.concatenate([RM[:, F], RN[:, F]], 1), "b")
    inv = lambda count: np.where((np.arange(count) % N == 0) | (np.arange(count) % N == N - 1), 0.5, 1.0)
    Wxy = np.kron(np.diag(inv(EX * N)), np.diag(inv(YF)))
    RW = (Sxyc @ Rxy @ Wxy)[selc]
    out["Bw"] = right3(np.diag(inv(ZF)) @ JZ @ Szc, "b")
    out["Gw"] = left3(RW, "b")
    _, wc, Kc = gll_tables(COARSE_ORDER)
    Wzc, Kzc = np.diag(np.tile(wc, EZ)), blocks(EZ, Kc)
    out["Bc"] = right3(np.concatenate([Wzc @ Szc, Kzc @ Szc], 0), "c")
    cx, cy = coarse_places()
    grid = (cx + NC) * (YC + 2 * NC) + cy + NC
    wx4, wy6 = np.diag(np.tile(wc, EX + 2)), np.diag(np.tile(wc, EY + 2))
    Me = np.kron(blocks(EX + 2, Kc), wy6) + np.kron(wx4, blocks(EY + 2, Kc))
    Ne = np.kron(wx4, wy6)
    Se = np.kron(sum_matrix(EX + 2, NC), sum_matrix(EY + 2, NC))
    own = grid[: XC * YC]
    out["Gc"] = left3(np.concatenate([(Se @ Me)[own][:, grid], (Se @ Ne)[own][:, grid]], 0), "c")
    pick = np.zeros((len(cx), 80))
    for i, (x, y) in enumerate(zip(cx // NC, cy // NC)):
        pick[i, ((x // EX + 1) * 3 + y // EY + 1) * 8 + (x % EX) * EY + y % EY] = 1.0
    out["Pc"] = np.concatenate([pick.astype(np.float32).astype(BF16)] * 3, 1)
    Jxy = blocks(EX, np.kron(J, blocks(EY, J)))
    out["Bj"] = right3(np.concatenate([JZ.T @ Wz @ Sz, JZ.T @ Kz @ Sz, JZ.T], 1), "d")
    out["Bjv"] = right3(np.concatenate([JZ.T @ Wz @ Sz, JZ.T @ Kz @ Sz], 0), "d")
    JM, JN = SM @ Jxy, SN @ Jxy
    out["Gj"] = left3(np.concatenate([JM, JN], 1), "d")
    out["Gjf"] = left3(np.concatenate([JM[F], JN[F]], 0), "d")
    out["Gp"] = left3(Jxy, "d")
    fine_x, fine_y = np.divmod(np.arange(EX * ROWS), YF)
    places = {"f": (np.concatenate([fine_x, F // YF]), np.concatenate([fine_y, F % YF])), "c": (cx, cy)}
    for name, degree in (("f", ORDER), ("c", COARSE_ORDER)):
        n = degree + 1
        _, w, K = gll_tables(degree)
        kd = np.diag(K)
        S = sum_matrix(EZ, n)
        spread_w = np.zeros((128, EZ * n))
        spread_k = np.zeros((128, EZ * n))
        for ez in range(EZ):
            spread_w[ez, ez * n : (ez + 1) * n] = w
            spread_k[ez, ez * n : (ez + 1) * n] = kd
        out["Bd" + name] = right3(np.concatenate([spread_w @ S, spread_k @ S], 1), "g")
        left = np.zeros((len(places[name][0]), 2, 80))
        for i, (x, y) in enumerate(zip(*places[name])):
            xs = [(x // n, x % n)]
            if x % n == 0:
                xs.append((x // n - 1, n - 1))
            if x % n == n - 1:
                xs.append((x // n + 1, 0))
            ys = [(y // n, y % n)]
            if y % n == 0:
                ys.append((y // n - 1, n - 1))
            if y % n == n - 1:
                ys.append((y // n + 1, 0))
            for ex, a in xs:
                for ey, b in ys:
                    col = ((ex // EX + 1) * 3 + ey // EY + 1) * 8 + (ex % EX) * EY + ey % EY
                    left[i, 0, col] += kd[a] * w[b] + w[a] * kd[b]
                    left[i, 1, col] += w[a] * w[b]
        left = left.reshape(len(left), 160)
        if name == "f":
            here = left.reshape(len(left), 2, 80)[: EX * ROWS, :, 32:40].reshape(EX * ROWS, 16)
            out["Gdo"] = left3(here, "g")
            left = left[EX * ROWS :]
        out["Gd" + name] = left3(left, "g")
    spread = np.zeros((128, ZF + ZC))
    for ez in range(EZ):
        spread[ez, ez * N : (ez + 1) * N] = 1.0
        spread[ez, ZF + ez * NC : ZF + (ez + 1) * NC] = 1.0
    out["Bs"] = np.concatenate([spread.astype(np.float32).astype(BF16)] * 3, 0)
    return out


def dot(a, b):
    return jnp.dot(a, b, preferred_element_type=F32)


def split(x, n):
    out = []
    for i in range(1 + max(i for i, _ in TERMS[:n])):
        out.append(x.astype(BF16))
        x = x - out[-1].astype(F32)
    return out


def rmul(x, b, n, cols=slice(None)):
    p = split(x, n)
    x3 = jnp.concatenate([p[i] for i, _ in TERMS[:n]], 1)
    return dot(x3, b[: x3.shape[1], cols])


def lmul(g, *parts, n, rows=slice(None)):
    split_parts = [split(x, n) for x in parts]
    x3 = jnp.concatenate([p[i] for i, _ in TERMS[:n] for p in split_parts], 0)
    return dot(g[rows, : x3.shape[0]], x3)


def kernel_body(shape, names, rhs_ref, coef_ref, *refs):
    gxn, gyn = shape
    n_const = len(names)
    const_hbm = dict(zip(names, refs[:n_const]))
    sol_ref, res_ref = refs[n_const : n_const + 2]
    rest = refs[n_const + 2 :]
    const = dict(zip(names, rest[:n_const]))
    (Fr, Zr, Dr, Cr, W3r, W3Fr, Er, gr, DFr, DcFr, Lr, Sr, Rr, Ar, FXr, FFr, Hr, Wr, WLr, WFr, WLFr,
     Dc_r, Cc_r, cpad, coef, tiles,
     sx, sy, rx, ry, rc, cs, cr, dots, d1, d2,
     const_sem, send_sem, recv_sem, csend_sem, crecv_sem, tsend_sem, trecv_sem, dsend_sem, drecv_sem) = rest[n_const:]

    inv_center, a_f, k_f = cheb_numbers(ORDER)
    inv_center_c, a_c, k_c = cheb_numbers(COARSE_ORDER)
    px, py = lax.axis_index("gx"), lax.axis_index("gy")
    XF, XC, OWN = EX * N, EX * NC, EX * ROWS_C

    def at(dx, dy):
        return (lax.rem(px + dx + gxn, gxn), lax.rem(py + dy + gyn, gyn))

    def inside(dx, dy):
        ok = None
        for p, d, n in ((px, dx, gxn), (py, dy, gyn)):
            if d:
                here = (p > 0) if d < 0 else (p < n - 1)
                ok = here if ok is None else ok & here
        return ok

    corners = [(dx, dy) for dx in (-1, 1) for dy in (-1, 1)]
    around = corners + [(-1, 0), (1, 0), (0, -1), (0, 1)]
    def ring(coarse_n, fine_n, hops):
        every = [(a, b) for a in range(coarse_n) for b in range(fine_n) if (a, b) != (0, 0)]
        near = lambda d, n: min(d, n - d)
        return sorted(every, key=lambda o: -(near(o[0], coarse_n) + hops * near(o[1], fine_n)))

    def shifted(p, fine_n, coarse_n, o):
        return lax.rem(p // fine_n + o[0], coarse_n) * fine_n + lax.rem(lax.rem(p, fine_n) + o[1], fine_n)

    nz = 8 if gxn % 8 == 0 else 2
    nx, ny = gyn // 2, gxn // nz
    stages = [
        [(px, shifted(py, 2, nx, o)) for o in ring(nx, 2, 0.5)],
        [(shifted(px, nz, ny, o), py) for o in ring(ny, nz, 1)],
    ]

    copies = [pltpu.make_async_copy(const_hbm[m], const[m], const_sem.at[i]) for i, m in enumerate(names)]
    load_rhs = pltpu.make_async_copy(rhs_ref, Ar, const_sem.at[n_const])
    load_coef = pltpu.make_async_copy(coef_ref, coef, const_sem.at[n_const + 1])
    load_rhs.start()
    load_coef.start()
    for c in copies:
        c.start()

    for ref in (rx, ry, rc, cr, tiles, cpad):
        ref[...] = jnp.zeros_like(ref)

    barrier = pltpu.get_barrier_semaphore()
    expected = 0
    for d in around:
        pl.when(inside(*d))(
            lambda d=d: pl.semaphore_signal(barrier, inc=1, device_id=at(*d), device_id_type=MESH)
        )
        expected = expected + inside(*d).astype(jnp.int32)
    for stage in stages:
        for p in stage:
            pl.semaphore_signal(barrier, inc=1, device_id=p, device_id_type=MESH)
        expected = expected + len(stage)

    def local_sum(v):
        rows = lax.broadcasted_iota(jnp.int32, v.shape, 0)
        lanes = lax.broadcasted_iota(jnp.int32, v.shape, 1)
        y = lax.rem(rows, YF)
        up = (lax.rem(y, N) == N - 1) & (y != YF - 1)
        down = (lax.rem(y, N) == 0) & (y != 0)
        v = v + jnp.where(up, pltpu.roll(v, ROWS - 1, 0), 0.0) + jnp.where(down, pltpu.roll(v, 1, 0), 0.0)
        up = (lax.rem(lanes, N) == N - 1) & (lanes != ZF - 1)
        down = (lax.rem(lanes, N) == 0) & (lanes != 0)
        return v + jnp.where(up, pltpu.roll(v, ZF - 1, 1), 0.0) + jnp.where(down, pltpu.roll(v, 1, 1), 0.0)

    def middle(ref, *index):
        total = ref[(*index, 0, pl.ds(ROWS - YF, YF))] + ref[(*index, 1, pl.ds(0, YF))]
        ref[(*index, 0, pl.ds(ROWS - YF, YF))] = total
        ref[(*index, 1, pl.ds(0, YF))] = total

    load_coef.wait()
    cpad[0:EY, 0:EZ] = coef[0]
    cpad[EY : 2 * EY, 0:EZ] = coef[1]
    load_rhs.wait()
    for e in range(EX):
        Fr[0, e] = local_sum(Ar[e])
    middle(Fr, 0)
    sx[0, 0] = Fr[0, 0, 0:YF]
    sx[0, 1] = Fr[0, 1, ROWS - YF : ROWS]
    for x in range(XF):
        e, r = x // N, (x % N) * YF
        sy[0, 0, x : x + 1] = Fr[0, e, r : r + 1]
        sy[0, 1, x : x + 1] = Fr[0, e, r + YF - 1 : r + YF]

    interior = inside(-1, -1) & inside(1, 1)

    class Exchange:
        def __init__(self, plan, send, recv):
            self.plan = [
                (pltpu.make_async_remote_copy(
                    src_ref=s, dst_ref=t, send_sem=send(j), recv_sem=recv(j), device_id=at(*d), device_id_type=MESH,
                ), inside(*d), inside(-d[0], -d[1]))
                for j, (s, t, d) in enumerate(plan)
            ]

        def start(self):
            @pl.when(interior)
            def _():
                for c, _, _ in self.plan:
                    c.start()

            @pl.when(~interior)
            def _():
                for c, to, _ in self.plan:
                    pl.when(to)(c.start)

        def arrive(self):
            @pl.when(interior)
            def _():
                for c, _, _ in self.plan:
                    c.wait_recv()

            @pl.when(~interior)
            def _():
                for c, _, come in self.plan:
                    pl.when(come)(c.wait_recv)

        def drain(self):
            for c, to, _ in self.plan:
                pl.when(to)(c.wait_send)

    def fine(i):
        one = lambda r: pl.ds(r, 1)
        plan = [
            (sy.at[i, 0, one(0)], rc.at[i, 1, one(XF - 1)], (-1, -1)),
            (sy.at[i, 1, one(0)], rc.at[i, 0, one(XF - 1)], (-1, 1)),
            (sy.at[i, 0, one(XF - 1)], rc.at[i, 1, one(0)], (1, -1)),
            (sy.at[i, 1, one(XF - 1)], rc.at[i, 0, one(0)], (1, 1)),
            (sx.at[i, 0], rx.at[i, 1], (-1, 0)),
            (sx.at[i, 1], rx.at[i, 0], (1, 0)),
            (sy.at[i, 0], ry.at[i, 1], (0, -1)),
            (sy.at[i, 1], ry.at[i, 0], (0, 1)),
        ]
        return Exchange(plan, lambda j: send_sem.at[i, j], lambda j: recv_sem.at[i, j])

    def coarse(k):
        h, q = ROWS_C, NC * NC
        y0, y1 = OWN, OWN + XC * NC
        c0 = 2 * h + 4 * q
        src = lambda a, n: cs.at[k, pl.ds(a, n)]
        dst = lambda a, n: cr.at[k, pl.ds(a, n)]
        plan = [
            (src(y0, q), dst(c0 + 3 * q, q), (-1, -1)),
            (src(y1, q), dst(c0 + 2 * q, q), (-1, 1)),
            (src(y0 + q, q), dst(c0 + q, q), (1, -1)),
            (src(y1 + q, q), dst(c0, q), (1, 1)),
            (src(0, h), dst(h, h), (-1, 0)),
            (src(h, h), dst(0, h), (1, 0)),
            (src(y0, 2 * q), dst(2 * h + 2 * q, 2 * q), (0, -1)),
            (src(y1, 2 * q), dst(2 * h, 2 * q), (0, 1)),
        ]
        return Exchange(plan, lambda j: csend_sem.at[k, j], lambda j: crecv_sem.at[k, j])

    pl.semaphore_wait(barrier, expected)

    tile_plan = []
    for dx, dy in around:
        slot = ((1 - dx) * 3 + (1 - dy)) * 8
        tile_plan.append((cpad, tiles.at[pl.ds(slot, 8)], (dx, dy)))
    tile_exchange = Exchange(tile_plan, lambda j: tsend_sem.at[j], lambda j: trecv_sem.at[j])
    tile_exchange.start()
    fine(0).start()
    tiles[32:40] = cpad[...]

    for c in copies:
        c.wait()

    def spread(x):
        h1 = x.astype(BF16)
        r1 = x - h1.astype(F32)
        h2 = r1.astype(BF16)
        return [h1, h2, (r1 - h2.astype(F32)).astype(BF16)]

    spread_own = dot(jnp.concatenate(spread(cpad[...]), 1), const["Bs"][...])
    for e in range(EX):
        lines = [spread_own[e * EY + ey : e * EY + ey + 1] for ey in range(EY)]
        cf = [jnp.broadcast_to(l[:, :ZF], (N, ZF)) for l in lines]
        one = jnp.concatenate(cf, 0)
        Cr[e] = jnp.concatenate([one] * N, 0)
        W3r[e] = Cr[e] * const["w3"][...]
        FXr[0, e * YF : (e + 1) * YF] = one
        FXr[0, 2 * YF + e * N : 2 * YF + (e + 1) * N] = cf[0]
        FXr[0, 2 * YF + (EX + e) * N : 2 * YF + (EX + e + 1) * N] = cf[EY - 1]

    W3Fr[...] = FXr[0] * const["w3f"][...]

    rows = lax.broadcasted_iota(jnp.int32, (ROWS, ZF), 0)
    lanes = lax.broadcasted_iota(jnp.int32, (ROWS, ZF), 1)
    xr, yr = rows // YF, lax.rem(rows, YF)
    frow = lax.broadcasted_iota(jnp.int32, (96, ZF), 0)
    flane = lax.broadcasted_iota(jnp.int32, (96, ZF), 1)
    fx = jnp.where(frow < YF, 0, jnp.where(frow < 2 * YF, XF - 1, lax.rem(frow, XF)))
    fy = jnp.where(frow < 2 * YF, lax.rem(frow, YF), jnp.where(frow < 2 * YF + XF, 0, YF - 1))

    def edge(i, count=0):
        e = (lax.rem(i, N) == 0) | (lax.rem(i, N) == N - 1)
        return jnp.where(e & (i != 0) & (i != count - 1) if count else e, 0.5, 1.0)

    Wr[...] = edge(lanes) * edge(yr) * edge(xr)
    WLr[...] = edge(lanes) * edge(yr, YF)
    WFr[...] = edge(flane) * edge(fx) * edge(fy)
    WLFr[...] = edge(flane) * edge(fx, XF) * edge(fy, YF)

    def mask_of(x, y, z, n):
        inner = (x > 0) & (x < gxn * EX * n - 1) & (y > 0) & (y < gyn * EY * n - 1)
        return inner & (z != 0) & (z != EZ * n - 1)

    pd = rmul(cpad[...], const["Bdf"], HOW["g"])
    diag = lmul(const["Gdo"], jnp.concatenate([pd[:, :ZF], pd[:, ZF:]], 0), n=HOW["g"])
    for e in range(EX):
        keep = mask_of(px * XF + e * N + xr, py * YF + yr, lanes, N)
        Dr[e] = jnp.where(keep, 1.0 / diag[e * ROWS : (e + 1) * ROWS], 0.0)
    fkeep = mask_of(px * XF + fx, py * YF + fy, flane, N)
    tile_exchange.arrive()
    pd = rmul(tiles[...], const["Bdf"], HOW["g"])
    diag = lmul(const["Gdf"], pd[:, :ZF], pd[:, ZF:], n=HOW["g"])
    df = jnp.where(fkeep, 1.0 / diag, 0.0)
    DFr[...] = df
    DcFr[...] = df * FXr[0]
    Dr[0, 0:YF] = df[0:YF]
    Dr[1, ROWS - YF : ROWS] = df[YF : 2 * YF]
    for x in range(XF):
        e, r = x // N, (x % N) * YF
        Dr[e, r : r + 1] = df[2 * YF + x : 2 * YF + x + 1]
        b = 2 * YF + XF + x
        Dr[e, r + YF - 1 : r + YF] = df[b : b + 1]

    def coarse_setup():
        ext = tiles[...]
        pdc = rmul(ext, const["Bdc"], HOW["g"])
        diag_c = lmul(const["Gdc"], pdc[:, :ZC], pdc[:, ZC:], n=HOW["g"])
        crow = lax.broadcasted_iota(jnp.int32, (384, ZC), 0)
        clane = lax.broadcasted_iota(jnp.int32, (384, ZC), 1)

        def place(r, width, x0, y0):
            return (x0 + r // width, y0 + lax.rem(r, width))

        cx, cy = place(crow, YC, 0, 0)
        base = OWN
        for count, width, x0, y0 in (
            (ROWS_C, YC, -NC, 0), (ROWS_C, YC, XC, 0), (XC * NC, NC, 0, -NC), (XC * NC, NC, 0, YC),
            (16, NC, -NC, -NC), (16, NC, -NC, YC), (16, NC, XC, -NC), (16, NC, XC, YC),
        ):
            nx, ny = place(crow - base, width, x0, y0)
            cx, cy = jnp.where(crow >= base, nx, cx), jnp.where(crow >= base, ny, cy)
            base += count
        keep = mask_of(px * XC + cx, py * YC + cy, clane, NC)
        Dc_r[...] = jnp.where(keep, 1.0 / diag_c, 0.0)
        lines = dot(jnp.concatenate(spread(ext), 1), const["Bs"][:, ZF:])
        Cc_r[...] = dot(const["Pc"][...], jnp.concatenate(spread(lines), 0))

    def halo(i):
        fine(i).arrive()
        return jnp.concatenate([rx[i, 0], rx[i, 1], ry[i, 0] + rc[i, 0], ry[i, 1] + rc[i, 1]], 0)

    def add_faces(ref, index, h):
        ref[(*index, 0, pl.ds(0, YF))] += h[0:YF]
        ref[(*index, 1, pl.ds(ROWS - YF, YF))] += h[YF : 2 * YF]
        for x in range(XF):
            e, r = x // N, (x % N) * YF
            ref[(*index, e, pl.ds(r, 1))] += h[2 * YF + x : 2 * YF + x + 1]
            b = 2 * YF + XF + x
            ref[(*index, e, pl.ds(r + YF - 1, 1))] += h[b : b + 1]

    def sums_inside(v):
        wide = lambda name: jnp.concatenate([const[name][...]] * 2, 1)
        v = v + wide("yu") * pltpu.roll(v, ROWS - 1, 0) + wide("yd") * pltpu.roll(v, 1, 0)
        return v + const["zu"][0:1] * pltpu.roll(v, ZF - 1, 1) + const["zd"][0:1] * pltpu.roll(v, 1, 1)

    def bulk(values, n):
        for e in range(EX):
            p = split(values(e), n)
            p = [p[i] for i, _ in TERMS[:n]]
            t = dot(const["Mh"][:, : n * ROWS], jnp.concatenate(p, 0))
            t = t + dot(jnp.concatenate(p, 1), const["Kh"][: n * ZF])
            Lr[e] = sums_inside(W3r[e] * t)
        FXr[1, 0:YF] = Lr[0, 0:YF]
        FXr[1, YF : 2 * YF] = Lr[1, ROWS - YF : ROWS]
        for side, y in ((2 * YF, 0), (2 * YF + XF, YF - 1)):
            for x in range(XF):
                e, r = x // N, (x % N) * YF + y
                FXr[1, side + x : side + x + 1] = Lr[e, r : r + 1]
            both = Lr[0, ROWS - YF + y : ROWS - YF + y + 1] + Lr[1, y : y + 1]
            FXr[1, side + N - 1 : side + N] = both
            FXr[1, side + N : side + N + 1] = both

    def face_z(hs, n):
        return rmul(hs, const["Bf"], n)

    def send_faces(i, faces):
        sx[i, 0] = faces[0:YF]
        sx[i, 1] = faces[YF : 2 * YF]
        sy[i, 0] = faces[2 * YF : 2 * YF + XF]
        sy[i, 1] = faces[2 * YF + XF :]
        fine(i).start()

    def face_to_face(delta, n):
        p = split(delta, n)
        p = [p[i] for i, _ in TERMS[:n]]
        t = dot(const["Mff"][:, : n * 96], jnp.concatenate(p, 0))
        halves = [jnp.concatenate([q[:, :128], q[:, 128:]], 0) for q in p]
        r = dot(jnp.concatenate(halves, 1), const["Kz1"][: n * 128])
        Er[...] = jnp.concatenate([r[:96], r[96:]], 1)
        for a, b in ((0, 2 * YF), (YF - 1, 2 * YF + XF), (YF, 2 * YF + XF - 1), (2 * YF - 1, 2 * YF + 2 * XF - 1)):
            both = Er[a : a + 1] + Er[b : b + 1]
            Er[a : a + 1] = both
            Er[b : b + 1] = both
        v = W3Fr[...] * (t + Er[...])
        wide = lambda name: jnp.concatenate([const[name][...]] * 2, 1)
        v = v + wide("fu") * pltpu.roll(v, 95, 0) + wide("fd") * pltpu.roll(v, 1, 0)
        return v + const["zu"][0:1] * pltpu.roll(v, ZF - 1, 1) + const["zd"][0:1] * pltpu.roll(v, 1, 1)

    def face_to_all(ph, n):
        for e in range(EX):
            part = jnp.concatenate([ph[e * YF : (e + 1) * YF], ph[2 * YF :]], 0)
            Lr[e] += lmul(const[f"F2A{e}"], part[:, :ZF], part[:, ZF:], n=n)
        middle(Lr)

    def finish(k):
        add_faces(Zr, (k,), (-k_f) * DFr[...] * Hr[...])
        face_to_all(face_z((-k_f) * DcFr[...] * Hr[...], HOW["h"]), HOW["h"])
        for e in range(EX):
            Fr[k + 1, e] = Lr[e]

    def total(x):
        x = jnp.sum(x, axis=0, keepdims=True)
        return x[:, : ZF // 2] + x[:, ZF // 2 :]

    def cycle(k, carry):
        pl.when(k > 0)(lambda: finish(k - 1))
        bulk(lambda e: (Dr[e] * inv_center) * Fr[k, e], HOW["a"])
        @pl.when(k > 0)
        def _():
            h = halo(4 * k)
            FXr[1] = FXr[1] + face_to_face(DFr[...] * inv_center * h, HOW["a"])
            Hr[...] = h

        send_faces(4 * k + 1, FXr[1])

        @pl.when(k > 0)
        def _():
            add_faces(Fr, (k,), Hr[...])
            face_to_all(face_z(DcFr[...] * inv_center * Hr[...], HOW["a"]), HOW["a"])

        @pl.when(k == 0)
        def _():
            middle(Lr)
            coarse_setup()

        FFr[k, 0:YF] = Fr[k, 0, 0:YF]
        FFr[k, YF : 2 * YF] = Fr[k, 1, ROWS - YF : ROWS]
        for x in range(XF):
            e, r = x // N, (x % N) * YF
            FFr[k, 2 * YF + x : 2 * YF + x + 1] = Fr[k, e, r : r + 1]
            b = 2 * YF + XF + x
            FFr[k, b : b + 1] = Fr[k, e, r + YF - 1 : r + YF]
        gl = None
        for e in range(EX):
            s = Dr[e] * (a_f * Fr[k, e] - k_f * Lr[e])
            Sr[e] = s
            p = rmul(Cr[e] * s, const["Br"], HOW["b"])
            Ar[e, :, 0:ZC] = rmul(Fr[k, e], const["Bw"], HOW["b"])
            o = lmul(const[f"Gr{e}"], p[:, :ZC], p[:, ZC:], n=HOW["b"])
            gl = o if e == 0 else gl + o
        gl = lmul(const["Gw"], Ar[0, :, 0:ZC], Ar[1, :, 0:ZC], n=HOW["b"]) - gl
        h = halo(4 * k + 1)
        hs = (-k_f) * DcFr[...] * h
        pr = rmul(hs, const["Br"], HOW["b"])
        gl = gl - lmul(const["F2R"], pr[:, :ZC], pr[:, ZC:], n=HOW["b"])
        cs[k] = gl
        coarse(k).start()
        gr[0:OWN] = gl[0:OWN]
        bulk(lambda e: Sr[e], HOW["s"])
        ph = face_z(hs, HOW["s"])
        face_to_all(ph, HOW["s"])
        FXr[1] = FXr[1] + face_to_face((-k_f) * DFr[...] * h, HOW["s"])
        add_faces(Sr, (), (-k_f) * DFr[...] * h)
        coarse(k).arrive()
        gr[OWN:] = cr[k]
        for a, b, n in coarse_pairs():
            t = gr[a : a + n] + gr[b : b + n]
            gr[a : a + n] = t
            gr[b : b + n] = t
        p = lmul(const["Gc"], Cc_r[...] * (Dc_r[...] * inv_center_c) * gr[...], n=HOW["c"])
        o = rmul(jnp.concatenate([p[:OWN], p[OWN:]], 1), const["Bc"], HOW["c"])
        g = gr[0:OWN]
        fix = Dc_r[0:OWN] * (a_c * g - k_c * o)
        fix_c = Cc_r[0:OWN] * fix
        p = lmul(const["Gjf"], fix_c, n=HOW["d"])
        o = rmul(jnp.concatenate([p[:96], p[96:]], 1), const["Bjv"], HOW["d"])
        send_faces(4 * k + 2, FXr[1] + o)
        p = rmul(fix_c, const["Bj"], HOW["d"], slice(0, 2 * ZF))
        o = lmul(const["Gj"], p[:, :ZF], p[:, ZF:], n=HOW["d"])
        p = rmul(fix, const["Bj"], HOW["d"], slice(2 * ZF, 3 * ZF))
        up = lmul(const["Gp"], p, n=HOW["d"])
        for e in range(EX):
            part = slice(e * ROWS, (e + 1) * ROWS)
            Sr[e] = Sr[e] + up[part]
            Rr[e] = Fr[k, e] - Lr[e] - o[part]
        bulk(lambda e: (Dr[e] * inv_center) * Rr[e], HOW["e"])
        h = halo(4 * k + 2)
        send_faces(4 * k + 3, FXr[1] + face_to_face((-inv_center) * DFr[...] * h, HOW["e"]))
        add_faces(Rr, (), -h)
        face_to_all(face_z((-inv_center) * DcFr[...] * h, HOW["e"]), HOW["e"])
        for e in range(EX):
            Zr[k, e] = Sr[e] + Dr[e] * (a_f * Rr[e] - k_f * Lr[e])
        bulk(lambda e: Zr[k, e], HOW["f"])
        sums = [0.0] * 3
        for e in range(EX):
            z = Zr[k, e]
            wz = Wr[...] * z
            for i, t in enumerate((Fr[0, e] * wz, Fr[k, e] * wz, WLr[...] * Lr[e] * z)):
                sums[i] = sums[i] + total(t)
        h = halo(4 * k + 3)
        delta = (-k_f) * DFr[...] * h
        ff = face_to_face(delta, HOW["h"])
        send_faces(4 * k + 4, FXr[1] + ff)
        wd = WFr[...] * delta
        faces = (FFr[0] * wd, FFr[k] * wd, WLFr[...] * delta * (2.0 * FXr[1] + ff))
        for i, t in enumerate(faces):
            dots[k, i : i + 1] = sums[i] + total(t)
        Hr[...] = h
        return carry

    add_faces(Fr, (0,), halo(0))
    lax.fori_loop(0, 2, cycle, 0)

    def reduce_stage(buf, stage, base):
        return [
            pltpu.make_async_remote_copy(
                src_ref=buf.at[0], dst_ref=buf.at[j + 1], send_sem=dsend_sem.at[base + j], recv_sem=drecv_sem.at[base + j],
                device_id=p, device_id_type=MESH,
            )
            for j, p in enumerate(stage)
        ]

    def summed(buf, stage, n):
        for c in stage:
            c.wait_recv()
        out = buf[0]
        for j in range(n):
            out = out + buf[j + 1]
        return out

    d1[0, 0:3] = dots[0, 0:3]
    d1[0, 3:6] = dots[1, 0:3]
    d1[0, 6:8] = jnp.zeros((2, 128), F32)
    stage1 = reduce_stage(d1, stages[0], 0)
    stage2 = reduce_stage(d2, stages[1], len(stage1))
    for c in stage1:
        c.start()
    finish(1)
    d2[0] = summed(d1, stage1, len(stage1))
    for c in stage2:
        c.start()
    tile_exchange.drain()
    for c in stage1:
        c.wait_send()

    def drain(i, carry):
        fine(i).drain()
        return carry

    lax.fori_loop(0, 9, drain, 0)
    for k in range(2):
        coarse(k).drain()
    h = halo(8)
    add_faces(Fr, (2,), h)
    lanes_sum = jnp.sum(summed(d2, stage2, len(stage2)), axis=1, keepdims=True)
    pick = lambda i: lanes_sum[i : i + 1, 0:1]
    rz0, c00 = pick(1), pick(2)
    r0u, wu, uv = pick(3), pick(4), pick(5)
    alpha0 = rz0 / c00
    rz1 = alpha0 * (alpha0 * wu - r0u)
    beta1 = 1.0 + rz1 / rz0
    curve = beta1 * beta1 * c00 - 2.0 * beta1 * alpha0 * wu + alpha0 * alpha0 * uv
    alpha1 = rz1 / curve
    c_z = alpha0 + alpha1 * beta1
    c_u = alpha1 * alpha0
    for e in range(EX):
        sol_ref[e] = c_z * Zr[0, e] - c_u * Zr[1, e]
        res_ref[e] = jnp.where(Dr[e] > 0.0, Fr[0, e] - c_z * Fr[1, e] + c_u * Fr[2, e], 0.0)
    for c in stage2:
        c.wait_send()


def solution(mesh):
    gxn, gyn = mesh.shape["gx"], mesh.shape["gy"]
    table = constants()
    names = tuple(table)
    n_dots = gyn - 1 + gxn - 1

    def per_device(right_side, coefficient):
        rhs = right_side.reshape(EX, ROWS, ZF)
        field = (EX, ROWS, ZF)
        vm = lambda *s: pltpu.VMEM(s, F32)
        dma = lambda *s: pltpu.SemaphoreType.DMA(s)
        face = (96, ZF)
        scratch = [pltpu.VMEM(table[m].shape, table[m].dtype) for m in names]
        scratch += [
            vm(3, *field), vm(2, *field), vm(*field), vm(*field), vm(*field), vm(*face), vm(*face), vm(384, ZC), vm(*face), vm(*face),
            vm(*field), vm(*field), vm(*field), vm(*field), vm(2, *face), vm(2, *face), vm(*face),
            vm(ROWS, ZF), vm(ROWS, ZF), vm(*face), vm(*face),
            vm(384, ZC), vm(384, ZC), vm(8, 128), vm(EX, EY, EZ), vm(80, 128),
            vm(9, 2, YF, ZF), vm(9, 2, EX * N, ZF), vm(9, 2, YF, ZF), vm(9, 2, EX * N, ZF), vm(9, 2, EX * N, ZF),
            vm(2, 192, ZC), vm(2, 256, ZC),
            vm(2, 8, 128), vm(gyn, 8, 128), vm(gxn, 8, 128),
            dma(len(names) + 2), dma(9, 8), dma(9, 8), dma(2, 8), dma(2, 8), dma(8), dma(8), dma(n_dots), dma(n_dots),
        ]
        sol, res = pl.pallas_call(
            functools.partial(kernel_body, (gxn, gyn), names),
            out_shape=[pltpu.VMEM(field, F32)] * 2,
            in_specs=[pl.BlockSpec(memory_space=pl.ANY)] * (2 + len(names)),
            out_specs=[pl.BlockSpec(memory_space=pltpu.VMEM)] * 2,
            scratch_shapes=scratch,
            compiler_params=pltpu.CompilerParams(
                collective_id=0, has_side_effects=True, vmem_limit_bytes=56 * 2**20
            ),
        )(rhs, coefficient, *[jnp.asarray(table[m]) for m in names])
        return sol.reshape(right_side.shape), res.reshape(right_side.shape)

    spec = P("gx", "gy", None)
    return jax.shard_map(
        per_device, mesh=mesh, in_specs=(spec, spec), out_specs=(spec, spec), check_vma=False
    )
```

```python
import functools
import math

import jax
import jax.numpy as jnp
import numpy as np
from jax import lax
from jax.experimental import pallas as pl
from jax.experimental.pallas import tpu as pltpu
from jax.sharding import PartitionSpec as P

ORDER = 7
COARSE_ORDER = 3
F32 = jnp.float32
BF16 = jnp.bfloat16
MESH = pl.DeviceIdType.MESH

EX, EY, EZ = 2, 4, 32
N, NC = ORDER + 1, COARSE_ORDER + 1
YF, ZF = EY * N, EZ * N
YC, ZC = EY * NC, EZ * NC
ROWS = N * YF
ROWS_C = NC * YC


def legendre_pair(degree, points):
    before = points * 0.0 + 1.0
    now = points.copy()
    for power in range(2, degree + 1):
        after = ((2 * power - 1) * points * now - (power - 1) * before) / power
        before = now
        now = after
    return (now, before)


def gll_tables(degree):
    number = degree + 1
    points = np.cos(math.pi * np.arange(number) / degree)
    for newton in range(60):
        top, below = legendre_pair(degree, points)
        points = points - (points * top - below) / (number * top)
    points = points[::-1].copy()
    points[0] = -1.0
    points[degree] = 1.0
    values = legendre_pair(degree, points)[0]
    weights = 2.0 / (degree * (degree + 1) * values**2)
    derivative = np.zeros((number, number))
    for row_index in range(number):
        for column_index in range(number):
            if row_index != column_index:
                derivative[row_index, column_index] = values[row_index] / (
                    values[column_index] * (points[row_index] - points[column_index])
                )
    derivative[0, 0] = -degree * (degree + 1) / 4.0
    derivative[degree, degree] = degree * (degree + 1) / 4.0
    stiffness = derivative.T @ (weights[:, None] * derivative)
    return (points, weights, stiffness)


def upper_bound(degree):
    points, weights, stiffness = gll_tables(degree)
    rowsum = np.abs(stiffness).sum(1)
    diagonal = np.diag(stiffness)
    outer = lambda a, b, c: a[:, None, None] * b[None, :, None] * c[None, None, :]
    top = outer(rowsum, weights, weights) + outer(weights, rowsum, weights) + outer(weights, weights, rowsum)
    bottom = outer(diagonal, weights, weights) + outer(weights, diagonal, weights) + outer(weights, weights, diagonal)
    return float((top / bottom).max())


def interpolation_matrix(fine_degree, coarse_degree):
    fine_points = gll_tables(fine_degree)[0]
    coarse_points = gll_tables(coarse_degree)[0]
    matrix = np.ones((fine_degree + 1, coarse_degree + 1))
    for column_index in range(coarse_degree + 1):
        for other_index in range(coarse_degree + 1):
            if other_index != column_index:
                matrix[:, column_index] *= (fine_points - coarse_points[other_index]) / (
                    coarse_points[column_index] - coarse_points[other_index]
                )
    return matrix


def cheb_numbers(degree):
    upper = upper_bound(degree)
    lower = 0.1 * upper
    center = 0.5 * (upper + lower)
    half = 0.5 * (upper - lower)
    previous = half / center
    current = 1.0 / (2.0 * center / half - previous)
    k = 2.0 * current / half
    return (1.0 / center, (1.0 + current * previous) / center + k, k)


def sum_matrix(elements, number):
    matrix = np.eye(elements * number)
    for e in range(elements - 1):
        a, b = e * number + number - 1, (e + 1) * number
        matrix[a, b] = matrix[b, a] = 1.0
    return matrix


def blocks(count, matrix):
    return np.kron(np.eye(count), matrix)


TERMS = ((0, 0), (1, 0), (0, 1), (2, 0), (0, 2), (1, 1))
HOW = dict(a=3, b=3, s=6, c=3, d=6, e=3, f=6, g=3, h=3)


def pieces_of(matrix, count):
    rest, out = np.asarray(matrix, np.float64), []
    for _ in range(count):
        out.append(rest.astype(np.float32).astype(BF16))
        rest = rest - out[-1].astype(np.float64)
    return out


def right3(matrix, steps="asef"):
    p = pieces_of(matrix, 3)
    return np.concatenate([p[j] for _, j in TERMS[: max(HOW[t] for t in steps)]], 0)


def left3(matrix, steps="asef"):
    p = pieces_of(matrix, 3)
    return np.concatenate([p[j] for _, j in TERMS[: max(HOW[t] for t in steps)]], 1)


def level_matrices(degree):
    _, w, K = gll_tables(degree)
    n = degree + 1
    wy = np.tile(w, EY)
    M0 = np.kron(K, np.diag(wy)) + np.kron(np.diag(w), blocks(EY, K))
    N0 = np.kron(np.diag(w), np.diag(wy))
    return M0, N0, np.diag(np.tile(w, EZ)), blocks(EZ, K)


def face_rows(n):
    y = EY * n
    x = EX * n
    rows = [j for j in range(y)] + [(x - 1) * y + j for j in range(y)]
    rows += [i * y for i in range(x)] + [i * y + y - 1 for i in range(x)]
    return np.array(rows)


def coarse_places():
    XC = EX * NC
    before, after_x, after_y = range(-NC, 0), range(XC, XC + NC), range(YC, YC + NC)
    grids = [(range(XC), range(YC)), (before, range(YC)), (after_x, range(YC)), (range(XC), before), (range(XC), after_y)]
    grids += [(a, b) for a in (before, after_x) for b in (before, after_y)]
    both = [(x, y) for xs, ys in grids for x in xs for y in ys]
    return np.array([p[0] for p in both]), np.array([p[1] for p in both])


def coarse_pairs():
    x, y = coarse_places()
    row = {p: i for i, p in enumerate(zip(x.tolist(), y.tolist()))}
    XC, out = EX * NC, []
    for a, b in ((-1, 0), (XC - 1, XC)):
        for first, n in ((-NC, NC), (0, YC), (YC, NC)):
            out.append((row[a, first], row[b, first], n))
    for a, b in ((-1, 0), (YC - 1, YC)):
        out += [(row[i, a], row[i, b], 1) for i in range(-NC, XC + NC)]
    return out


@functools.cache
def constants():
    J = interpolation_matrix(ORDER, COARSE_ORDER)
    out = {}
    M0, N0, Wz, Kz = level_matrices(ORDER)
    Sz, Szc = sum_matrix(EZ, N), sum_matrix(EZ, NC)
    Sxy = np.kron(sum_matrix(EX, N), sum_matrix(EY, N))
    Sxyc = np.kron(sum_matrix(EX, NC), sum_matrix(EY, NC))
    Mf, Nf = blocks(EX, M0), blocks(EX, N0)
    SM, SN = Sxy @ Mf, Sxy @ Nf
    F = face_rows(N)
    out["Bf"] = right3(np.concatenate([Wz @ Sz, Kz @ Sz], 1))
    _, w, K = gll_tables(ORDER)
    wxy, wz = np.kron(w, np.tile(w, EY)), np.tile(w, EZ)
    out["Mh"] = left3(M0 / wxy[:, None])
    out["Kh"] = right3(Kz / wz[None, :])
    out["w3"] = (wxy[:, None] * wz[None, :]).astype(np.float32)
    y, z = np.arange(ROWS) % YF, np.arange(ZF)
    wide = lambda m, shape: np.broadcast_to(m, shape).astype(np.float32)
    out["yu"] = wide(((y % N == N - 1) & (y != YF - 1))[:, None], (ROWS, 128))
    out["yd"] = wide(((y % N == 0) & (y != 0))[:, None], (ROWS, 128))
    out["zu"] = wide(((z % N == N - 1) & (z != ZF - 1))[None, :], (8, ZF))
    out["zd"] = wide(((z % N == 0) & (z != 0))[None, :], (8, ZF))
    Sy = np.kron(np.eye(EX * N), sum_matrix(EY, N))
    out["Mff"] = left3(blocks(EX, M0 / wxy[:, None])[F][:, F])
    out["Kz1"] = right3((Kz / wz[None, :])[:128, :128])
    out["w3f"] = (np.tile(wxy, EX)[F][:, None] * wz[None, :]).astype(np.float32)
    along = np.concatenate([np.arange(YF), np.arange(YF), np.arange(EX * N), np.arange(EX * N)])
    ends = np.concatenate([np.full(2 * YF, YF), np.full(2 * EX * N, EX * N)])
    out["fu"] = wide(((along % N == N - 1) & (along != ends - 1))[:, None], (96, 128))
    out["fd"] = wide(((along % N == 0) & (along != 0))[:, None], (96, 128))
    for e in range(EX):
        rows = slice(e * ROWS, (e + 1) * ROWS)
        here = np.concatenate([np.arange(e * YF, (e + 1) * YF), np.arange(2 * YF, len(F))])
        keep = ((F[here] // ROWS) == e).astype(float)[None, :]
        full = np.concatenate([(Sy @ Mf)[rows][:, F[here]] * keep, (Sy @ Nf)[rows][:, F[here]] * keep], 1)
        out[f"F2A{e}"] = left3(full)
    Rxy = blocks(EX, np.kron(J.T, blocks(EY, J.T)))
    JZ = blocks(EZ, J)
    XC = EX * NC
    first = [x * YC + y for x in range(XC) for y in range(NC)]
    last = [x * YC + YC - NC + y for x in range(XC) for y in range(NC)]
    selc = np.concatenate([np.arange(XC * YC), first, last]).astype(int)
    RM, RN = (Sxyc @ Rxy @ Mf)[selc], (Sxyc @ Rxy @ Nf)[selc]
    out["Br"] = right3(np.concatenate([Wz @ JZ @ Szc, Kz @ JZ @ Szc], 1), "b")
    for e in range(EX):
        cols = slice(e * ROWS, (e + 1) * ROWS)
        out[f"Gr{e}"] = left3(np.concatenate([RM[:, cols], RN[:, cols]], 1), "b")
    out["F2R"] = left3(np.concatenate([RM[:, F], RN[:, F]], 1), "b")
    inv = lambda count: np.where((np.arange(count) % N == 0) | (np.arange(count) % N == N - 1), 0.5, 1.0)
    Wxy = np.kron(np.diag(inv(EX * N)), np.diag(inv(YF)))
    RW = (Sxyc @ Rxy @ Wxy)[selc]
    out["Bw"] = right3(np.diag(inv(ZF)) @ JZ @ Szc, "b")
    out["Gw"] = left3(RW, "b")
    _, wc, Kc = gll_tables(COARSE_ORDER)
    Wzc, Kzc = np.diag(np.tile(wc, EZ)), blocks(EZ, Kc)
    out["Bc"] = right3(np.concatenate([Wzc @ Szc, Kzc @ Szc], 0), "c")
    cx, cy = coarse_places()
    grid = (cx + NC) * (YC + 2 * NC) + cy + NC
    wx4, wy6 = np.diag(np.tile(wc, EX + 2)), np.diag(np.tile(wc, EY + 2))
    Me = np.kron(blocks(EX + 2, Kc), wy6) + np.kron(wx4, blocks(EY + 2, Kc))
    Ne = np.kron(wx4, wy6)
    Se = np.kron(sum_matrix(EX + 2, NC), sum_matrix(EY + 2, NC))
    own = grid[: XC * YC]
    out["Gc"] = left3(np.concatenate([(Se @ Me)[own][:, grid], (Se @ Ne)[own][:, grid]], 0), "c")
    pick = np.zeros((len(cx), 80))
    for i, (x, y) in enumerate(zip(cx // NC, cy // NC)):
        pick[i, ((x // EX + 1) * 3 + y // EY + 1) * 8 + (x % EX) * EY + y % EY] = 1.0
    out["Pc"] = np.concatenate([pick.astype(np.float32).astype(BF16)] * 3, 1)
    Jxy = blocks(EX, np.kron(J, blocks(EY, J)))
    out["Bj"] = right3(np.concatenate([JZ.T @ Wz @ Sz, JZ.T @ Kz @ Sz, JZ.T], 1), "d")
    out["Bjv"] = right3(np.concatenate([JZ.T @ Wz @ Sz, JZ.T @ Kz @ Sz], 0), "d")
    JM, JN = SM @ Jxy, SN @ Jxy
    out["Gj"] = left3(np.concatenate([JM, JN], 1), "d")
    out["Gjf"] = left3(np.concatenate([JM[F], JN[F]], 0), "d")
    out["Gp"] = left3(Jxy, "d")
    fine_x, fine_y = np.divmod(np.arange(EX * ROWS), YF)
    places = {"f": (np.concatenate([fine_x, F // YF]), np.concatenate([fine_y, F % YF])), "c": (cx, cy)}
    for name, degree in (("f", ORDER), ("c", COARSE_ORDER)):
        n = degree + 1
        _, w, K = gll_tables(degree)
        kd = np.diag(K)
        S = sum_matrix(EZ, n)
        spread_w = np.zeros((128, EZ * n))
        spread_k = np.zeros((128, EZ * n))
        for ez in range(EZ):
            spread_w[ez, ez * n : (ez + 1) * n] = w
            spread_k[ez, ez * n : (ez + 1) * n] = kd
        out["Bd" + name] = right3(np.concatenate([spread_w @ S, spread_k @ S], 1), "g")
        left = np.zeros((len(places[name][0]), 2, 80))
        for i, (x, y) in enumerate(zip(*places[name])):
            xs = [(x // n, x % n)]
            if x % n == 0:
                xs.append((x // n - 1, n - 1))
            if x % n == n - 1:
                xs.append((x // n + 1, 0))
            ys = [(y // n, y % n)]
            if y % n == 0:
                ys.append((y // n - 1, n - 1))
            if y % n == n - 1:
                ys.append((y // n + 1, 0))
            for ex, a in xs:
                for ey, b in ys:
                    col = ((ex // EX + 1) * 3 + ey // EY + 1) * 8 + (ex % EX) * EY + ey % EY
                    left[i, 0, col] += kd[a] * w[b] + w[a] * kd[b]
                    left[i, 1, col] += w[a] * w[b]
        left = left.reshape(len(left), 160)
        if name == "f":
            here = left.reshape(len(left), 2, 80)[: EX * ROWS, :, 32:40].reshape(EX * ROWS, 16)
            out["Gdo"] = left3(here, "g")
            left = left[EX * ROWS :]
        out["Gd" + name] = left3(left, "g")
    spread = np.zeros((128, ZF + ZC))
    for ez in range(EZ):
        spread[ez, ez * N : (ez + 1) * N] = 1.0
        spread[ez, ZF + ez * NC : ZF + (ez + 1) * NC] = 1.0
    out["Bs"] = np.concatenate([spread.astype(np.float32).astype(BF16)] * 3, 0)
    return out


def dot(a, b):
    return jnp.dot(a, b, preferred_element_type=F32)


def split(x, n):
    out = []
    for i in range(1 + max(i for i, _ in TERMS[:n])):
        out.append(x.astype(BF16))
        x = x - out[-1].astype(F32)
    return out


def rmul(x, b, n, cols=slice(None)):
    p = split(x, n)
    x3 = jnp.concatenate([p[i] for i, _ in TERMS[:n]], 1)
    return dot(x3, b[: x3.shape[1], cols])


def lmul(g, *parts, n, rows=slice(None)):
    split_parts = [split(x, n) for x in parts]
    x3 = jnp.concatenate([p[i] for i, _ in TERMS[:n] for p in split_parts], 0)
    return dot(g[rows, : x3.shape[0]], x3)


def kernel_body(shape, names, rhs_ref, coef_ref, *refs):
    gxn, gyn = shape
    n_const = len(names)
    const_hbm = dict(zip(names, refs[:n_const]))
    sol_ref, res_ref = refs[n_const : n_const + 2]
    rest = refs[n_const + 2 :]
    const = dict(zip(names, rest[:n_const]))
    (Fr, Zr, Dr, Cr, W3r, W3Fr, Er, gr, DFr, DcFr, Lr, Sr, Rr, Ar, FXr, FFr, Hr, Wr, WLr, WFr, WLFr,
     Dc_r, Cc_r, cpad, coef, tiles,
     sx, sy, rx, ry, rc, cs, cr, dots, d1, d2,
     const_sem, send_sem, recv_sem, csend_sem, crecv_sem, tsend_sem, trecv_sem, dsend_sem, drecv_sem) = rest[n_const:]

    inv_center, a_f, k_f = cheb_numbers(ORDER)
    inv_center_c, a_c, k_c = cheb_numbers(COARSE_ORDER)
    px, py = lax.axis_index("gx"), lax.axis_index("gy")
    XF, XC, OWN = EX * N, EX * NC, EX * ROWS_C

    def at(dx, dy):
        return (lax.rem(px + dx + gxn, gxn), lax.rem(py + dy + gyn, gyn))

    def inside(dx, dy):
        ok = None
        for p, d, n in ((px, dx, gxn), (py, dy, gyn)):
            if d:
                here = (p > 0) if d < 0 else (p < n - 1)
                ok = here if ok is None else ok & here
        return ok

    corners = [(dx, dy) for dx in (-1, 1) for dy in (-1, 1)]
    around = corners + [(-1, 0), (1, 0), (0, -1), (0, 1)]
    def ring(coarse_n, fine_n, hops):
        every = [(a, b) for a in range(coarse_n) for b in range(fine_n) if (a, b) != (0, 0)]
        near = lambda d, n: min(d, n - d)
        return sorted(every, key=lambda o: -(near(o[0], coarse_n) + hops * near(o[1], fine_n)))

    def shifted(p, fine_n, coarse_n, o):
        return lax.rem(p // fine_n + o[0], coarse_n) * fine_n + lax.rem(lax.rem(p, fine_n) + o[1], fine_n)

    nz = 8 if gxn % 8 == 0 else 2
    nx, ny = gyn // 2, gxn // nz
    stages = [
        [(px, shifted(py, 2, nx, o)) for o in ring(nx, 2, 0.5)],
        [(shifted(px, nz, ny, o), py) for o in ring(ny, nz, 1)],
    ]

    copies = [pltpu.make_async_copy(const_hbm[m], const[m], const_sem.at[i]) for i, m in enumerate(names)]
    load_rhs = pltpu.make_async_copy(rhs_ref, Ar, const_sem.at[n_const])
    load_coef = pltpu.make_async_copy(coef_ref, coef, const_sem.at[n_const + 1])
    load_rhs.start()
    load_coef.start()

    for ref in (rx, ry, rc, cr, tiles, cpad):
        ref[...] = jnp.zeros_like(ref)

    barrier = pltpu.get_barrier_semaphore()
    expected = 0
    for stage in stages[::-1]:
        for p in stage:
            pl.semaphore_signal(barrier, inc=1, device_id=p, device_id_type=MESH)
        expected = expected + len(stage)
    for d in around:
        pl.when(inside(*d))(
            lambda d=d: pl.semaphore_signal(barrier, inc=1, device_id=at(*d), device_id_type=MESH)
        )
        expected = expected + inside(*d).astype(jnp.int32)
    for c in copies:
        c.start()

    def local_sum(v):
        rows = lax.broadcasted_iota(jnp.int32, v.shape, 0)
        lanes = lax.broadcasted_iota(jnp.int32, v.shape, 1)
        y = lax.rem(rows, YF)
        up = (lax.rem(y, N) == N - 1) & (y != YF - 1)
        down = (lax.rem(y, N) == 0) & (y != 0)
        v = v + jnp.where(up, pltpu.roll(v, ROWS - 1, 0), 0.0) + jnp.where(down, pltpu.roll(v, 1, 0), 0.0)
        up = (lax.rem(lanes, N) == N - 1) & (lanes != ZF - 1)
        down = (lax.rem(lanes, N) == 0) & (lanes != 0)
        return v + jnp.where(up, pltpu.roll(v, ZF - 1, 1), 0.0) + jnp.where(down, pltpu.roll(v, 1, 1), 0.0)

    def middle(ref, *index):
        total = ref[(*index, 0, pl.ds(ROWS - YF, YF))] + ref[(*index, 1, pl.ds(0, YF))]
        ref[(*index, 0, pl.ds(ROWS - YF, YF))] = total
        ref[(*index, 1, pl.ds(0, YF))] = total

    load_coef.wait()
    cpad[0:EY, 0:EZ] = coef[0]
    cpad[EY : 2 * EY, 0:EZ] = coef[1]
    load_rhs.wait()
    for e in range(EX):
        Fr[0, e] = local_sum(Ar[e])
    middle(Fr, 0)
    sx[0, 0] = Fr[0, 0, 0:YF]
    sx[0, 1] = Fr[0, 1, ROWS - YF : ROWS]
    for x in range(XF):
        e, r = x // N, (x % N) * YF
        sy[0, 0, x : x + 1] = Fr[0, e, r : r + 1]
        sy[0, 1, x : x + 1] = Fr[0, e, r + YF - 1 : r + YF]

    interior = inside(-1, -1) & inside(1, 1)

    class Exchange:
        def __init__(self, plan, send, recv):
            self.plan = [
                (pltpu.make_async_remote_copy(
                    src_ref=s, dst_ref=t, send_sem=send(j), recv_sem=recv(j), device_id=at(*d), device_id_type=MESH,
                ), inside(*d), inside(-d[0], -d[1]))
                for j, (s, t, d) in enumerate(plan)
            ]

        def start(self):
            @pl.when(interior)
            def _():
                for c, _, _ in self.plan:
                    c.start()

            @pl.when(~interior)
            def _():
                for c, to, _ in self.plan:
                    pl.when(to)(c.start)

        def arrive(self):
            @pl.when(interior)
            def _():
                for c, _, _ in self.plan:
                    c.wait_recv()

            @pl.when(~interior)
            def _():
                for c, _, come in self.plan:
                    pl.when(come)(c.wait_recv)

        def drain(self):
            for c, to, _ in self.plan:
                pl.when(to)(c.wait_send)

    def fine(i):
        one = lambda r: pl.ds(r, 1)
        plan = [
            (sy.at[i, 0, one(0)], rc.at[i, 1, one(XF - 1)], (-1, -1)),
            (sy.at[i, 1, one(0)], rc.at[i, 0, one(XF - 1)], (-1, 1)),
            (sy.at[i, 0, one(XF - 1)], rc.at[i, 1, one(0)], (1, -1)),
            (sy.at[i, 1, one(XF - 1)], rc.at[i, 0, one(0)], (1, 1)),
            (sx.at[i, 0], rx.at[i, 1], (-1, 0)),
            (sx.at[i, 1], rx.at[i, 0], (1, 0)),
            (sy.at[i, 0], ry.at[i, 1], (0, -1)),
            (sy.at[i, 1], ry.at[i, 0], (0, 1)),
        ]
        return Exchange(plan, lambda j: send_sem.at[i, j], lambda j: recv_sem.at[i, j])

    def coarse(k):
        h, q = ROWS_C, NC * NC
        y0, y1 = OWN, OWN + XC * NC
        c0 = 2 * h + 4 * q
        src = lambda a, n: cs.at[k, pl.ds(a, n)]
        dst = lambda a, n: cr.at[k, pl.ds(a, n)]
        plan = [
            (src(y0, q), dst(c0 + 3 * q, q), (-1, -1)),
            (src(y1, q), dst(c0 + 2 * q, q), (-1, 1)),
            (src(y0 + q, q), dst(c0 + q, q), (1, -1)),
            (src(y1 + q, q), dst(c0, q), (1, 1)),
            (src(0, h), dst(h, h), (-1, 0)),
            (src(h, h), dst(0, h), (1, 0)),
            (src(y0, 2 * q), dst(2 * h + 2 * q, 2 * q), (0, -1)),
            (src(y1, 2 * q), dst(2 * h, 2 * q), (0, 1)),
        ]
        return Exchange(plan, lambda j: csend_sem.at[k, j], lambda j: crecv_sem.at[k, j])

    pl.semaphore_wait(barrier, expected)

    tile_plan = []
    for dx, dy in around:
        slot = ((1 - dx) * 3 + (1 - dy)) * 8
        tile_plan.append((cpad, tiles.at[pl.ds(slot, 8)], (dx, dy)))
    tile_exchange = Exchange(tile_plan, lambda j: tsend_sem.at[j], lambda j: trecv_sem.at[j])
    tile_exchange.start()
    fine(0).start()
    tiles[32:40] = cpad[...]

    for c in copies:
        c.wait()

    def spread(x):
        h1 = x.astype(BF16)
        r1 = x - h1.astype(F32)
        h2 = r1.astype(BF16)
        return [h1, h2, (r1 - h2.astype(F32)).astype(BF16)]

    spread_own = dot(jnp.concatenate(spread(cpad[...]), 1), const["Bs"][...])
    for e in range(EX):
        lines = [spread_own[e * EY + ey : e * EY + ey + 1] for ey in range(EY)]
        cf = [jnp.broadcast_to(l[:, :ZF], (N, ZF)) for l in lines]
        one = jnp.concatenate(cf, 0)
        Cr[e] = jnp.concatenate([one] * N, 0)
        W3r[e] = Cr[e] * const["w3"][...]
        FXr[0, e * YF : (e + 1) * YF] = one
        FXr[0, 2 * YF + e * N : 2 * YF + (e + 1) * N] = cf[0]
        FXr[0, 2 * YF + (EX + e) * N : 2 * YF + (EX + e + 1) * N] = cf[EY - 1]

    W3Fr[...] = FXr[0] * const["w3f"][...]

    rows = lax.broadcasted_iota(jnp.int32, (ROWS, ZF), 0)
    lanes = lax.broadcasted_iota(jnp.int32, (ROWS, ZF), 1)
    xr, yr = rows // YF, lax.rem(rows, YF)
    frow = lax.broadcasted_iota(jnp.int32, (96, ZF), 0)
    flane = lax.broadcasted_iota(jnp.int32, (96, ZF), 1)
    fx = jnp.where(frow < YF, 0, jnp.where(frow < 2 * YF, XF - 1, lax.rem(frow, XF)))
    fy = jnp.where(frow < 2 * YF, lax.rem(frow, YF), jnp.where(frow < 2 * YF + XF, 0, YF - 1))

    def edge(i, count=0):
        e = (lax.rem(i, N) == 0) | (lax.rem(i, N) == N - 1)
        return jnp.where(e & (i != 0) & (i != count - 1) if count else e, 0.5, 1.0)

    Wr[...] = edge(lanes) * edge(yr) * edge(xr)
    WLr[...] = edge(lanes) * edge(yr, YF)
    WFr[...] = edge(flane) * edge(fx) * edge(fy)
    WLFr[...] = edge(flane) * edge(fx, XF) * edge(fy, YF)

    def mask_of(x, y, z, n):
        inner = (x > 0) & (x < gxn * EX * n - 1) & (y > 0) & (y < gyn * EY * n - 1)
        return inner & (z != 0) & (z != EZ * n - 1)

    pd = rmul(cpad[...], const["Bdf"], HOW["g"])
    diag = lmul(const["Gdo"], jnp.concatenate([pd[:, :ZF], pd[:, ZF:]], 0), n=HOW["g"])
    for e in range(EX):
        keep = mask_of(px * XF + e * N + xr, py * YF + yr, lanes, N)
        Dr[e] = jnp.where(keep, 1.0 / diag[e * ROWS : (e + 1) * ROWS], 0.0)
    fkeep = mask_of(px * XF + fx, py * YF + fy, flane, N)
    tile_exchange.arrive()
    pd = rmul(tiles[...], const["Bdf"], HOW["g"])
    diag = lmul(const["Gdf"], pd[:, :ZF], pd[:, ZF:], n=HOW["g"])
    df = jnp.where(fkeep, 1.0 / diag, 0.0)
    DFr[...] = df
    DcFr[...] = df * FXr[0]
    Dr[0, 0:YF] = df[0:YF]
    Dr[1, ROWS - YF : ROWS] = df[YF : 2 * YF]
    for x in range(XF):
        e, r = x // N, (x % N) * YF
        Dr[e, r : r + 1] = df[2 * YF + x : 2 * YF + x + 1]
        b = 2 * YF + XF + x
        Dr[e, r + YF - 1 : r + YF] = df[b : b + 1]

    def coarse_setup():
        ext = tiles[...]
        pdc = rmul(ext, const["Bdc"], HOW["g"])
        diag_c = lmul(const["Gdc"], pdc[:, :ZC], pdc[:, ZC:], n=HOW["g"])
        crow = lax.broadcasted_iota(jnp.int32, (384, ZC), 0)
        clane = lax.broadcasted_iota(jnp.int32, (384, ZC), 1)

        def place(r, width, x0, y0):
            return (x0 + r // width, y0 + lax.rem(r, width))

        cx, cy = place(crow, YC, 0, 0)
        base = OWN
        for count, width, x0, y0 in (
            (ROWS_C, YC, -NC, 0), (ROWS_C, YC, XC, 0), (XC * NC, NC, 0, -NC), (XC * NC, NC, 0, YC),
            (16, NC, -NC, -NC), (16, NC, -NC, YC), (16, NC, XC, -NC), (16, NC, XC, YC),
        ):
            nx, ny = place(crow - base, width, x0, y0)
            cx, cy = jnp.where(crow >= base, nx, cx), jnp.where(crow >= base, ny, cy)
            base += count
        keep = mask_of(px * XC + cx, py * YC + cy, clane, NC)
        Dc_r[...] = jnp.where(keep, 1.0 / diag_c, 0.0)
        lines = dot(jnp.concatenate(spread(ext), 1), const["Bs"][:, ZF:])
        Cc_r[...] = dot(const["Pc"][...], jnp.concatenate(spread(lines), 0))

    def halo(i):
        fine(i).arrive()
        return jnp.concatenate([rx[i, 0], rx[i, 1], ry[i, 0] + rc[i, 0], ry[i, 1] + rc[i, 1]], 0)

    def add_faces(ref, index, h):
        ref[(*index, 0, pl.ds(0, YF))] += h[0:YF]
        ref[(*index, 1, pl.ds(ROWS - YF, YF))] += h[YF : 2 * YF]
        for x in range(XF):
            e, r = x // N, (x % N) * YF
            ref[(*index, e, pl.ds(r, 1))] += h[2 * YF + x : 2 * YF + x + 1]
            b = 2 * YF + XF + x
            ref[(*index, e, pl.ds(r + YF - 1, 1))] += h[b : b + 1]

    def sums_inside(v):
        wide = lambda name: jnp.concatenate([const[name][...]] * 2, 1)
        v = v + wide("yu") * pltpu.roll(v, ROWS - 1, 0) + wide("yd") * pltpu.roll(v, 1, 0)
        return v + const["zu"][0:1] * pltpu.roll(v, ZF - 1, 1) + const["zd"][0:1] * pltpu.roll(v, 1, 1)

    def bulk(values, n):
        for e in range(EX):
            p = split(values(e), n)
            p = [p[i] for i, _ in TERMS[:n]]
            t = dot(const["Mh"][:, : n * ROWS], jnp.concatenate(p, 0))
            t = t + dot(jnp.concatenate(p, 1), const["Kh"][: n * ZF])
            Lr[e] = sums_inside(W3r[e] * t)
        FXr[1, 0:YF] = Lr[0, 0:YF]
        FXr[1, YF : 2 * YF] = Lr[1, ROWS - YF : ROWS]
        for side, y in ((2 * YF, 0), (2 * YF + XF, YF - 1)):
            for x in range(XF):
                e, r = x // N, (x % N) * YF + y
                FXr[1, side + x : side + x + 1] = Lr[e, r : r + 1]
            both = Lr[0, ROWS - YF + y : ROWS - YF + y + 1] + Lr[1, y : y + 1]
            FXr[1, side + N - 1 : side + N] = both
            FXr[1, side + N : side + N + 1] = both

    def face_z(hs, n):
        return rmul(hs, const["Bf"], n)

    def send_faces(i, faces):
        sx[i, 0] = faces[0:YF]
        sx[i, 1] = faces[YF : 2 * YF]
        sy[i, 0] = faces[2 * YF : 2 * YF + XF]
        sy[i, 1] = faces[2 * YF + XF :]
        fine(i).start()

    def face_to_face(delta, n):
        p = split(delta, n)
        p = [p[i] for i, _ in TERMS[:n]]
        t = dot(const["Mff"][:, : n * 96], jnp.concatenate(p, 0))
        halves = [jnp.concatenate([q[:, :128], q[:, 128:]], 0) for q in p]
        r = dot(jnp.concatenate(halves, 1), const["Kz1"][: n * 128])
        Er[...] = jnp.concatenate([r[:96], r[96:]], 1)
        for a, b in ((0, 2 * YF), (YF - 1, 2 * YF + XF), (YF, 2 * YF + XF - 1), (2 * YF - 1, 2 * YF + 2 * XF - 1)):
            both = Er[a : a + 1] + Er[b : b + 1]
            Er[a : a + 1] = both
            Er[b : b + 1] = both
        v = W3Fr[...] * (t + Er[...])
        wide = lambda name: jnp.concatenate([const[name][...]] * 2, 1)
        v = v + wide("fu") * pltpu.roll(v, 95, 0) + wide("fd") * pltpu.roll(v, 1, 0)
        return v + const["zu"][0:1] * pltpu.roll(v, ZF - 1, 1) + const["zd"][0:1] * pltpu.roll(v, 1, 1)

    def face_to_all(ph, n):
        for e in range(EX):
            part = jnp.concatenate([ph[e * YF : (e + 1) * YF], ph[2 * YF :]], 0)
            Lr[e] += lmul(const[f"F2A{e}"], part[:, :ZF], part[:, ZF:], n=n)
        middle(Lr)

    def finish(k):
        add_faces(Zr, (k,), (-k_f) * DFr[...] * Hr[...])
        face_to_all(face_z((-k_f) * DcFr[...] * Hr[...], HOW["h"]), HOW["h"])
        for e in range(EX):
            Fr[k + 1, e] = Lr[e]

    def total(x):
        x = jnp.sum(x, axis=0, keepdims=True)
        return x[:, : ZF // 2] + x[:, ZF // 2 :]

    def cycle(k, carry):
        pl.when(k > 0)(lambda: finish(k - 1))
        bulk(lambda e: (Dr[e] * inv_center) * Fr[k, e], HOW["a"])
        @pl.when(k > 0)
        def _():
            h = halo(4 * k)
            FXr[1] = FXr[1] + face_to_face(DFr[...] * inv_center * h, HOW["a"])
            Hr[...] = h

        send_faces(4 * k + 1, FXr[1])

        @pl.when(k > 0)
        def _():
            add_faces(Fr, (k,), Hr[...])
            face_to_all(face_z(DcFr[...] * inv_center * Hr[...], HOW["a"]), HOW["a"])

        @pl.when(k == 0)
        def _():
            middle(Lr)
            coarse_setup()

        FFr[k, 0:YF] = Fr[k, 0, 0:YF]
        FFr[k, YF : 2 * YF] = Fr[k, 1, ROWS - YF : ROWS]
        for x in range(XF):
            e, r = x // N, (x % N) * YF
            FFr[k, 2 * YF + x : 2 * YF + x + 1] = Fr[k, e, r : r + 1]
            b = 2 * YF + XF + x
            FFr[k, b : b + 1] = Fr[k, e, r + YF - 1 : r + YF]
        gl = None
        for e in range(EX):
            s = Dr[e] * (a_f * Fr[k, e] - k_f * Lr[e])
            Sr[e] = s
            p = rmul(Cr[e] * s, const["Br"], HOW["b"])
            Ar[e, :, 0:ZC] = rmul(Fr[k, e], const["Bw"], HOW["b"])
            o = lmul(const[f"Gr{e}"], p[:, :ZC], p[:, ZC:], n=HOW["b"])
            gl = o if e == 0 else gl + o
        gl = lmul(const["Gw"], Ar[0, :, 0:ZC], Ar[1, :, 0:ZC], n=HOW["b"]) - gl
        h = halo(4 * k + 1)
        hs = (-k_f) * DcFr[...] * h
        pr = rmul(hs, const["Br"], HOW["b"])
        gl = gl - lmul(const["F2R"], pr[:, :ZC], pr[:, ZC:], n=HOW["b"])
        cs[k] = gl
        coarse(k).start()
        gr[0:OWN] = gl[0:OWN]
        bulk(lambda e: Sr[e], HOW["s"])
        ph = face_z(hs, HOW["s"])
        face_to_all(ph, HOW["s"])
        FXr[1] = FXr[1] + face_to_face((-k_f) * DFr[...] * h, HOW["s"])
        add_faces(Sr, (), (-k_f) * DFr[...] * h)
        coarse(k).arrive()
        gr[OWN:] = cr[k]
        for a, b, n in coarse_pairs():
            t = gr[a : a + n] + gr[b : b + n]
            gr[a : a + n] = t
            gr[b : b + n] = t
        p = lmul(const["Gc"], Cc_r[...] * (Dc_r[...] * inv_center_c) * gr[...], n=HOW["c"])
        o = rmul(jnp.concatenate([p[:OWN], p[OWN:]], 1), const["Bc"], HOW["c"])
        g = gr[0:OWN]
        fix = Dc_r[0:OWN] * (a_c * g - k_c * o)
        fix_c = Cc_r[0:OWN] * fix
        p = lmul(const["Gjf"], fix_c, n=HOW["d"])
        o = rmul(jnp.concatenate([p[:96], p[96:]], 1), const["Bjv"], HOW["d"])
        send_faces(4 * k + 2, FXr[1] + o)
        p = rmul(fix_c, const["Bj"], HOW["d"], slice(0, 2 * ZF))
        o = lmul(const["Gj"], p[:, :ZF], p[:, ZF:], n=HOW["d"])
        p = rmul(fix, const["Bj"], HOW["d"], slice(2 * ZF, 3 * ZF))
        up = lmul(const["Gp"], p, n=HOW["d"])
        for e in range(EX):
            part = slice(e * ROWS, (e + 1) * ROWS)
            Sr[e] = Sr[e] + up[part]
            Rr[e] = Fr[k, e] - Lr[e] - o[part]
        bulk(lambda e: (Dr[e] * inv_center) * Rr[e], HOW["e"])
        h = halo(4 * k + 2)
        send_faces(4 * k + 3, FXr[1] + face_to_face((-inv_center) * DFr[...] * h, HOW["e"]))
        add_faces(Rr, (), -h)
        face_to_all(face_z((-inv_center) * DcFr[...] * h, HOW["e"]), HOW["e"])
        for e in range(EX):
            Zr[k, e] = Sr[e] + Dr[e] * (a_f * Rr[e] - k_f * Lr[e])
        bulk(lambda e: Zr[k, e], HOW["f"])
        sums = [0.0] * 3
        for e in range(EX):
            z = Zr[k, e]
            wz = Wr[...] * z
            for i, t in enumerate((Fr[0, e] * wz, Fr[k, e] * wz, WLr[...] * Lr[e] * z)):
                sums[i] = sums[i] + total(t)
        h = halo(4 * k + 3)
        delta = (-k_f) * DFr[...] * h
        ff = face_to_face(delta, HOW["h"])
        Er[...] = FXr[1] + ff
        pl.when(k == 0)(lambda: send_faces(4 * k + 4, Er[...]))
        wd = WFr[...] * delta
        faces = (FFr[0] * wd, FFr[k] * wd, WLFr[...] * delta * (2.0 * FXr[1] + ff))
        for i, t in enumerate(faces):
            dots[k, i : i + 1] = sums[i] + total(t)
        Hr[...] = h
        return carry

    add_faces(Fr, (0,), halo(0))
    lax.fori_loop(0, 2, cycle, 0)

    def reduce_stage(buf, stage, base):
        return [
            pltpu.make_async_remote_copy(
                src_ref=buf.at[0], dst_ref=buf.at[j + 1], send_sem=dsend_sem.at[base + j], recv_sem=drecv_sem.at[base + j],
                device_id=p, device_id_type=MESH,
            )
            for j, p in enumerate(stage)
        ]

    def summed(buf, stage, n):
        for c in stage:
            c.wait_recv()
        out = buf[0]
        for j in range(n):
            out = out + buf[j + 1]
        return out

    d1[0, 0:3] = dots[0, 0:3]
    d1[0, 3:6] = dots[1, 0:3]
    d1[0, 6:8] = jnp.zeros((2, 128), F32)
    stage1 = reduce_stage(d1, stages[0], 0)
    stage2 = reduce_stage(d2, stages[1], len(stage1))
    for c in stage1:
        c.start()
    send_faces(8, Er[...])
    finish(1)
    d2[0] = summed(d1, stage1, len(stage1))
    for c in stage2:
        c.start()
    tile_exchange.drain()
    for c in stage1:
        c.wait_send()

    def drain(i, carry):
        fine(i).drain()
        return carry

    lax.fori_loop(0, 9, drain, 0)
    for k in range(2):
        coarse(k).drain()
    h = halo(8)
    add_faces(Fr, (2,), h)
    lanes_sum = jnp.sum(summed(d2, stage2, len(stage2)), axis=1, keepdims=True)
    pick = lambda i: lanes_sum[i : i + 1, 0:1]
    rz0, c00 = pick(1), pick(2)
    r0u, wu, uv = pick(3), pick(4), pick(5)
    alpha0 = rz0 / c00
    rz1 = alpha0 * (alpha0 * wu - r0u)
    beta1 = 1.0 + rz1 / rz0
    curve = beta1 * beta1 * c00 - 2.0 * beta1 * alpha0 * wu + alpha0 * alpha0 * uv
    alpha1 = rz1 / curve
    c_z = alpha0 + alpha1 * beta1
    c_u = alpha1 * alpha0
    for e in range(EX):
        sol_ref[e] = c_z * Zr[0, e] - c_u * Zr[1, e]
        res_ref[e] = Fr[0, e] - c_z * Fr[1, e] + c_u * Fr[2, e]
    for c in stage2:
        c.wait_send()


def solution(mesh):
    gxn, gyn = mesh.shape["gx"], mesh.shape["gy"]
    table = constants()
    names = tuple(table)
    n_dots = gyn - 1 + gxn - 1

    def per_device(right_side, coefficient):
        rhs = right_side.reshape(EX, ROWS, ZF)
        field = (EX, ROWS, ZF)
        vm = lambda *s: pltpu.VMEM(s, F32)
        dma = lambda *s: pltpu.SemaphoreType.DMA(s)
        face = (96, ZF)
        scratch = [pltpu.VMEM(table[m].shape, table[m].dtype) for m in names]
        scratch += [
            vm(3, *field), vm(2, *field), vm(*field), vm(*field), vm(*field), vm(*face), vm(*face), vm(384, ZC), vm(*face), vm(*face),
            vm(*field), vm(*field), vm(*field), vm(*field), vm(2, *face), vm(2, *face), vm(*face),
            vm(ROWS, ZF), vm(ROWS, ZF), vm(*face), vm(*face),
            vm(384, ZC), vm(384, ZC), vm(8, 128), vm(EX, EY, EZ), vm(80, 128),
            vm(9, 2, YF, ZF), vm(9, 2, EX * N, ZF), vm(9, 2, YF, ZF), vm(9, 2, EX * N, ZF), vm(9, 2, EX * N, ZF),
            vm(2, 192, ZC), vm(2, 256, ZC),
            vm(2, 8, 128), vm(gyn, 8, 128), vm(gxn, 8, 128),
            dma(len(names) + 2), dma(9, 8), dma(9, 8), dma(2, 8), dma(2, 8), dma(8), dma(8), dma(n_dots), dma(n_dots),
        ]
        sol, res = pl.pallas_call(
            functools.partial(kernel_body, (gxn, gyn), names),
            out_shape=[pltpu.VMEM(field, F32)] * 2,
            in_specs=[pl.BlockSpec(memory_space=pl.ANY)] * (2 + len(names)),
            out_specs=[pl.BlockSpec(memory_space=pltpu.VMEM)] * 2,
            scratch_shapes=scratch,
            compiler_params=pltpu.CompilerParams(
                collective_id=0, has_side_effects=True, vmem_limit_bytes=56 * 2**20
            ),
        )(rhs, coefficient, *[jnp.asarray(table[m]) for m in names])
        def inner(dim, axis, n):
            i = lax.broadcasted_iota(jnp.int32, right_side.shape, dim)
            here = lax.axis_index(axis) * right_side.shape[dim] if axis else 0
            return (i != -here) & (i != n * right_side.shape[dim] - 1 - here)

        keep = inner(0, "gx", gxn) & inner(1, "gy", gyn) & inner(2, None, 1)
        zeroed = lambda x: jnp.where(keep, x.reshape(right_side.shape), 0.0)
        return zeroed(sol), zeroed(res)

    spec = P("gx", "gy", None)
    return jax.shard_map(
        per_device, mesh=mesh, in_specs=(spec, spec), out_specs=(spec, spec), check_vma=False
    )
```

```python
import functools
import math

import jax
import jax.numpy as jnp
import numpy as np
from jax import lax
from jax.experimental import pallas as pl
from jax.experimental.pallas import tpu as pltpu
from jax.sharding import PartitionSpec as P

ORDER = 7
COARSE_ORDER = 3
F32 = jnp.float32
BF16 = jnp.bfloat16
MESH = pl.DeviceIdType.MESH

EX, EY, EZ = 2, 4, 32
N, NC = ORDER + 1, COARSE_ORDER + 1
YF, ZF = EY * N, EZ * N
YC, ZC = EY * NC, EZ * NC
ROWS = N * YF
ROWS_C = NC * YC


def legendre_pair(degree, points):
    before = points * 0.0 + 1.0
    now = points.copy()
    for power in range(2, degree + 1):
        after = ((2 * power - 1) * points * now - (power - 1) * before) / power
        before = now
        now = after
    return (now, before)


def gll_tables(degree):
    number = degree + 1
    points = np.cos(math.pi * np.arange(number) / degree)
    for newton in range(60):
        top, below = legendre_pair(degree, points)
        points = points - (points * top - below) / (number * top)
    points = points[::-1].copy()
    points[0] = -1.0
    points[degree] = 1.0
    values = legendre_pair(degree, points)[0]
    weights = 2.0 / (degree * (degree + 1) * values**2)
    derivative = np.zeros((number, number))
    for row_index in range(number):
        for column_index in range(number):
            if row_index != column_index:
                derivative[row_index, column_index] = values[row_index] / (
                    values[column_index] * (points[row_index] - points[column_index])
                )
    derivative[0, 0] = -degree * (degree + 1) / 4.0
    derivative[degree, degree] = degree * (degree + 1) / 4.0
    stiffness = derivative.T @ (weights[:, None] * derivative)
    return (points, weights, stiffness)


def upper_bound(degree):
    points, weights, stiffness = gll_tables(degree)
    rowsum = np.abs(stiffness).sum(1)
    diagonal = np.diag(stiffness)
    outer = lambda a, b, c: a[:, None, None] * b[None, :, None] * c[None, None, :]
    top = outer(rowsum, weights, weights) + outer(weights, rowsum, weights) + outer(weights, weights, rowsum)
    bottom = outer(diagonal, weights, weights) + outer(weights, diagonal, weights) + outer(weights, weights, diagonal)
    return float((top / bottom).max())


def interpolation_matrix(fine_degree, coarse_degree):
    fine_points = gll_tables(fine_degree)[0]
    coarse_points = gll_tables(coarse_degree)[0]
    matrix = np.ones((fine_degree + 1, coarse_degree + 1))
    for column_index in range(coarse_degree + 1):
        for other_index in range(coarse_degree + 1):
            if other_index != column_index:
                matrix[:, column_index] *= (fine_points - coarse_points[other_index]) / (
                    coarse_points[column_index] - coarse_points[other_index]
                )
    return matrix


def cheb_numbers(degree):
    upper = upper_bound(degree)
    lower = 0.1 * upper
    center = 0.5 * (upper + lower)
    half = 0.5 * (upper - lower)
    previous = half / center
    current = 1.0 / (2.0 * center / half - previous)
    k = 2.0 * current / half
    return (1.0 / center, (1.0 + current * previous) / center + k, k)


def sum_matrix(elements, number):
    matrix = np.eye(elements * number)
    for e in range(elements - 1):
        a, b = e * number + number - 1, (e + 1) * number
        matrix[a, b] = matrix[b, a] = 1.0
    return matrix


def blocks(count, matrix):
    return np.kron(np.eye(count), matrix)


TERMS = ((0, 0), (1, 0), (0, 1), (2, 0), (0, 2), (1, 1))
HOW = dict(a=3, b=3, s=6, c=3, d=6, e=3, f=6, g=3, h=3)


def pieces_of(matrix, count):
    rest, out = np.asarray(matrix, np.float64), []
    for _ in range(count):
        out.append(rest.astype(np.float32).astype(BF16))
        rest = rest - out[-1].astype(np.float64)
    return out


def right3(matrix, steps="asef"):
    p = pieces_of(matrix, 3)
    return np.concatenate([p[j] for _, j in TERMS[: max(HOW[t] for t in steps)]], 0)


def left3(matrix, steps="asef"):
    p = pieces_of(matrix, 3)
    return np.concatenate([p[j] for _, j in TERMS[: max(HOW[t] for t in steps)]], 1)


def level_matrices(degree):
    _, w, K = gll_tables(degree)
    n = degree + 1
    wy = np.tile(w, EY)
    M0 = np.kron(K, np.diag(wy)) + np.kron(np.diag(w), blocks(EY, K))
    N0 = np.kron(np.diag(w), np.diag(wy))
    return M0, N0, np.diag(np.tile(w, EZ)), blocks(EZ, K)


def face_rows(n):
    y = EY * n
    x = EX * n
    rows = [j for j in range(y)] + [(x - 1) * y + j for j in range(y)]
    rows += [i * y for i in range(x)] + [i * y + y - 1 for i in range(x)]
    return np.array(rows)


def coarse_places():
    XC = EX * NC
    before, after_x, after_y = range(-NC, 0), range(XC, XC + NC), range(YC, YC + NC)
    grids = [(range(XC), range(YC)), (before, range(YC)), (after_x, range(YC)), (range(XC), before), (range(XC), after_y)]
    grids += [(a, b) for a in (before, after_x) for b in (before, after_y)]
    both = [(x, y) for xs, ys in grids for x in xs for y in ys]
    return np.array([p[0] for p in both]), np.array([p[1] for p in both])


def coarse_pairs():
    x, y = coarse_places()
    row = {p: i for i, p in enumerate(zip(x.tolist(), y.tolist()))}
    XC, out = EX * NC, []
    for a, b in ((-1, 0), (XC - 1, XC)):
        for first, n in ((-NC, NC), (0, YC), (YC, NC)):
            out.append((row[a, first], row[b, first], n))
    for a, b in ((-1, 0), (YC - 1, YC)):
        out += [(row[i, a], row[i, b], 1) for i in range(-NC, XC + NC)]
    return out


@functools.cache
def constants():
    J = interpolation_matrix(ORDER, COARSE_ORDER)
    out = {}
    M0, N0, Wz, Kz = level_matrices(ORDER)
    Sz, Szc = sum_matrix(EZ, N), sum_matrix(EZ, NC)
    Sxy = np.kron(sum_matrix(EX, N), sum_matrix(EY, N))
    Sxyc = np.kron(sum_matrix(EX, NC), sum_matrix(EY, NC))
    Mf, Nf = blocks(EX, M0), blocks(EX, N0)
    SM, SN = Sxy @ Mf, Sxy @ Nf
    F = face_rows(N)
    out["Bf"] = right3(np.concatenate([Wz @ Sz, Kz @ Sz], 1))
    _, w, K = gll_tables(ORDER)
    wxy, wz = np.kron(w, np.tile(w, EY)), np.tile(w, EZ)
    out["Mh"] = left3(M0 / wxy[:, None])
    out["Kh"] = right3(Kz / wz[None, :])
    out["w3"] = (wxy[:, None] * wz[None, :]).astype(np.float32)
    y, z = np.arange(ROWS) % YF, np.arange(ZF)
    wide = lambda m, shape: np.broadcast_to(m, shape).astype(np.float32)
    out["yu"] = wide(((y % N == N - 1) & (y != YF - 1))[:, None], (ROWS, 128))
    out["yd"] = wide(((y % N == 0) & (y != 0))[:, None], (ROWS, 128))
    out["zu"] = wide(((z % N == N - 1) & (z != ZF - 1))[None, :], (8, ZF))
    out["zd"] = wide(((z % N == 0) & (z != 0))[None, :], (8, ZF))
    Sy = np.kron(np.eye(EX * N), sum_matrix(EY, N))
    out["Mff"] = left3(blocks(EX, M0 / wxy[:, None])[F][:, F])
    out["Kz1"] = right3((Kz / wz[None, :])[:128, :128])
    out["w3f"] = (np.tile(wxy, EX)[F][:, None] * wz[None, :]).astype(np.float32)
    along = np.concatenate([np.arange(YF), np.arange(YF), np.arange(EX * N), np.arange(EX * N)])
    ends = np.concatenate([np.full(2 * YF, YF), np.full(2 * EX * N, EX * N)])
    out["fu"] = wide(((along % N == N - 1) & (along != ends - 1))[:, None], (96, 128))
    out["fd"] = wide(((along % N == 0) & (along != 0))[:, None], (96, 128))
    for e in range(EX):
        rows = slice(e * ROWS, (e + 1) * ROWS)
        here = np.concatenate([np.arange(e * YF, (e + 1) * YF), np.arange(2 * YF, len(F))])
        keep = ((F[here] // ROWS) == e).astype(float)[None, :]
        full = np.concatenate([(Sy @ Mf)[rows][:, F[here]] * keep, (Sy @ Nf)[rows][:, F[here]] * keep], 1)
        out[f"F2A{e}"] = left3(full)
    Rxy = blocks(EX, np.kron(J.T, blocks(EY, J.T)))
    JZ = blocks(EZ, J)
    XC = EX * NC
    first = [x * YC + y for x in range(XC) for y in range(NC)]
    last = [x * YC + YC - NC + y for x in range(XC) for y in range(NC)]
    selc = np.concatenate([np.arange(XC * YC), first, last]).astype(int)
    RM, RN = (Sxyc @ Rxy @ Mf)[selc], (Sxyc @ Rxy @ Nf)[selc]
    out["Br"] = right3(np.concatenate([Wz @ JZ @ Szc, Kz @ JZ @ Szc], 1), "b")
    for e in range(EX):
        cols = slice(e * ROWS, (e + 1) * ROWS)
        out[f"Gr{e}"] = left3(np.concatenate([RM[:, cols], RN[:, cols]], 1), "b")
    out["F2R"] = left3(np.concatenate([RM[:, F], RN[:, F]], 1), "b")
    inv = lambda count: np.where((np.arange(count) % N == 0) | (np.arange(count) % N == N - 1), 0.5, 1.0)
    Wxy = np.kron(np.diag(inv(EX * N)), np.diag(inv(YF)))
    RW = (Sxyc @ Rxy @ Wxy)[selc]
    out["Bw"] = right3(np.diag(inv(ZF)) @ JZ @ Szc, "b")
    out["Gw"] = left3(RW, "b")
    _, wc, Kc = gll_tables(COARSE_ORDER)
    Wzc, Kzc = np.diag(np.tile(wc, EZ)), blocks(EZ, Kc)
    out["Bc"] = right3(np.concatenate([Wzc @ Szc, Kzc @ Szc], 0), "c")
    cx, cy = coarse_places()
    grid = (cx + NC) * (YC + 2 * NC) + cy + NC
    wx4, wy6 = np.diag(np.tile(wc, EX + 2)), np.diag(np.tile(wc, EY + 2))
    Me = np.kron(blocks(EX + 2, Kc), wy6) + np.kron(wx4, blocks(EY + 2, Kc))
    Ne = np.kron(wx4, wy6)
    Se = np.kron(sum_matrix(EX + 2, NC), sum_matrix(EY + 2, NC))
    own = grid[: XC * YC]
    out["Gc"] = left3(np.concatenate([(Se @ Me)[own][:, grid], (Se @ Ne)[own][:, grid]], 0), "c")
    pick = np.zeros((len(cx), 80))
    for i, (x, y) in enumerate(zip(cx // NC, cy // NC)):
        pick[i, ((x // EX + 1) * 3 + y // EY + 1) * 8 + (x % EX) * EY + y % EY] = 1.0
    out["Pc"] = np.concatenate([pick.astype(np.float32).astype(BF16)] * 3, 1)
    Jxy = blocks(EX, np.kron(J, blocks(EY, J)))
    out["Bj"] = right3(np.concatenate([JZ.T @ Wz @ Sz, JZ.T @ Kz @ Sz, JZ.T], 1), "d")
    out["Bjv"] = right3(np.concatenate([JZ.T @ Wz @ Sz, JZ.T @ Kz @ Sz], 0), "d")
    JM, JN = SM @ Jxy, SN @ Jxy
    out["Gj"] = left3(np.concatenate([JM, JN], 1), "d")
    out["Gjf"] = left3(np.concatenate([JM[F], JN[F]], 0), "d")
    out["Gp"] = left3(Jxy, "d")
    fine_x, fine_y = np.divmod(np.arange(EX * ROWS), YF)
    places = {"f": (np.concatenate([fine_x, F // YF]), np.concatenate([fine_y, F % YF])), "c": (cx, cy)}
    for name, degree in (("f", ORDER), ("c", COARSE_ORDER)):
        n = degree + 1
        _, w, K = gll_tables(degree)
        kd = np.diag(K)
        S = sum_matrix(EZ, n)
        spread_w = np.zeros((128, EZ * n))
        spread_k = np.zeros((128, EZ * n))
        for ez in range(EZ):
            spread_w[ez, ez * n : (ez + 1) * n] = w
            spread_k[ez, ez * n : (ez + 1) * n] = kd
        out["Bd" + name] = right3(np.concatenate([spread_w @ S, spread_k @ S], 1), "g")
        left = np.zeros((len(places[name][0]), 2, 80))
        for i, (x, y) in enumerate(zip(*places[name])):
            xs = [(x // n, x % n)]
            if x % n == 0:
                xs.append((x // n - 1, n - 1))
            if x % n == n - 1:
                xs.append((x // n + 1, 0))
            ys = [(y // n, y % n)]
            if y % n == 0:
                ys.append((y // n - 1, n - 1))
            if y % n == n - 1:
                ys.append((y // n + 1, 0))
            for ex, a in xs:
                for ey, b in ys:
                    col = ((ex // EX + 1) * 3 + ey // EY + 1) * 8 + (ex % EX) * EY + ey % EY
                    left[i, 0, col] += kd[a] * w[b] + w[a] * kd[b]
                    left[i, 1, col] += w[a] * w[b]
        left = left.reshape(len(left), 160)
        if name == "f":
            here = left.reshape(len(left), 2, 80)[: EX * ROWS, :, 32:40].reshape(EX * ROWS, 16)
            out["Gdo"] = left3(here, "g")
            left = left[EX * ROWS :]
        out["Gd" + name] = left3(left, "g")
    spread = np.zeros((128, ZF + ZC))
    for ez in range(EZ):
        spread[ez, ez * N : (ez + 1) * N] = 1.0
        spread[ez, ZF + ez * NC : ZF + (ez + 1) * NC] = 1.0
    out["Bs"] = np.concatenate([spread.astype(np.float32).astype(BF16)] * 3, 0)
    return out


def dot(a, b):
    return jnp.dot(a, b, preferred_element_type=F32)


def split(x, n):
    out = []
    for i in range(1 + max(i for i, _ in TERMS[:n])):
        out.append(x.astype(BF16))
        x = x - out[-1].astype(F32)
    return out


def rmul(x, b, n, cols=slice(None)):
    p = split(x, n)
    x3 = jnp.concatenate([p[i] for i, _ in TERMS[:n]], 1)
    return dot(x3, b[: x3.shape[1], cols])


def lmul(g, *parts, n, rows=slice(None)):
    split_parts = [split(x, n) for x in parts]
    x3 = jnp.concatenate([p[i] for i, _ in TERMS[:n] for p in split_parts], 0)
    return dot(g[rows, : x3.shape[0]], x3)


def kernel_body(shape, names, rhs_ref, coef_ref, *refs):
    gxn, gyn = shape
    n_const = len(names)
    const_hbm = dict(zip(names, refs[:n_const]))
    sol_ref, res_ref = refs[n_const : n_const + 2]
    rest = refs[n_const + 2 :]
    const = dict(zip(names, rest[:n_const]))
    (Fr, Zr, Dr, Cr, W3r, W3Fr, Er, gr, DFr, DcFr, Lr, Sr, Rr, Ar, FXr, FFr, Hr, Wr, WLr, WFr, WLFr,
     Dc_r, Cc_r, cpad, coef, tiles,
     sx, sy, rx, ry, rc, cs, cr, dots, d1, d2,
     const_sem, send_sem, recv_sem, csend_sem, crecv_sem, tsend_sem, trecv_sem, dsend_sem, drecv_sem) = rest[n_const:]

    inv_center, a_f, k_f = cheb_numbers(ORDER)
    inv_center_c, a_c, k_c = cheb_numbers(COARSE_ORDER)
    px, py = lax.axis_index("gx"), lax.axis_index("gy")
    XF, XC, OWN = EX * N, EX * NC, EX * ROWS_C

    def at(dx, dy):
        return (lax.rem(px + dx + gxn, gxn), lax.rem(py + dy + gyn, gyn))

    def inside(dx, dy):
        ok = None
        for p, d, n in ((px, dx, gxn), (py, dy, gyn)):
            if d:
                here = (p > 0) if d < 0 else (p < n - 1)
                ok = here if ok is None else ok & here
        return ok

    corners = [(dx, dy) for dx in (-1, 1) for dy in (-1, 1)]
    around = corners + [(-1, 0), (1, 0), (0, -1), (0, 1)]
    def ring(coarse_n, fine_n, hops):
        every = [(a, b) for a in range(coarse_n) for b in range(fine_n) if (a, b) != (0, 0)]
        near = lambda d, n: min(d, n - d)
        return sorted(every, key=lambda o: -(near(o[0], coarse_n) + hops * near(o[1], fine_n)))

    def shifted(p, fine_n, coarse_n, o):
        return lax.rem(p // fine_n + o[0], coarse_n) * fine_n + lax.rem(lax.rem(p, fine_n) + o[1], fine_n)

    nz = 8 if gxn % 8 == 0 else 2
    nx, ny = gyn // 2, gxn // nz
    stages = [
        [(px, shifted(py, 2, nx, o)) for o in ring(nx, 2, 0.5)],
        [(shifted(px, nz, ny, o), py) for o in ring(ny, nz, 1)],
    ]

    copies = [pltpu.make_async_copy(const_hbm[m], const[m], const_sem.at[i]) for i, m in enumerate(names)]
    load_rhs = pltpu.make_async_copy(rhs_ref, Ar, const_sem.at[n_const])
    load_coef = pltpu.make_async_copy(coef_ref, coef, const_sem.at[n_const + 1])
    load_rhs.start()
    load_coef.start()

    interior = inside(-1, -1) & inside(1, 1)
    rc[...] = jnp.zeros_like(rc)

    @pl.when(~interior)
    def _():
        for ref in (rx, ry, cr, tiles):
            ref[...] = jnp.zeros_like(ref)


    barrier = pltpu.get_barrier_semaphore()
    expected = 0
    for stage in stages[::-1]:
        for p in stage:
            pl.semaphore_signal(barrier, inc=1, device_id=p, device_id_type=MESH)
        expected = expected + len(stage)
    for d in around:
        pl.when(inside(*d))(
            lambda d=d: pl.semaphore_signal(barrier, inc=1, device_id=at(*d), device_id_type=MESH)
        )
        expected = expected + inside(*d).astype(jnp.int32)
    for c in copies:
        c.start()

    def local_sum(v):
        rows = lax.broadcasted_iota(jnp.int32, v.shape, 0)
        lanes = lax.broadcasted_iota(jnp.int32, v.shape, 1)
        y = lax.rem(rows, YF)
        up = (lax.rem(y, N) == N - 1) & (y != YF - 1)
        down = (lax.rem(y, N) == 0) & (y != 0)
        v = v + jnp.where(up, pltpu.roll(v, ROWS - 1, 0), 0.0) + jnp.where(down, pltpu.roll(v, 1, 0), 0.0)
        up = (lax.rem(lanes, N) == N - 1) & (lanes != ZF - 1)
        down = (lax.rem(lanes, N) == 0) & (lanes != 0)
        return v + jnp.where(up, pltpu.roll(v, ZF - 1, 1), 0.0) + jnp.where(down, pltpu.roll(v, 1, 1), 0.0)

    def middle(ref, *index):
        total = ref[(*index, 0, pl.ds(ROWS - YF, YF))] + ref[(*index, 1, pl.ds(0, YF))]
        ref[(*index, 0, pl.ds(ROWS - YF, YF))] = total
        ref[(*index, 1, pl.ds(0, YF))] = total

    cpad[...] = jnp.zeros_like(cpad)
    load_coef.wait()
    cpad[0:EY, 0:EZ] = coef[0]
    cpad[EY : 2 * EY, 0:EZ] = coef[1]
    load_rhs.wait()
    for e in range(EX):
        Fr[0, e] = local_sum(Ar[e])
    middle(Fr, 0)
    sx[0, 0] = Fr[0, 0, 0:YF]
    sx[0, 1] = Fr[0, 1, ROWS - YF : ROWS]
    for x in range(XF):
        e, r = x // N, (x % N) * YF
        sy[0, 0, x : x + 1] = Fr[0, e, r : r + 1]
        sy[0, 1, x : x + 1] = Fr[0, e, r + YF - 1 : r + YF]

    class Exchange:
        def __init__(self, plan, send, recv):
            self.plan = [
                (pltpu.make_async_remote_copy(
                    src_ref=s, dst_ref=t, send_sem=send(j), recv_sem=recv(j), device_id=at(*d), device_id_type=MESH,
                ), inside(*d), inside(-d[0], -d[1]))
                for j, (s, t, d) in enumerate(plan)
            ]

        def start(self):
            @pl.when(interior)
            def _():
                for c, _, _ in self.plan:
                    c.start()

            @pl.when(~interior)
            def _():
                for c, to, _ in self.plan:
                    pl.when(to)(c.start)

        def arrive(self):
            @pl.when(interior)
            def _():
                for c, _, _ in self.plan:
                    c.wait_recv()

            @pl.when(~interior)
            def _():
                for c, _, come in self.plan:
                    pl.when(come)(c.wait_recv)

        def drain(self):
            for c, to, _ in self.plan:
                pl.when(to)(c.wait_send)

    def fine(i):
        one = lambda r: pl.ds(r, 1)
        plan = [
            (sy.at[i, 0, one(0)], rc.at[i, 1, one(XF - 1)], (-1, -1)),
            (sy.at[i, 1, one(0)], rc.at[i, 0, one(XF - 1)], (-1, 1)),
            (sy.at[i, 0, one(XF - 1)], rc.at[i, 1, one(0)], (1, -1)),
            (sy.at[i, 1, one(XF - 1)], rc.at[i, 0, one(0)], (1, 1)),
            (sx.at[i, 0], rx.at[i, 1], (-1, 0)),
            (sx.at[i, 1], rx.at[i, 0], (1, 0)),
            (sy.at[i, 0], ry.at[i, 1], (0, -1)),
            (sy.at[i, 1], ry.at[i, 0], (0, 1)),
        ]
        return Exchange(plan, lambda j: send_sem.at[i, j], lambda j: recv_sem.at[i, j])

    def coarse(k):
        h, q = ROWS_C, NC * NC
        y0, y1 = OWN, OWN + XC * NC
        c0 = 2 * h + 4 * q
        src = lambda a, n: cs.at[k, pl.ds(a, n)]
        dst = lambda a, n: cr.at[k, pl.ds(a, n)]
        plan = [
            (src(y0, q), dst(c0 + 3 * q, q), (-1, -1)),
            (src(y1, q), dst(c0 + 2 * q, q), (-1, 1)),
            (src(y0 + q, q), dst(c0 + q, q), (1, -1)),
            (src(y1 + q, q), dst(c0, q), (1, 1)),
            (src(0, h), dst(h, h), (-1, 0)),
            (src(h, h), dst(0, h), (1, 0)),
            (src(y0, 2 * q), dst(2 * h + 2 * q, 2 * q), (0, -1)),
            (src(y1, 2 * q), dst(2 * h, 2 * q), (0, 1)),
        ]
        return Exchange(plan, lambda j: csend_sem.at[k, j], lambda j: crecv_sem.at[k, j])

    pl.semaphore_wait(barrier, expected)

    tile_plan = []
    for dx, dy in around:
        slot = ((1 - dx) * 3 + (1 - dy)) * 8
        tile_plan.append((cpad, tiles.at[pl.ds(slot, 8)], (dx, dy)))
    tile_exchange = Exchange(tile_plan, lambda j: tsend_sem.at[j], lambda j: trecv_sem.at[j])
    tile_exchange.start()
    fine(0).start()
    tiles[32:40] = cpad[...]

    for c in copies:
        c.wait()

    def spread(x):
        h1 = x.astype(BF16)
        r1 = x - h1.astype(F32)
        h2 = r1.astype(BF16)
        return [h1, h2, (r1 - h2.astype(F32)).astype(BF16)]

    spread_own = dot(jnp.concatenate(spread(cpad[...]), 1), const["Bs"][...])
    for e in range(EX):
        lines = [spread_own[e * EY + ey : e * EY + ey + 1] for ey in range(EY)]
        cf = [jnp.broadcast_to(l[:, :ZF], (N, ZF)) for l in lines]
        one = jnp.concatenate(cf, 0)
        Cr[e] = jnp.concatenate([one] * N, 0)
        W3r[e] = Cr[e] * const["w3"][...]
        FXr[0, e * YF : (e + 1) * YF] = one
        FXr[0, 2 * YF + e * N : 2 * YF + (e + 1) * N] = cf[0]
        FXr[0, 2 * YF + (EX + e) * N : 2 * YF + (EX + e + 1) * N] = cf[EY - 1]

    W3Fr[...] = FXr[0] * const["w3f"][...]

    rows = lax.broadcasted_iota(jnp.int32, (ROWS, ZF), 0)
    lanes = lax.broadcasted_iota(jnp.int32, (ROWS, ZF), 1)
    xr, yr = rows // YF, lax.rem(rows, YF)
    frow = lax.broadcasted_iota(jnp.int32, (96, ZF), 0)
    flane = lax.broadcasted_iota(jnp.int32, (96, ZF), 1)
    fx = jnp.where(frow < YF, 0, jnp.where(frow < 2 * YF, XF - 1, lax.rem(frow, XF)))
    fy = jnp.where(frow < 2 * YF, lax.rem(frow, YF), jnp.where(frow < 2 * YF + XF, 0, YF - 1))

    def edge(i, count=0):
        e = (lax.rem(i, N) == 0) | (lax.rem(i, N) == N - 1)
        return jnp.where(e & (i != 0) & (i != count - 1) if count else e, 0.5, 1.0)

    Wr[...] = edge(lanes) * edge(yr) * edge(xr)
    WLr[...] = edge(lanes) * edge(yr, YF)
    WFr[...] = edge(flane) * edge(fx) * edge(fy)
    WLFr[...] = edge(flane) * edge(fx, XF) * edge(fy, YF)

    def mask_of(x, y, z, n):
        inner = (x > 0) & (x < gxn * EX * n - 1) & (y > 0) & (y < gyn * EY * n - 1)
        return inner & (z != 0) & (z != EZ * n - 1)

    pd = rmul(cpad[...], const["Bdf"], HOW["g"])
    diag = lmul(const["Gdo"], jnp.concatenate([pd[:, :ZF], pd[:, ZF:]], 0), n=HOW["g"])
    for e in range(EX):
        keep = mask_of(px * XF + e * N + xr, py * YF + yr, lanes, N)
        Dr[e] = jnp.where(keep, 1.0 / diag[e * ROWS : (e + 1) * ROWS], 0.0)
    fkeep = mask_of(px * XF + fx, py * YF + fy, flane, N)
    tile_exchange.arrive()
    pd = rmul(tiles[...], const["Bdf"], HOW["g"])
    diag = lmul(const["Gdf"], pd[:, :ZF], pd[:, ZF:], n=HOW["g"])
    df = jnp.where(fkeep, 1.0 / diag, 0.0)
    DFr[...] = df
    DcFr[...] = df * FXr[0]
    Dr[0, 0:YF] = df[0:YF]
    Dr[1, ROWS - YF : ROWS] = df[YF : 2 * YF]
    for x in range(XF):
        e, r = x // N, (x % N) * YF
        Dr[e, r : r + 1] = df[2 * YF + x : 2 * YF + x + 1]
        b = 2 * YF + XF + x
        Dr[e, r + YF - 1 : r + YF] = df[b : b + 1]

    def coarse_setup():
        ext = tiles[...]
        pdc = rmul(ext, const["Bdc"], HOW["g"])
        diag_c = lmul(const["Gdc"], pdc[:, :ZC], pdc[:, ZC:], n=HOW["g"])
        crow = lax.broadcasted_iota(jnp.int32, (384, ZC), 0)
        clane = lax.broadcasted_iota(jnp.int32, (384, ZC), 1)

        def place(r, width, x0, y0):
            return (x0 + r // width, y0 + lax.rem(r, width))

        cx, cy = place(crow, YC, 0, 0)
        base = OWN
        for count, width, x0, y0 in (
            (ROWS_C, YC, -NC, 0), (ROWS_C, YC, XC, 0), (XC * NC, NC, 0, -NC), (XC * NC, NC, 0, YC),
            (16, NC, -NC, -NC), (16, NC, -NC, YC), (16, NC, XC, -NC), (16, NC, XC, YC),
        ):
            nx, ny = place(crow - base, width, x0, y0)
            cx, cy = jnp.where(crow >= base, nx, cx), jnp.where(crow >= base, ny, cy)
            base += count
        keep = mask_of(px * XC + cx, py * YC + cy, clane, NC)
        Dc_r[...] = jnp.where(keep, 1.0 / diag_c, 0.0)
        lines = dot(jnp.concatenate(spread(ext), 1), const["Bs"][:, ZF:])
        Cc_r[...] = dot(const["Pc"][...], jnp.concatenate(spread(lines), 0))

    def halo(i):
        fine(i).arrive()
        return jnp.concatenate([rx[i, 0], rx[i, 1], ry[i, 0] + rc[i, 0], ry[i, 1] + rc[i, 1]], 0)

    def add_faces(ref, index, h):
        ref[(*index, 0, pl.ds(0, YF))] += h[0:YF]
        ref[(*index, 1, pl.ds(ROWS - YF, YF))] += h[YF : 2 * YF]
        for x in range(XF):
            e, r = x // N, (x % N) * YF
            ref[(*index, e, pl.ds(r, 1))] += h[2 * YF + x : 2 * YF + x + 1]
            b = 2 * YF + XF + x
            ref[(*index, e, pl.ds(r + YF - 1, 1))] += h[b : b + 1]

    def sums_inside(v):
        wide = lambda name: jnp.concatenate([const[name][...]] * 2, 1)
        v = v + wide("yu") * pltpu.roll(v, ROWS - 1, 0) + wide("yd") * pltpu.roll(v, 1, 0)
        return v + const["zu"][0:1] * pltpu.roll(v, ZF - 1, 1) + const["zd"][0:1] * pltpu.roll(v, 1, 1)

    def bulk(values, n):
        for e in range(EX):
            p = split(values(e), n)
            p = [p[i] for i, _ in TERMS[:n]]
            t = dot(const["Mh"][:, : n * ROWS], jnp.concatenate(p, 0))
            t = t + dot(jnp.concatenate(p, 1), const["Kh"][: n * ZF])
            Lr[e] = sums_inside(W3r[e] * t)
        FXr[1, 0:YF] = Lr[0, 0:YF]
        FXr[1, YF : 2 * YF] = Lr[1, ROWS - YF : ROWS]
        for side, y in ((2 * YF, 0), (2 * YF + XF, YF - 1)):
            for x in range(XF):
                e, r = x // N, (x % N) * YF + y
                FXr[1, side + x : side + x + 1] = Lr[e, r : r + 1]
            both = Lr[0, ROWS - YF + y : ROWS - YF + y + 1] + Lr[1, y : y + 1]
            FXr[1, side + N - 1 : side + N] = both
            FXr[1, side + N : side + N + 1] = both

    def face_z(hs, n):
        return rmul(hs, const["Bf"], n)

    def send_faces(i, faces):
        sx[i, 0] = faces[0:YF]
        sx[i, 1] = faces[YF : 2 * YF]
        sy[i, 0] = faces[2 * YF : 2 * YF + XF]
        sy[i, 1] = faces[2 * YF + XF :]
        fine(i).start()

    def face_to_face(delta, n):
        p = split(delta, n)
        p = [p[i] for i, _ in TERMS[:n]]
        t = dot(const["Mff"][:, : n * 96], jnp.concatenate(p, 0))
        halves = [jnp.concatenate([q[:, :128], q[:, 128:]], 0) for q in p]
        r = dot(jnp.concatenate(halves, 1), const["Kz1"][: n * 128])
        Er[...] = jnp.concatenate([r[:96], r[96:]], 1)
        for a, b in ((0, 2 * YF), (YF - 1, 2 * YF + XF), (YF, 2 * YF + XF - 1), (2 * YF - 1, 2 * YF + 2 * XF - 1)):
            both = Er[a : a + 1] + Er[b : b + 1]
            Er[a : a + 1] = both
            Er[b : b + 1] = both
        v = W3Fr[...] * (t + Er[...])
        wide = lambda name: jnp.concatenate([const[name][...]] * 2, 1)
        v = v + wide("fu") * pltpu.roll(v, 95, 0) + wide("fd") * pltpu.roll(v, 1, 0)
        return v + const["zu"][0:1] * pltpu.roll(v, ZF - 1, 1) + const["zd"][0:1] * pltpu.roll(v, 1, 1)

    def face_to_all(ph, n):
        for e in range(EX):
            part = jnp.concatenate([ph[e * YF : (e + 1) * YF], ph[2 * YF :]], 0)
            Lr[e] += lmul(const[f"F2A{e}"], part[:, :ZF], part[:, ZF:], n=n)
        middle(Lr)

    def finish(k):
        add_faces(Zr, (k,), (-k_f) * DFr[...] * Hr[...])
        face_to_all(face_z((-k_f) * DcFr[...] * Hr[...], HOW["h"]), HOW["h"])
        for e in range(EX):
            Fr[k + 1, e] = Lr[e]

    def total(x):
        x = jnp.sum(x, axis=0, keepdims=True)
        return x[:, : ZF // 2] + x[:, ZF // 2 :]

    def cycle(k, carry):
        pl.when(k > 0)(lambda: finish(k - 1))
        bulk(lambda e: (Dr[e] * inv_center) * Fr[k, e], HOW["a"])
        @pl.when(k > 0)
        def _():
            h = halo(4 * k)
            FXr[1] = FXr[1] + face_to_face(DFr[...] * inv_center * h, HOW["a"])
            Hr[...] = h

        send_faces(4 * k + 1, FXr[1])

        @pl.when(k > 0)
        def _():
            add_faces(Fr, (k,), Hr[...])
            face_to_all(face_z(DcFr[...] * inv_center * Hr[...], HOW["a"]), HOW["a"])

        @pl.when(k == 0)
        def _():
            middle(Lr)
            coarse_setup()

        FFr[k, 0:YF] = Fr[k, 0, 0:YF]
        FFr[k, YF : 2 * YF] = Fr[k, 1, ROWS - YF : ROWS]
        for x in range(XF):
            e, r = x // N, (x % N) * YF
            FFr[k, 2 * YF + x : 2 * YF + x + 1] = Fr[k, e, r : r + 1]
            b = 2 * YF + XF + x
            FFr[k, b : b + 1] = Fr[k, e, r + YF - 1 : r + YF]
        gl = None
        for e in range(EX):
            s = Dr[e] * (a_f * Fr[k, e] - k_f * Lr[e])
            Sr[e] = s
            p = rmul(Cr[e] * s, const["Br"], HOW["b"])
            Ar[e, :, 0:ZC] = rmul(Fr[k, e], const["Bw"], HOW["b"])
            o = lmul(const[f"Gr{e}"], p[:, :ZC], p[:, ZC:], n=HOW["b"])
            gl = o if e == 0 else gl + o
        gl = lmul(const["Gw"], Ar[0, :, 0:ZC], Ar[1, :, 0:ZC], n=HOW["b"]) - gl
        h = halo(4 * k + 1)
        hs = (-k_f) * DcFr[...] * h
        pr = rmul(hs, const["Br"], HOW["b"])
        gl = gl - lmul(const["F2R"], pr[:, :ZC], pr[:, ZC:], n=HOW["b"])
        cs[k] = gl
        coarse(k).start()
        gr[0:OWN] = gl[0:OWN]
        bulk(lambda e: Sr[e], HOW["s"])
        ph = face_z(hs, HOW["s"])
        face_to_all(ph, HOW["s"])
        FXr[1] = FXr[1] + face_to_face((-k_f) * DFr[...] * h, HOW["s"])
        add_faces(Sr, (), (-k_f) * DFr[...] * h)
        coarse(k).arrive()
        gr[OWN:] = cr[k]
        for a, b, n in coarse_pairs():
            t = gr[a : a + n] + gr[b : b + n]
            gr[a : a + n] = t
            gr[b : b + n] = t
        p = lmul(const["Gc"], Cc_r[...] * (Dc_r[...] * inv_center_c) * gr[...], n=HOW["c"])
        o = rmul(jnp.concatenate([p[:OWN], p[OWN:]], 1), const["Bc"], HOW["c"])
        g = gr[0:OWN]
        fix = Dc_r[0:OWN] * (a_c * g - k_c * o)
        fix_c = Cc_r[0:OWN] * fix
        p = lmul(const["Gjf"], fix_c, n=HOW["d"])
        o = rmul(jnp.concatenate([p[:96], p[96:]], 1), const["Bjv"], HOW["d"])
        send_faces(4 * k + 2, FXr[1] + o)
        p = rmul(fix_c, const["Bj"], HOW["d"], slice(0, 2 * ZF))
        o = lmul(const["Gj"], p[:, :ZF], p[:, ZF:], n=HOW["d"])
        p = rmul(fix, const["Bj"], HOW["d"], slice(2 * ZF, 3 * ZF))
        up = lmul(const["Gp"], p, n=HOW["d"])
        for e in range(EX):
            part = slice(e * ROWS, (e + 1) * ROWS)
            Sr[e] = Sr[e] + up[part]
            Rr[e] = Fr[k, e] - Lr[e] - o[part]
        bulk(lambda e: (Dr[e] * inv_center) * Rr[e], HOW["e"])
        h = halo(4 * k + 2)
        send_faces(4 * k + 3, FXr[1] + face_to_face((-inv_center) * DFr[...] * h, HOW["e"]))
        add_faces(Rr, (), -h)
        face_to_all(face_z((-inv_center) * DcFr[...] * h, HOW["e"]), HOW["e"])
        for e in range(EX):
            Zr[k, e] = Sr[e] + Dr[e] * (a_f * Rr[e] - k_f * Lr[e])
        bulk(lambda e: Zr[k, e], HOW["f"])
        sums = [0.0] * 3
        for e in range(EX):
            z = Zr[k, e]
            wz = Wr[...] * z
            for i, t in enumerate((Fr[0, e] * wz, Fr[k, e] * wz, WLr[...] * Lr[e] * z)):
                sums[i] = sums[i] + total(t)
        h = halo(4 * k + 3)
        delta = (-k_f) * DFr[...] * h
        ff = face_to_face(delta, HOW["h"])
        Er[...] = FXr[1] + ff
        pl.when(k == 0)(lambda: send_faces(4 * k + 4, Er[...]))
        wd = WFr[...] * delta
        faces = (FFr[0] * wd, FFr[k] * wd, WLFr[...] * delta * (2.0 * FXr[1] + ff))
        for i, t in enumerate(faces):
            dots[k, i : i + 1] = sums[i] + total(t)
        Hr[...] = h
        return carry

    add_faces(Fr, (0,), halo(0))
    lax.fori_loop(0, 2, cycle, 0)

    def reduce_stage(buf, stage, base):
        return [
            pltpu.make_async_remote_copy(
                src_ref=buf.at[0], dst_ref=buf.at[j + 1], send_sem=dsend_sem.at[base + j], recv_sem=drecv_sem.at[base + j],
                device_id=p, device_id_type=MESH,
            )
            for j, p in enumerate(stage)
        ]

    def summed(buf, stage, n):
        for c in stage:
            c.wait_recv()
        out = buf[0]
        for j in range(n):
            out = out + buf[j + 1]
        return out

    d1[0, 0:3] = dots[0, 0:3]
    d1[0, 3:6] = dots[1, 0:3]
    d1[0, 6:8] = jnp.zeros((2, 128), F32)
    stage1 = reduce_stage(d1, stages[0], 0)
    stage2 = reduce_stage(d2, stages[1], len(stage1))
    for c in stage1:
        c.start()
    send_faces(8, Er[...])
    finish(1)
    d2[0] = summed(d1, stage1, len(stage1))
    for c in stage2:
        c.start()
    tile_exchange.drain()
    for c in stage1:
        c.wait_send()

    def drain(i, carry):
        fine(i).drain()
        return carry

    lax.fori_loop(0, 9, drain, 0)
    for k in range(2):
        coarse(k).drain()
    h = halo(8)
    add_faces(Fr, (2,), h)
    lanes_sum = jnp.sum(summed(d2, stage2, len(stage2)), axis=1, keepdims=True)
    pick = lambda i: lanes_sum[i : i + 1, 0:1]
    rz0, c00 = pick(1), pick(2)
    r0u, wu, uv = pick(3), pick(4), pick(5)
    alpha0 = rz0 / c00
    rz1 = alpha0 * (alpha0 * wu - r0u)
    beta1 = 1.0 + rz1 / rz0
    curve = beta1 * beta1 * c00 - 2.0 * beta1 * alpha0 * wu + alpha0 * alpha0 * uv
    alpha1 = rz1 / curve
    c_z = alpha0 + alpha1 * beta1
    c_u = alpha1 * alpha0
    for e in range(EX):
        sol_ref[e] = c_z * Zr[0, e] - c_u * Zr[1, e]
        res_ref[e] = Fr[0, e] - c_z * Fr[1, e] + c_u * Fr[2, e]
    for c in stage2:
        c.wait_send()


def solution(mesh):
    gxn, gyn = mesh.shape["gx"], mesh.shape["gy"]
    table = constants()
    names = tuple(table)
    n_dots = gyn - 1 + gxn - 1

    def per_device(right_side, coefficient):
        rhs = right_side.reshape(EX, ROWS, ZF)
        field = (EX, ROWS, ZF)
        vm = lambda *s: pltpu.VMEM(s, F32)
        dma = lambda *s: pltpu.SemaphoreType.DMA(s)
        face = (96, ZF)
        scratch = [pltpu.VMEM(table[m].shape, table[m].dtype) for m in names]
        scratch += [
            vm(3, *field), vm(2, *field), vm(*field), vm(*field), vm(*field), vm(*face), vm(*face), vm(384, ZC), vm(*face), vm(*face),
            vm(*field), vm(*field), vm(*field), vm(*field), vm(2, *face), vm(2, *face), vm(*face),
            vm(ROWS, ZF), vm(ROWS, ZF), vm(*face), vm(*face),
            vm(384, ZC), vm(384, ZC), vm(8, 128), vm(EX, EY, EZ), vm(80, 128),
            vm(9, 2, YF, ZF), vm(9, 2, EX * N, ZF), vm(9, 2, YF, ZF), vm(9, 2, EX * N, ZF), vm(9, 2, EX * N, ZF),
            vm(2, 192, ZC), vm(2, 256, ZC),
            vm(2, 8, 128), vm(gyn, 8, 128), vm(gxn, 8, 128),
            dma(len(names) + 2), dma(9, 8), dma(9, 8), dma(2, 8), dma(2, 8), dma(8), dma(8), dma(n_dots), dma(n_dots),
        ]
        sol, res = pl.pallas_call(
            functools.partial(kernel_body, (gxn, gyn), names),
            out_shape=[pltpu.VMEM(field, F32)] * 2,
            in_specs=[pl.BlockSpec(memory_space=pl.ANY)] * (2 + len(names)),
            out_specs=[pl.BlockSpec(memory_space=pltpu.VMEM)] * 2,
            scratch_shapes=scratch,
            compiler_params=pltpu.CompilerParams(
                collective_id=0, has_side_effects=True, vmem_limit_bytes=56 * 2**20
            ),
        )(rhs, coefficient, *[jnp.asarray(table[m]) for m in names])
        def inner(dim, axis, n):
            i = lax.broadcasted_iota(jnp.int32, right_side.shape, dim)
            here = lax.axis_index(axis) * right_side.shape[dim] if axis else 0
            return (i != -here) & (i != n * right_side.shape[dim] - 1 - here)

        keep = inner(0, "gx", gxn) & inner(1, "gy", gyn) & inner(2, None, 1)
        zeroed = lambda x: jnp.where(keep, x.reshape(right_side.shape), 0.0)
        return zeroed(sol), zeroed(res)

    spec = P("gx", "gy", None)
    return jax.shard_map(
        per_device, mesh=mesh, in_specs=(spec, spec), out_specs=(spec, spec), check_vma=False
    )
```
